32 devices in a mesh: blk: 8 (over z, x), head: 4 (over y, core).
Axes of the slice: x: 2, y: 2, z: 4, core: 2. Of those that a mesh axis runs over, the one named last changes fastest.
Arguments:
- tokens: bfloat16 [4096, 512], P('blk'), may hold values from -6 to 6
- gain_attn: bfloat16 [512], replicated, may hold values from 0.5 to 1.5
- gain_ffn: bfloat16 [512], replicated, may hold values from 0.5 to 1.5
- w_qkv: bfloat16 [512, 3, 512], P(None, None, 'head'), may hold values from -0.25 to 0.25
- w_out: bfloat16 [512, 512], P('head'), may hold values from -3 to 3
- w_sort: bfloat16 [512, 512], P(None, 'head'), may hold values from -0.75 to 0.75
- w_up: bfloat16 [512, 2048], P(None, 'head'), may hold values from -0.25 to 0.25
- w_down: bfloat16 [2048, 512], P('head'), may hold values from -0.125 to 0.125
- gumbel_noise: float32 [64, 8, 64], P('blk', 'head'), may hold values from -1.4 to 7, as said below
- partner: int32 [64, 8], P(None, 'head'), may hold values from 0 to 63
- cotangent: bfloat16 [4096, 512], P('blk'), may hold values from -6 to 6
Outputs:
- output: float32 [4096, 512], P('blk')
- d_tokens: float32 [4096, 512], P('blk')
- g_gain_attn: float32 [512], replicated
- g_gain_ffn: float32 [512], replicated
- g_qkv: float32 [512, 3, 512], P(None, None, 'head')
- g_out: float32 [512, 512], P('head')
- g_sort: float32 [512, 512], P(None, 'head')
- g_up: float32 [512, 2048], P(None, 'head')
- g_down: float32 [2048, 512], P('head')
The draws below stay inside these ranges and needn't reach their ends.
Inputs may be any that keep to these rules, and one draw needn't show every extreme that they name: `gumbel_noise`: gumbel noise of scale one half: -0.5 log(-log u) for a uniform u. A partner is a block number of the sequence.
All inputs are finite; a program needn't handle non-finite values.
Results may differ from the reference program's by a relative error of at most 0.006.
The reference program's roundings to bfloat16 on the way count: a program that leaves them out, or rounds other values in their place, can miss the bound.
Values may be sent and summed in bfloat16 or wider, within the bound.
No kernel may reach another device: no remote copies, remote signals or barrier semaphores. Data moves between devices by JAX's collectives and lax.ppermute only.
A program may use at most 128 MiB of HBM per device.

```python
import jax
import jax.numpy as jnp
from jax import lax

D = 512
HEADS = 8
DH = 64
FF = 2048
BLOCK = 64
SINK = 8
TOKENS = 4096
LEN = 4096
NBLK = 64
NB = 64


def draw_gumbel_noise(key, part):
    key = jax.random.fold_in(key, 7)
    uniform_draw = jax.random.uniform(key, (NBLK, HEADS, NB), jnp.float32, 1e-06, 1.0 - 1e-06)
    return -0.5 * jnp.log(-jnp.log(uniform_draw))


def place_ends(array, key, least, top_value):
    longest = array.shape.index(max(array.shape))
    spots = []
    for shift in (0, 1):
        where = [jax.random.randint(jax.random.fold_in(key, axis), (), 0, length) for axis, length in enumerate(array.shape)]
        where[longest] = (where[longest] + shift) % array.shape[longest]
        spots.append(tuple(where))
    return array.at[spots[0]].set(least).at[spots[1]].set(top_value)


def steps_of(key, shape, split, low, high):
    factor_of = 1.0
    for axis_at, shards_of in split:
        draws = jax.random.uniform(jax.random.fold_in(jax.random.fold_in(key, 6), axis_at), (shards_of,), jnp.float32, low / len(split), high / len(split))
        factor_of = factor_of * jnp.repeat(jnp.exp(draws), shape[axis_at] // shards_of).reshape((-1,) + (1,) * (len(shape) - 1 - axis_at))
    return factor_of


def scatter_about(stream_key, dims, scale, most, cuts=(), held_as=jnp.bfloat16):
    drawn = jax.random.normal(stream_key, dims, jnp.float32) * scale
    if len(cuts) > 0:
        drawn = steps_of(stream_key, dims, cuts, -0.22, 0.18) * drawn
    return jnp.clip(drawn, min=-most, max=most).astype(held_as)


def setup_inputs(seed: int = 0) -> dict:
    splits = jax.random.split(jax.random.key(seed), 12)
    return {
        "tokens": scatter_about(splits[0], (TOKENS, D), 1.0, 6.0, ((0, 8),)),
        "gain_attn": jnp.clip(1.0 + 0.1 * jax.random.normal(splits[1], (D,), jnp.float32), 0.5, 1.5).astype(jnp.bfloat16),
        "gain_ffn": jnp.clip(1.0 + 0.1 * jax.random.normal(splits[2], (D,), jnp.float32), 0.5, 1.5).astype(jnp.bfloat16),
        "w_qkv": scatter_about(splits[3], (D, 3, HEADS * DH), D ** -0.5, 0.25, ((2, 4),)),
        "w_out": scatter_about(splits[4], (HEADS * DH, D), (HEADS * DH // (2 * BLOCK)) ** -0.5, 3.0, ((0, 4),)),
        "w_sort": scatter_about(splits[5], (D, HEADS * NB), BLOCK ** -0.5, 0.75, ((1, 4),)),
        "w_up": scatter_about(splits[6], (D, FF), D ** -0.5, 0.25, ((1, 4),)),
        "w_down": scatter_about(splits[7], (FF, D), FF ** -0.5, 0.125, ((0, 4),)),
        "gumbel_noise": draw_gumbel_noise(jax.random.fold_in(splits[11], 71), 0),
        "partner": place_ends(jax.random.randint(splits[9], (NBLK, HEADS), 0, NB), jax.random.fold_in(splits[9], 1), 0, NB - 1).astype(jnp.int32),
        "cotangent": scatter_about(splits[10], (TOKENS, D), 1.0, 6.0, ((0, 8),)),
    }


EPS = 1e-05
TEMPER = 0.75
ROOT_HALF = 0.7071067811865476
HIGHEST = lax.Precision.HIGHEST

@jax.custom_vjp
def low(v):
    return lax.optimization_barrier(v.astype(jnp.bfloat16)).astype(jnp.float32)

@jax.custom_vjp
def low_back(v):
    return v

def low_keep(v):
    return (low(v), None)

def low_pass(kept, grad):
    return (grad,)

def back_keep(v):
    return (v, None)

def back_low(kept, grad):
    return (low(grad),)
low.defvjp(low_keep, low_pass)
low_back.defvjp(back_keep, back_low)

def layer_norm(values, norm_gain):
    average = lax.optimization_barrier(jnp.mean(values, -1, keepdims=True))
    centred = values - average
    spread = lax.optimization_barrier(jnp.mean(centred * centred, -1, keepdims=True))
    return centred * lax.rsqrt(spread + EPS) * norm_gain

def log_total(values, axis):
    highest = lax.optimization_barrier(jnp.max(values, axis=axis, keepdims=True))
    return highest + jnp.log(lax.optimization_barrier(jnp.sum(jnp.exp(values - highest), axis=axis, keepdims=True)))

def balancing_log_space(sort_logits):
    for sweep in range(SINK):
        sort_logits = sort_logits - log_total(sort_logits, 2)
        sort_logits = sort_logits - log_total(sort_logits, 1)
    return sort_logits

def gelu_value(values):
    return 0.5 * values * (1.0 + lax.erf(values * ROOT_HALF))

def sequence_forward(values, params, seq_noise, sequence_partner):
    gain_one, gain_two, qkv_mat, out_mat, sort_mat, up_mat, down_mat = params
    scale = DH ** (-0.5)
    h_one = layer_norm(values, gain_one)
    qkv = low(low_back(jnp.einsum('td,dcf->tcf', low(h_one), qkv_mat, precision=HIGHEST)))
    query = qkv[:, 0].reshape(NB, BLOCK, HEADS, DH)
    key_near = qkv[:, 1].reshape(NB, BLOCK, HEADS, DH)
    value_near = qkv[:, 2].reshape(NB, BLOCK, HEADS, DH)
    summary = lax.optimization_barrier(jnp.mean(h_one.reshape(NB, BLOCK, D), axis=1))
    row_block = (jnp.dot(summary, sort_mat, precision=HIGHEST).reshape(NB, HEADS, NB) + seq_noise) / TEMPER
    balanced_plan = balancing_log_space(row_block.transpose(1, 0, 2))
    picked = jnp.take_along_axis(jnp.exp(balanced_plan), sequence_partner.T[:, :, None], axis=2)[:, :, 0]
    weight_matrix = (NB * picked).T
    index = jnp.broadcast_to(sequence_partner[:, None, :, None], key_near.shape)
    key_far = low_back(jnp.take_along_axis(key_near, index, axis=0))
    value_far = low_back(jnp.take_along_axis(value_near, index, axis=0))
    near_z = low_back(scale * jnp.einsum('bqhd,bkhd->bhqk', query, key_near, precision=HIGHEST))
    far_z = low_back(scale * jnp.einsum('bqhd,bkhd->bhqk', query, key_far, precision=HIGHEST))
    scores = jnp.concatenate([near_z, weight_matrix[:, :, None, None] * far_z], -1)
    highest = lax.optimization_barrier(jnp.max(scores, -1, keepdims=True))
    expo = jnp.exp(scores - highest)
    probs = low(expo / lax.optimization_barrier(jnp.sum(expo, -1, keepdims=True)))
    near_ctx = jnp.einsum('bhqk,bkhd->bqhd', probs[..., :BLOCK], value_near, precision=HIGHEST)
    far_ctx = jnp.einsum('bhqk,bkhd->bqhd', probs[..., BLOCK:], value_far, precision=HIGHEST)
    context = near_ctx + weight_matrix[:, None, :, None] * far_ctx
    context = low(low_back(context.reshape(LEN, HEADS * DH)))
    middle = values + low_back(jnp.dot(context, out_mat, precision=HIGHEST))
    h_two = low(layer_norm(middle, gain_two))
    hidden_pre = low_back(jnp.dot(h_two, up_mat, precision=HIGHEST))
    active_rows = low(gelu_value(hidden_pre))
    return middle + low_back(jnp.dot(active_rows, down_mat, precision=HIGHEST))

def reference(tokens, gain_attn, gain_ffn, w_qkv, w_out, w_sort, w_up, w_down, gumbel_noise, partner, cotangent):
    weights = tuple((item.astype(jnp.float32) for item in (gain_attn, gain_ffn, w_qkv, w_out, w_sort, w_up, w_down)))
    seq_count = tokens.shape[0] // LEN
    inputs = tokens.astype(jnp.float32).reshape(seq_count, LEN, D)
    noises = gumbel_noise.reshape(seq_count, NB, HEADS, NB)
    partners = partner.reshape(seq_count, NB, HEADS)
    cotangents = cotangent.astype(jnp.float32).reshape(seq_count, LEN, D)

    def one_sequence(carry, item):
        seq_in, seq_noise, sequence_partner, seq_cot = item

        def forward(values, *params):
            return sequence_forward(values, params, seq_noise, sequence_partner)
        result, pull = jax.vjp(forward, seq_in, *weights)
        grads = pull(seq_cot)
        summed = tuple((total + grad for total, grad in zip(carry, grads[1:])))
        return (summed, (result, grads[0]))
    start = tuple((jnp.zeros_like(item) for item in weights))
    totals, (results, d_inputs) = lax.scan(one_sequence, start, (inputs, noises, partners, cotangents))
    return (results.reshape(-1, D), d_inputs.reshape(-1, D), totals[0], totals[1], totals[2], totals[3], totals[4], totals[5], totals[6])
```

```python
import jax
import jax.numpy as jnp
from jax import lax
from jax.sharding import PartitionSpec as P

D = 512
DH = 64
BLOCK = 64
SINK = 8


EPS = 1e-05
TEMPER = 0.75
ROOT_HALF = 0.7071067811865476
INV_ROOT_TWO_PI = 0.3989422804014327
HIGHEST = lax.Precision.HIGHEST


def normalize(values, norm_gain):
    average = jnp.mean(values, -1, keepdims=True)
    centred = values - average
    inv_std = lax.rsqrt(jnp.mean(centred * centred, -1, keepdims=True) + EPS)
    normed = centred * inv_std
    return (normed * norm_gain, normed, inv_std)


def norm_back(d_out, normed, inv_std, norm_gain):
    d_normed = d_out * norm_gain
    return inv_std * (
        d_normed
        - jnp.mean(d_normed, -1, keepdims=True)
        - normed * jnp.mean(d_normed * normed, -1, keepdims=True)
    )


def log_total(values, axis):
    highest = jnp.max(values, axis=axis, keepdims=True)
    return highest + jnp.log(jnp.sum(jnp.exp(values - highest), axis=axis, keepdims=True))


def balancing_log_space(sort_logits):
    for sweep in range(SINK):
        sort_logits = sort_logits - log_total(sort_logits, 2)
        sort_logits = sort_logits - log_total(sort_logits, 1)
    return sort_logits


def gelu_value(values):
    return 0.5 * values * (1.0 + lax.erf(values * ROOT_HALF))


def gelu_slope(values):
    return (
        0.5 * (1.0 + lax.erf(values * ROOT_HALF))
        + values * jnp.exp(-0.5 * values * values) * INV_ROOT_TWO_PI
    )


def local(
    tokens,
    gain_attn,
    gain_ffn,
    w_qkv,
    w_out,
    w_sort,
    w_up,
    w_down,
    gumbel_noise,
    partner,
    cotangent,
):
    f32 = jnp.float32
    bf16 = jnp.bfloat16
    tok_rows = tokens.shape[0]
    blocks_dev = tok_rows // BLOCK
    heads_dev = w_out.shape[0] // DH
    width_dev = heads_dev * DH
    requests = blocks_dev * heads_dev
    dev_count = lax.axis_size("blk")
    my_index = lax.axis_index("blk")
    first_block = my_index * blocks_dev
    seq_blocks = partner.shape[0]
    scale = DH ** (-0.5)
    gain_one = gain_attn.astype(f32)
    gain_two = gain_ffn.astype(f32)
    inputs = tokens.astype(f32)
    h_one, normed_one, inv_one = normalize(inputs, gain_one)
    h_one_low = h_one.astype(bf16)
    qkv = jnp.einsum("td,dcf->tcf", h_one_low, w_qkv, preferred_element_type=f32).astype(bf16)
    summary = jnp.mean(h_one.reshape(blocks_dev, BLOCK, D), axis=1)
    sort_mat = w_sort.astype(f32)
    own_rows = (
        jnp.dot(summary, sort_mat, precision=HIGHEST).reshape(blocks_dev, heads_dev, seq_blocks)
        + gumbel_noise
    ) / TEMPER
    every_rows = lax.all_gather(own_rows, "blk", axis=0, tiled=True)
    my_partner = lax.dynamic_slice_in_dim(partner, first_block, blocks_dev, 0)

    def own_weights(sequence_rows):
        balanced_plan = balancing_log_space(sequence_rows.transpose(1, 0, 2))
        mine = lax.dynamic_slice_in_dim(jnp.exp(balanced_plan), first_block, blocks_dev, 1)
        return seq_blocks * jnp.take_along_axis(mine, my_partner.T[:, :, None], axis=2)[:, :, 0]

    weight_hb, sink_pull = jax.vjp(own_weights, every_rows)
    weight_matrix = weight_hb.T
    owner_all = (partner // blocks_dev).reshape(dev_count, requests)
    slot_all = (
        partner % blocks_dev * heads_dev + jnp.arange(heads_dev, dtype=jnp.int32)[None, :]
    ).reshape(dev_count, requests)
    owner_mine = lax.dynamic_index_in_dim(owner_all, my_index, 0, keepdims=False)
    tile_ids = jnp.arange(requests, dtype=jnp.int32)
    key_value = (
        qkv[:, 1:3]
        .reshape(blocks_dev, BLOCK, 2, heads_dev, DH)
        .transpose(0, 3, 1, 2, 4)
        .reshape(requests, BLOCK, 2 * DH)
    )
    empty_tile = jnp.zeros((), bf16)
    wanted = owner_all == my_index
    outgoing = jnp.where(
        wanted[:, :, None, None], jnp.take(key_value, slot_all, axis=0), empty_tile
    )
    incoming = lax.all_to_all(outgoing, "blk", split_axis=0, concat_axis=0, tiled=True)
    partner_tiles = jnp.sum(incoming, axis=0, dtype=f32).astype(bf16)
    far_tiles = partner_tiles.reshape(blocks_dev, heads_dev, BLOCK, 2, DH)
    key_far = far_tiles[:, :, :, 0]
    value_far = far_tiles[:, :, :, 1]
    query_b = qkv[:, 0].reshape(blocks_dev, BLOCK, heads_dev, DH)
    key_b = qkv[:, 1].reshape(blocks_dev, BLOCK, heads_dev, DH)
    value_b = qkv[:, 2].reshape(blocks_dev, BLOCK, heads_dev, DH)
    weight_s = weight_matrix[:, :, None, None]

    def score_parts():
        near_z = scale * jnp.einsum("bqhd,bkhd->bhqk", query_b, key_b, preferred_element_type=f32)
        far_z = scale * jnp.einsum("bqhd,bhkd->bhqk", query_b, key_far, preferred_element_type=f32)
        return (near_z, far_z, jnp.concatenate([near_z, weight_s * far_z], -1))

    near_z, far_z, scores = score_parts()
    highest = jnp.max(scores, -1, keepdims=True)
    expo = jnp.exp(scores - highest)
    row_total = jnp.sum(expo, -1, keepdims=True)
    log_sum = highest + jnp.log(row_total)
    probs_low = (expo / row_total).astype(bf16)
    near_ctx = jnp.einsum(
        "bhqk,bkhd->bqhd", probs_low[..., :BLOCK], value_b, preferred_element_type=f32
    )
    far_ctx = jnp.einsum(
        "bhqk,bhkd->bqhd", probs_low[..., BLOCK:], value_far, preferred_element_type=f32
    )
    context = near_ctx + weight_matrix[:, None, :, None] * far_ctx
    context_low = context.reshape(tok_rows, width_dev).astype(bf16)
    attn = lax.psum(jnp.dot(context_low, w_out, preferred_element_type=f32), "head")
    middle = inputs + attn
    h_two, normed_two, inv_two = normalize(middle, gain_two)
    h_two_low = h_two.astype(bf16)
    hidden_pre = jnp.dot(h_two_low, w_up, preferred_element_type=f32)
    active_low = gelu_value(hidden_pre).astype(bf16)
    ffn = lax.psum(
        jnp.dot(active_low, w_down, preferred_element_type=f32).astype(jnp.bfloat16), "head"
    ).astype(jnp.float32)
    output = middle + ffn
    g_down = jnp.einsum("tf,td->fd", active_low, cotangent, preferred_element_type=f32)
    d_active = jnp.einsum("td,fd->tf", cotangent, w_down, preferred_element_type=f32)
    d_hidden = (d_active * gelu_slope(hidden_pre)).astype(bf16)
    g_up = jnp.einsum("td,tf->df", h_two_low, d_hidden, preferred_element_type=f32)
    d_h_two = lax.psum(jnp.einsum("tf,df->td", d_hidden, w_up, preferred_element_type=f32), "head")
    g_gain_two = jnp.sum(d_h_two * normed_two, 0)
    d_middle = cotangent.astype(f32) + norm_back(d_h_two, normed_two, inv_two, gain_two)
    d_attn_low = d_middle.astype(bf16)
    g_out = jnp.einsum("tf,td->fd", context_low, d_attn_low, preferred_element_type=f32)
    d_context = jnp.einsum("td,fd->tf", d_attn_low, w_out, preferred_element_type=f32).astype(bf16)
    d_context = d_context.reshape(blocks_dev, BLOCK, heads_dev, DH)
    near_z, far_z, scores = score_parts()
    probs = jnp.exp(scores - log_sum)
    probs_low = probs.astype(bf16)
    far_ctx = jnp.einsum(
        "bhqk,bhkd->bqhd", probs_low[..., BLOCK:], value_far, preferred_element_type=f32
    )
    d_probs_near = jnp.einsum("bqhd,bkhd->bhqk", d_context, value_b, preferred_element_type=f32)
    d_probs_far = weight_s * jnp.einsum(
        "bqhd,bhkd->bhqk", d_context, value_far, preferred_element_type=f32
    )
    d_probs = jnp.concatenate([d_probs_near, d_probs_far], -1)
    d_scores = probs * (d_probs - jnp.sum(d_probs * probs, -1, keepdims=True))
    d_near = d_scores[..., :BLOCK].astype(bf16)
    d_far_raw = d_scores[..., BLOCK:]
    d_far = (weight_s * d_far_raw).astype(bf16)
    d_weight = jnp.sum(d_far_raw * far_z, (2, 3)) + jnp.sum(d_context.astype(f32) * far_ctx, (1, 3))
    d_query = scale * (
        jnp.einsum("bhqk,bkhd->bqhd", d_near, key_b, preferred_element_type=f32)
        + jnp.einsum("bhqk,bhkd->bqhd", d_far, key_far, preferred_element_type=f32)
    )
    d_key = scale * jnp.einsum("bhqk,bqhd->bkhd", d_near, query_b, preferred_element_type=f32)
    d_value = jnp.einsum(
        "bhqk,bqhd->bkhd", probs_low[..., :BLOCK], d_context, preferred_element_type=f32
    )
    d_key_far = scale * jnp.einsum("bhqk,bqhd->bhkd", d_far, query_b, preferred_element_type=f32)
    d_value_far = weight_s * jnp.einsum(
        "bhqk,bqhd->bhkd", probs_low[..., BLOCK:], d_context, preferred_element_type=f32
    )
    grad_tiles = jnp.stack([d_key_far.astype(bf16), d_value_far.astype(bf16)], 3).reshape(
        requests, BLOCK * 2 * DH
    )
    peers = jnp.arange(dev_count, dtype=jnp.int32)
    outgoing_grads = jnp.where(
        (owner_mine[None, :] == peers[:, None])[:, :, None], grad_tiles[None], empty_tile
    )
    returned = lax.all_to_all(outgoing_grads, "blk", split_axis=0, concat_axis=0, tiled=True)
    selector = (owner_all == my_index)[:, :, None] & (
        slot_all[:, :, None] == tile_ids[None, None, :]
    )
    selector = selector.reshape(dev_count * requests, requests).astype(bf16)
    remote = jnp.einsum(
        "st,sf->tf",
        selector,
        returned.reshape(dev_count * requests, BLOCK * 2 * DH),
        preferred_element_type=f32,
    )
    remote = (
        remote.reshape(blocks_dev, heads_dev, BLOCK, 2, DH)
        .transpose(0, 2, 3, 1, 4)
        .reshape(tok_rows, 2, width_dev)
    )
    near_kv = (
        jnp.stack([d_key.reshape(tok_rows, width_dev), d_value.reshape(tok_rows, width_dev)], 1)
        + remote
    )
    d_qkv = jnp.concatenate([d_query.reshape(tok_rows, 1, width_dev), near_kv], 1).astype(bf16)
    g_qkv = jnp.einsum("td,tcf->dcf", h_one_low, d_qkv, preferred_element_type=f32)
    d_h_part = jnp.einsum("tcf,dcf->td", d_qkv, w_qkv, preferred_element_type=f32)
    (d_every,) = sink_pull(d_weight.T)
    d_own = lax.psum_scatter(d_every, "blk", scatter_dimension=0, tiled=True) / TEMPER
    d_flat = d_own.reshape(blocks_dev, heads_dev * seq_blocks)
    g_sort = jnp.dot(summary.T, d_flat, precision=HIGHEST)
    d_summary = jnp.dot(d_flat, sort_mat.T, precision=HIGHEST)
    d_h_part = (d_h_part.reshape(blocks_dev, BLOCK, D) + d_summary[:, None, :] / BLOCK).reshape(
        tok_rows, D
    )
    d_h_one = lax.psum(d_h_part, "head")
    g_gain_one = jnp.sum(d_h_one * normed_one, 0)
    d_tokens = d_middle + norm_back(d_h_one, normed_one, inv_one, gain_one)
    summed = lax.psum((g_gain_one, g_gain_two, g_qkv, g_out, g_sort, g_up, g_down), "blk")
    return (
        output,
        d_tokens,
        summed[0],
        summed[1],
        summed[2],
        summed[3],
        summed[4],
        summed[5],
        summed[6],
    )


def solution(mesh):
    in_specs = (
        P("blk", None),
        P(),
        P(),
        P(None, None, "head"),
        P("head", None),
        P(None, "head"),
        P(None, "head"),
        P("head", None),
        P("blk", "head", None),
        P(None, "head"),
        P("blk", None),
    )
    out_specs = (
        P("blk", None),
        P("blk", None),
        P(),
        P(),
        P(None, None, "head"),
        P("head", None),
        P(None, "head"),
        P(None, "head"),
        P("head", None),
    )
    return jax.shard_map(local, mesh=mesh, in_specs=in_specs, out_specs=out_specs, check_vma=False)
```

```python
import functools
import math

import jax
import jax.numpy as jnp
from jax import lax
from jax.experimental import pallas as pl
from jax.experimental.pallas import tpu as pltpu
from jax.sharding import PartitionSpec as P

D = 512
DH = 64
BLOCK = 64
SINK = 8


EPS = 1e-05
TEMPER = 0.75
ROOT_HALF = 0.7071067811865476
INV_ROOT_TWO_PI = 0.3989422804014327
HIGHEST = lax.Precision.HIGHEST
VMEM_LIMIT = 48 * 1024 * 1024


def normalize(values, norm_gain):
    average = jnp.mean(values, -1, keepdims=True)
    centred = values - average
    inv_std = lax.rsqrt(jnp.mean(centred * centred, -1, keepdims=True) + EPS)
    normed = centred * inv_std
    return (normed * norm_gain, normed, inv_std)


def norm_back(d_out, normed, inv_std, norm_gain):
    d_normed = d_out * norm_gain
    return inv_std * (
        d_normed
        - jnp.mean(d_normed, -1, keepdims=True)
        - normed * jnp.mean(d_normed * normed, -1, keepdims=True)
    )


def log_total(values, axis):
    highest = jnp.max(values, axis=axis, keepdims=True)
    return highest + jnp.log(jnp.sum(jnp.exp(values - highest), axis=axis, keepdims=True))


def balancing_log_space(sort_logits):
    for sweep in range(SINK):
        sort_logits = sort_logits - log_total(sort_logits, 2)
        sort_logits = sort_logits - log_total(sort_logits, 1)
    return sort_logits


def gelu_value(values):
    return 0.5 * values * (1.0 + lax.erf(values * ROOT_HALF))


def gelu_slope(values):
    return (
        0.5 * (1.0 + lax.erf(values * ROOT_HALF))
        + values * jnp.exp(-0.5 * values * values) * INV_ROOT_TWO_PI
    )


def local(
    tokens,
    gain_attn,
    gain_ffn,
    w_qkv,
    w_out,
    w_sort,
    w_up,
    w_down,
    gumbel_noise,
    partner,
    cotangent,
):
    f32 = jnp.float32
    bf16 = jnp.bfloat16
    tok_rows = tokens.shape[0]
    blocks_dev = tok_rows // BLOCK
    heads_dev = w_out.shape[0] // DH
    width_dev = heads_dev * DH
    requests = blocks_dev * heads_dev
    dev_count = lax.axis_size("blk")
    my_index = lax.axis_index("blk")
    first_block = my_index * blocks_dev
    seq_blocks = partner.shape[0]
    scale = DH ** (-0.5)
    gain_one = gain_attn.astype(f32)
    gain_two = gain_ffn.astype(f32)
    inputs = tokens.astype(f32)
    h_one, normed_one, inv_one = normalize(inputs, gain_one)
    h_one_low = h_one.astype(bf16)
    qkv = jnp.einsum("td,dcf->tcf", h_one_low, w_qkv, preferred_element_type=f32).astype(bf16)
    summary = jnp.mean(h_one.reshape(blocks_dev, BLOCK, D), axis=1)
    sort_mat = w_sort.astype(f32)
    own_rows = (
        jnp.dot(summary, sort_mat, precision=HIGHEST).reshape(blocks_dev, heads_dev, seq_blocks)
        + gumbel_noise
    ) / TEMPER
    every_rows = lax.all_gather(own_rows, "blk", axis=0, tiled=True)
    my_partner = lax.dynamic_slice_in_dim(partner, first_block, blocks_dev, 0)

    def own_weights(sequence_rows):
        balanced_plan = balancing_log_space(sequence_rows.transpose(1, 0, 2))
        mine = lax.dynamic_slice_in_dim(jnp.exp(balanced_plan), first_block, blocks_dev, 1)
        return seq_blocks * jnp.take_along_axis(mine, my_partner.T[:, :, None], axis=2)[:, :, 0]

    weight_hb, sink_pull = jax.vjp(own_weights, every_rows)
    weight_matrix = weight_hb.T
    owner_all = (partner // blocks_dev).reshape(dev_count, requests)
    slot_all = (
        partner % blocks_dev * heads_dev + jnp.arange(heads_dev, dtype=jnp.int32)[None, :]
    ).reshape(dev_count, requests)
    owner_mine = lax.dynamic_index_in_dim(owner_all, my_index, 0, keepdims=False)
    tile_ids = jnp.arange(requests, dtype=jnp.int32)
    key_value = (
        qkv[:, 1:3]
        .reshape(blocks_dev, BLOCK, 2, heads_dev, DH)
        .transpose(0, 3, 1, 2, 4)
        .reshape(requests, BLOCK, 2 * DH)
    )
    empty_tile = jnp.zeros((), bf16)
    wanted = owner_all == my_index
    outgoing = jnp.where(
        wanted[:, :, None, None], jnp.take(key_value, slot_all, axis=0), empty_tile
    )
    incoming = lax.all_to_all(outgoing, "blk", split_axis=0, concat_axis=0, tiled=True)
    partner_tiles = jnp.sum(incoming, axis=0, dtype=f32).astype(bf16)
    far_tiles = partner_tiles.reshape(blocks_dev, heads_dev, BLOCK, 2, DH)
    key_far = far_tiles[:, :, :, 0]
    value_far = far_tiles[:, :, :, 1]
    query_b = qkv[:, 0].reshape(blocks_dev, BLOCK, heads_dev, DH)
    key_b = qkv[:, 1].reshape(blocks_dev, BLOCK, heads_dev, DH)
    value_b = qkv[:, 2].reshape(blocks_dev, BLOCK, heads_dev, DH)
    weight_s = weight_matrix[:, :, None, None]

    def score_parts():
        near_z = scale * jnp.einsum("bqhd,bkhd->bhqk", query_b, key_b, preferred_element_type=f32)
        far_z = scale * jnp.einsum("bqhd,bhkd->bhqk", query_b, key_far, preferred_element_type=f32)
        return (near_z, far_z, jnp.concatenate([near_z, weight_s * far_z], -1))

    near_z, far_z, scores = score_parts()
    highest = jnp.max(scores, -1, keepdims=True)
    expo = jnp.exp(scores - highest)
    row_total = jnp.sum(expo, -1, keepdims=True)
    log_sum = highest + jnp.log(row_total)
    probs_low = (expo / row_total).astype(bf16)
    near_ctx = jnp.einsum(
        "bhqk,bkhd->bqhd", probs_low[..., :BLOCK], value_b, preferred_element_type=f32
    )
    far_ctx = jnp.einsum(
        "bhqk,bhkd->bqhd", probs_low[..., BLOCK:], value_far, preferred_element_type=f32
    )
    context = near_ctx + weight_matrix[:, None, :, None] * far_ctx
    context_low = context.reshape(tok_rows, width_dev).astype(bf16)
    attn = lax.psum(jnp.dot(context_low, w_out, preferred_element_type=f32), "head")
    middle = inputs + attn
    h_two, normed_two, inv_two = normalize(middle, gain_two)
    h_two_low = h_two.astype(bf16)
    hidden_pre = jnp.dot(h_two_low, w_up, preferred_element_type=f32)
    active_low = gelu_value(hidden_pre).astype(bf16)
    ffn = lax.psum(
        jnp.dot(active_low, w_down, preferred_element_type=f32).astype(jnp.bfloat16), "head"
    ).astype(jnp.float32)
    output = middle + ffn
    g_down = jnp.einsum("tf,td->fd", active_low, cotangent, preferred_element_type=f32)
    d_active = jnp.einsum("td,fd->tf", cotangent, w_down, preferred_element_type=f32)
    d_hidden = (d_active * gelu_slope(hidden_pre)).astype(bf16)
    g_up = jnp.einsum("td,tf->df", h_two_low, d_hidden, preferred_element_type=f32)
    d_h_two = lax.psum(jnp.einsum("tf,df->td", d_hidden, w_up, preferred_element_type=f32), "head")
    g_gain_two = jnp.sum(d_h_two * normed_two, 0)
    d_middle = cotangent.astype(f32) + norm_back(d_h_two, normed_two, inv_two, gain_two)
    d_attn_low = d_middle.astype(bf16)
    g_out = jnp.einsum("tf,td->fd", context_low, d_attn_low, preferred_element_type=f32)
    d_context = jnp.einsum("td,fd->tf", d_attn_low, w_out, preferred_element_type=f32).astype(bf16)
    d_context = d_context.reshape(blocks_dev, BLOCK, heads_dev, DH)
    near_z, far_z, scores = score_parts()
    probs = jnp.exp(scores - log_sum)
    probs_low = probs.astype(bf16)
    far_ctx = jnp.einsum(
        "bhqk,bhkd->bqhd", probs_low[..., BLOCK:], value_far, preferred_element_type=f32
    )
    d_probs_near = jnp.einsum("bqhd,bkhd->bhqk", d_context, value_b, preferred_element_type=f32)
    d_probs_far = weight_s * jnp.einsum(
        "bqhd,bhkd->bhqk", d_context, value_far, preferred_element_type=f32
    )
    d_probs = jnp.concatenate([d_probs_near, d_probs_far], -1)
    d_scores = probs * (d_probs - jnp.sum(d_probs * probs, -1, keepdims=True))
    d_near = d_scores[..., :BLOCK].astype(bf16)
    d_far_raw = d_scores[..., BLOCK:]
    d_far = (weight_s * d_far_raw).astype(bf16)
    d_weight = jnp.sum(d_far_raw * far_z, (2, 3)) + jnp.sum(d_context.astype(f32) * far_ctx, (1, 3))
    d_query = scale * (
        jnp.einsum("bhqk,bkhd->bqhd", d_near, key_b, preferred_element_type=f32)
        + jnp.einsum("bhqk,bhkd->bqhd", d_far, key_far, preferred_element_type=f32)
    )
    d_key = scale * jnp.einsum("bhqk,bqhd->bkhd", d_near, query_b, preferred_element_type=f32)
    d_value = jnp.einsum(
        "bhqk,bqhd->bkhd", probs_low[..., :BLOCK], d_context, preferred_element_type=f32
    )
    d_key_far = scale * jnp.einsum("bhqk,bqhd->bhkd", d_far, query_b, preferred_element_type=f32)
    d_value_far = weight_s * jnp.einsum(
        "bhqk,bqhd->bhkd", probs_low[..., BLOCK:], d_context, preferred_element_type=f32
    )
    grad_tiles = jnp.stack([d_key_far.astype(bf16), d_value_far.astype(bf16)], 3).reshape(
        requests, BLOCK * 2 * DH
    )
    peers = jnp.arange(dev_count, dtype=jnp.int32)
    outgoing_grads = jnp.where(
        (owner_mine[None, :] == peers[:, None])[:, :, None], grad_tiles[None], empty_tile
    )
    returned = lax.all_to_all(outgoing_grads, "blk", split_axis=0, concat_axis=0, tiled=True)
    selector = (owner_all == my_index)[:, :, None] & (
        slot_all[:, :, None] == tile_ids[None, None, :]
    )
    selector = selector.reshape(dev_count * requests, requests).astype(bf16)
    remote = jnp.einsum(
        "st,sf->tf",
        selector,
        returned.reshape(dev_count * requests, BLOCK * 2 * DH),
        preferred_element_type=f32,
    )
    remote = (
        remote.reshape(blocks_dev, heads_dev, BLOCK, 2, DH)
        .transpose(0, 2, 3, 1, 4)
        .reshape(tok_rows, 2, width_dev)
    )
    near_kv = (
        jnp.stack([d_key.reshape(tok_rows, width_dev), d_value.reshape(tok_rows, width_dev)], 1)
        + remote
    )
    d_qkv = jnp.concatenate([d_query.reshape(tok_rows, 1, width_dev), near_kv], 1).astype(bf16)
    g_qkv = jnp.einsum("td,tcf->dcf", h_one_low, d_qkv, preferred_element_type=f32)
    d_h_part = jnp.einsum("tcf,dcf->td", d_qkv, w_qkv, preferred_element_type=f32)
    (d_every,) = sink_pull(d_weight.T)
    d_own = lax.psum_scatter(d_every, "blk", scatter_dimension=0, tiled=True) / TEMPER
    d_flat = d_own.reshape(blocks_dev, heads_dev * seq_blocks)
    g_sort = jnp.dot(summary.T, d_flat, precision=HIGHEST)
    d_summary = jnp.dot(d_flat, sort_mat.T, precision=HIGHEST)
    d_h_part = (d_h_part.reshape(blocks_dev, BLOCK, D) + d_summary[:, None, :] / BLOCK).reshape(
        tok_rows, D
    )
    d_h_one = lax.psum(d_h_part, "head")
    g_gain_one = jnp.sum(d_h_one * normed_one, 0)
    d_tokens = d_middle + norm_back(d_h_one, normed_one, inv_one, gain_one)
    summed = lax.psum((g_gain_one, g_gain_two, g_qkv, g_out, g_sort, g_up, g_down), "blk")
    return (
        output,
        d_tokens,
        summed[0],
        summed[1],
        summed[2],
        summed[3],
        summed[4],
        summed[5],
        summed[6],
    )


def mask_pair(values, near):
    zero = jnp.zeros_like(values)
    return jnp.where(near, values, zero), jnp.where(near, zero, values)


def first_lanes():
    return lax.broadcasted_iota(jnp.int32, (1, 2 * DH), 1) < DH


def dot_nn(a, b):
    return lax.dot_general(a, b, (((1,), (0,)), ((), ())), preferred_element_type=jnp.float32)


def dot_nt(a, b):
    return lax.dot_general(a, b, (((1,), (1,)), ((), ())), preferred_element_type=jnp.float32)


def dot_tn(a, b):
    return lax.dot_general(a, b, (((0,), (0,)), ((), ())), preferred_element_type=jnp.float32)


def three_parts(values):
    high = values.astype(jnp.bfloat16)
    rest = values - high.astype(jnp.float32)
    mid = rest.astype(jnp.bfloat16)
    low = (rest - mid.astype(jnp.float32)).astype(jnp.bfloat16)
    return high, mid, low


def norm_parts(values):
    centred = values - jnp.mean(values, -1, keepdims=True)
    inv_std = lax.rsqrt(jnp.mean(centred * centred, -1, keepdims=True) + EPS)
    return centred * inv_std, inv_std


def head_kernel(tokens, gain, noise, h_one, payload):
    f32 = jnp.float32
    rows = tokens.shape[0]
    normed, _ = norm_parts(tokens[...].astype(f32))
    h = normed * gain[...].astype(f32)
    h_one[...] = h.astype(jnp.bfloat16)
    payload[:, :D] = jnp.mean(h.reshape(rows // BLOCK, BLOCK, D), axis=1)
    nb = noise.shape[2]
    payload[:, D : D + nb] = noise[:, 0, :]
    payload[:, D + nb :] = noise[:, 1, :]


def project_kernel(*refs):
    *pieces, weight, out = refs
    at = 0
    for piece in pieces:
        for start in range(0, piece.shape[0], 2 * BLOCK):
            rows = piece[start : start + 2 * BLOCK, :]
            out[at : at + 2 * BLOCK, :] = dot_nn(rows, weight[...]).astype(jnp.bfloat16)
            at += 2 * BLOCK


def sink_kernel(near_rows, far_rows, w_sort, partner, summary, steps, scale_rows, weight_rows):
    f32 = jnp.float32
    me = lax.axis_index("blk")
    nb = partner.shape[0]
    per = near_rows.shape[0] // 4
    noise = weight_rows
    for j in range(8):
        source = near_rows if j < 4 else far_rows
        piece = source[(j % 4) * per : (j % 4 + 1) * per, :]
        distance = (0, 1, 2, 3, 4, 5, 6, 7)[j]
        at = pl.multiple_of((me ^ distance) * per, per)
        summary[pl.ds(at, per), :] = piece[:, :D]
        noise[pl.ds(at, per), :] = piece[:, D:]
    parts = three_parts(summary[...])
    logits = sum(dot_nn(part, w_sort[...]) for part in parts[::-1])
    logits = (logits + noise[...]) / TEMPER
    plan = jnp.stack([logits[:, :nb], logits[:, nb:]])
    for sweep in range(SINK):
        for k, axis in enumerate((2, 1)):
            plan = plan - log_total(plan, axis)
            steps[2 * sweep + k] = jnp.exp(plan)
    final = jnp.exp(plan)
    lanes = lax.broadcasted_iota(jnp.int32, (nb, nb), 1)
    picked = []
    for h in range(2):
        chosen = partner[:, h : h + 1] == lanes
        picked.append(
            nb * jnp.sum(jnp.where(chosen, final[h], 0.0), axis=1, keepdims=True)
        )
    ones = jnp.ones((nb, DH), f32)
    scale_rows[...] = jnp.concatenate([ones, picked[0] * ones, ones, picked[1] * ones], 1)
    weight_rows[...] = jnp.concatenate([picked[0] * ones, picked[1] * ones], 1)


def ring_of(position):
    return jnp.where(position < 4, 2 * position, 2 * (7 - position) + 1)


def place_of(index):
    return jnp.where(index % 2 == 0, index // 2, 7 - index // 2)


def spread(pieces, full, span, core):
    place = place_of(lax.axis_index("blk"))
    for start, rows, ref, ref_start, step in pieces:
        owner = ring_of((place - step + 8) % 8)
        at = pl.multiple_of(owner * span + start, rows)
        full[pl.ds(at, rows), :] = ref[ref_start : ref_start + rows, :]


def far_near(table, at, lanes):
    return table[pl.ds(pl.multiple_of(at * BLOCK, BLOCK), BLOCK), lanes]


def block_operands(qkv, block, first, second, near):
    k_lanes, v_lanes = slice(2 * DH, 4 * DH), slice(4 * DH, 6 * DH)
    query = far_near(qkv, block, slice(0, 2 * DH))
    keys, values = [], []
    for lanes, store in ((k_lanes, keys), (v_lanes, values)):
        own0, own1 = mask_pair(far_near(qkv, block, lanes), near)
        far0, _ = mask_pair(far_near(qkv, first, lanes), near)
        _, far1 = mask_pair(far_near(qkv, second, lanes), near)
        store.extend([own0, far0, own1, far1])
    return query, keys, values


def block_probs(query, keys, scale_row):
    z = dot_nt(query, jnp.concatenate(keys, 0)) * (DH**-0.5)
    scores = z * scale_row
    probs = []
    for h in range(2):
        part = scores[:, h * 2 * DH : (h + 1) * 2 * DH]
        expo = jnp.exp(part - jnp.max(part, -1, keepdims=True))
        probs.append(expo / jnp.sum(expo, -1, keepdims=True))
    return z, probs


def attend_kernel(own, step1, step2, step3, step4, partner, scale_rows, weight_rows, qkv, context):
    me = lax.axis_index("blk")
    core = lax.axis_index("head") % 2
    place = place_of(me)
    rows = own.shape[0]
    half = rows // 2
    quarter = rows // 4

    def put(owner, start, n, ref, ref_start):
        at = pl.multiple_of(owner * rows + start, n)
        qkv[pl.ds(at, n), :] = ref[ref_start : ref_start + n, :]

    put(me, 0, rows, own, 0)
    for step, ref in ((1, step1), (2, step2), (3, step3)):
        for side, owner in enumerate(
            (ring_of((place + 8 - step) % 8), ring_of((place + step) % 8))
        ):
            put(owner, core * half, half, ref, side * 2 * half)
            put(owner, (1 - core) * half, half, ref, side * 2 * half + half)
    owner = ring_of((place + 4) % 8)
    put(owner, core * half, quarter, step4, 0)
    put(owner, (1 - core) * half, quarter, step4, quarter)
    put(owner, core * half + quarter, quarter, step4, 2 * quarter)
    put(owner, (1 - core) * half + quarter, quarter, step4, 3 * quarter)
    near = first_lanes()
    for i in range(rows // BLOCK):
        block = me * (rows // BLOCK) + i
        query, keys, values = block_operands(
            qkv, block, partner[block, 0], partner[block, 1], near
        )
        scale_row = scale_rows[pl.ds(block, 1), :]
        weight_row = weight_rows[pl.ds(block, 1), :]
        _, probs = block_probs(query, keys, scale_row)
        probs_low = jnp.concatenate([p.astype(jnp.bfloat16) for p in probs], 1)
        none = jnp.zeros_like(values[0])
        table = jnp.concatenate(
            [
                jnp.concatenate([values[0], none, values[2], none], 0),
                jnp.concatenate([none, values[1], none, values[3]], 0),
            ],
            1,
        )
        out = dot_nn(probs_low, table)
        ctx = out[:, : 2 * DH] + weight_row * out[:, 2 * DH :]
        context[i * BLOCK : (i + 1) * BLOCK, :] = ctx.astype(jnp.bfloat16)


def feed_kernel(
    tokens, cotangent, gain, ctx0, ctx1, ctx2, ctx3, wo0, wo1, wo2, wo3, up_a, up_b, down_a, down_b,
    middle, h_two, active, d_hidden, ffn, d_h_two,
    ctx_full, wo_full, up_full, down_full,
):
    f32, bf16 = jnp.float32, jnp.bfloat16
    hd = lax.axis_index("head")
    row = hd // 2
    width = ctx0.shape[1]
    ff = up_a.shape[1]
    for j, (c, w) in enumerate(((ctx0, wo0), (ctx1, wo1), (ctx2, wo2), (ctx3, wo3))):
        at = pl.multiple_of((hd ^ j) * width, width)
        ctx_full[:, pl.ds(at, width)] = c[...]
        wo_full[pl.ds(at, width), :] = w[...]
    for j, (u, w) in enumerate(((up_a, down_a), (up_b, down_b))):
        at = pl.multiple_of((row ^ j) * ff, ff)
        up_full[:, pl.ds(at, ff)] = u[...]
        down_full[pl.ds(at, ff), :] = w[...]
    chunk = 256
    for start in range(0, tokens.shape[0], chunk):
        sl = slice(start, start + chunk)
        mid = tokens[sl, :].astype(f32) + dot_nn(ctx_full[sl, :], wo_full[...])
        middle[sl, :] = mid
        normed, _ = norm_parts(mid)
        low = (normed * gain[...].astype(f32)).astype(bf16)
        h_two[sl, :] = low
        ffn_sum = None
        back_sum = None
        for j in range(2):
            cols = slice(j * ff, (j + 1) * ff)
            pre = dot_nn(low, up_full[:, cols])
            d_act = dot_nt(cotangent[sl, :], down_full[cols, :])
            bell = 0.5 * (1.0 + lax.erf(pre * ROOT_HALF))
            act = (pre * bell).astype(bf16)
            slope = bell + pre * jnp.exp(-0.5 * pre * pre) * INV_ROOT_TWO_PI
            d_pre = (d_act * slope).astype(bf16)

            @pl.when(row == j)
            def _():
                active[sl, :] = act
                d_hidden[sl, :] = d_pre

            f = dot_nn(act, down_full[cols, :])
            b = dot_nt(d_pre, up_full[:, cols])
            ffn_sum = f if ffn_sum is None else ffn_sum + f
            back_sum = b if back_sum is None else back_sum + b
        ffn[sl, :] = ffn_sum
        d_h_two[sl, :] = back_sum


def back_kernel(middle, own, other, cotangent, gain, w_out, d_middle, d_low, d_ctx, g_gain):
    f32, bf16 = jnp.float32, jnp.bfloat16
    normed, inv = norm_parts(middle[...])
    d_h = own[...] + other[...]
    g_gain[...] = jnp.broadcast_to(jnp.sum(d_h * normed, 0, keepdims=True), g_gain.shape)
    d_mid = cotangent[...].astype(f32) + norm_back(d_h, normed, inv, gain[...].astype(f32))
    d_middle[...] = d_mid
    low = d_mid.astype(bf16)
    d_low[...] = low
    d_ctx[...] = dot_nt(low, w_out[...]).astype(bf16)


def grads_kernel(h_two, d_hidden, active, cotangent, context, d_low, keep, send, total):
    f = h_two.shape[1]
    total[:f, :] = dot_tn(h_two[...], d_hidden[...])
    ff = active.shape[1]
    total[f : f + ff, :] = dot_tn(active[...], cotangent[...])
    total[f + ff :, :] = dot_tn(context[...], d_low[...])
    bit = lax.axis_index("blk") & 1
    half = keep.shape[0]
    keep[...] = total[pl.ds(pl.multiple_of(bit * half, 16), half), :]
    send[...] = total[pl.ds(pl.multiple_of((1 - bit) * half, 16), half), :].astype(jnp.bfloat16)


def merge_kernel(shift, held, arrived, keep, send, total):
    total[...] = held[...] + arrived[...].astype(jnp.float32)
    bit = (lax.axis_index("blk") >> shift) & 1
    half = keep.shape[0]
    keep[...] = total[pl.ds(pl.multiple_of(bit * half, 16), half), :]
    send[...] = total[pl.ds(pl.multiple_of((1 - bit) * half, 16), half), :].astype(jnp.bfloat16)


def lay_kernel(here, there, g_up, g_down, g_out, total):
    me = lax.axis_index("blk")
    n = here.shape[0] // 4
    for j in range(8):
        ref = here if j < 4 else there
        source = me ^ ((0, 4, 2, 6)[j % 4] + j // 4)
        at = (source & 1) * (4 * n) + ((source >> 1) & 1) * (2 * n) + (source >> 2) * n
        total[pl.ds(pl.multiple_of(at, 16), n), :] = ref[(j % 4) * n : (j % 4 + 1) * n, :]
    f = g_up.shape[0]
    ff = g_down.shape[0]
    g_up[...] = total[:f, :].astype(jnp.float32)
    g_down[...] = total[f : f + ff, :].astype(jnp.float32)
    g_out[...] = total[f + ff :, :].astype(jnp.float32)


def pull_kernel(
    qkv, own, f1, b1, f2, b2, f3, b3, f4, b4, partner, scale_rows, weight_rows,
    d_qkv, d_weight, d_ctx, acc_k, acc_v,
):
    f32, bf16 = jnp.float32, jnp.bfloat16
    me = lax.axis_index("blk")
    place = place_of(me)
    rows = own.shape[0]
    half = rows // 2

    def put(owner, start, ref):
        n = ref.shape[0]
        d_ctx[pl.ds(pl.multiple_of(owner * rows + start, n), n), :] = ref[...]

    put(me, 0, own)
    for step, (f, b) in enumerate(((f1, b1), (f2, b2), (f3, b3)), 1):
        put(ring_of((place + 8 - step) % 8), 0, f)
        put(ring_of((place + step) % 8), 0, b)
    far = ring_of((place + 4) % 8)
    put(far, 0, f4)
    put(far, half, b4)
    near = first_lanes()
    acc_k[...] = jnp.zeros_like(acc_k)
    acc_v[...] = jnp.zeros_like(acc_v)
    scale = DH**-0.5

    def add(acc, at, tile):
        place_at = pl.ds(pl.multiple_of(at * BLOCK, BLOCK), BLOCK)
        acc[place_at, :] += tile

    def one(block):
        first, second = partner[block, 0], partner[block, 1]
        query, keys, values = block_operands(qkv, block, first, second, near)
        scale_row = scale_rows[pl.ds(block, 1), :]
        weight_row = weight_rows[pl.ds(block, 1), :]
        z, probs = block_probs(query, keys, scale_row)
        probs = jnp.concatenate(probs, 1)
        probs_low = probs.astype(bf16)
        d_out = far_near(d_ctx, block, slice(0, 2 * DH))
        d_raw = dot_nt(d_out, jnp.concatenate(values, 0))
        d_probs = d_raw * scale_row
        weighted = d_probs * probs
        sums = [
            jnp.sum(weighted[:, h * 2 * DH : (h + 1) * 2 * DH], -1, keepdims=True) for h in range(2)
        ]
        spread_sums = jnp.concatenate([jnp.broadcast_to(s, (BLOCK, 2 * DH)) for s in sums], 1)
        d_scores = probs * (d_probs - spread_sums)
        d_z = (d_scores * scale_row).astype(bf16)
        d_weight[pl.ds(block, 1), :] = jnp.sum(
            d_scores * z + probs_low.astype(f32) * d_raw, 0, keepdims=True
        )
        d_query = dot_nn(d_z, jnp.concatenate(keys, 0)) * scale
        at = pl.ds(pl.multiple_of(block * BLOCK, BLOCK), BLOCK)
        d_qkv[at, : 2 * DH] = d_query.astype(bf16)
        d_keys = dot_tn(d_z, query) * scale
        d_values = dot_tn(probs_low, d_out)
        for acc, grads, far_scale in ((acc_k, d_keys, None), (acc_v, d_values, weight_row)):
            parts = [grads[i * BLOCK : (i + 1) * BLOCK, :] for i in range(4)]
            far0, far1 = parts[1], parts[3]
            if far_scale is not None:
                far0, far1 = far0 * far_scale, far1 * far_scale
            far0 = far0.astype(bf16).astype(f32)
            far1 = far1.astype(bf16).astype(f32)
            add(acc, block, jnp.where(near, parts[0], parts[2]))
            add(acc, first, jnp.where(near, far0, 0.0))
            add(acc, second, jnp.where(near, 0.0, far1))

    def body(i, _):
        one(i)
        return 0

    lax.fori_loop(0, partner.shape[0], body, 0, unroll=2)
    d_qkv[:, 2 * DH : 4 * DH] = acc_k[...].astype(bf16)
    d_qkv[:, 4 * DH :] = acc_v[...].astype(bf16)


def sink_back_kernel(d_weight, steps, partner, summary, d_flat, g_sort):
    nb = partner.shape[0]
    lanes = lax.broadcasted_iota(jnp.int32, (nb, nb), 1)
    grads = []
    for h in range(2):
        chosen = partner[:, h : h + 1] == lanes
        total = jnp.sum(
            d_weight[:, (2 * h + 1) * DH : (2 * h + 2) * DH], axis=1, keepdims=True
        )
        grads.append(jnp.where(chosen, nb * total, 0.0))
    last = steps.shape[0] - 1
    grad = jnp.stack(grads) * steps[last]
    for t in range(last, -1, -1):
        grad = grad - steps[t] * jnp.sum(grad, axis=1 if t % 2 else 2, keepdims=True)
    flat = jnp.concatenate([grad[0], grad[1]], 1) / TEMPER
    d_flat[...] = flat
    g_sort[...] = lax.dot_general(
        summary[...],
        flat,
        (((0,), (0,)), ((), ())),
        precision=HIGHEST,
        preferred_element_type=jnp.float32,
    )


def weight_kernel(*refs):
    own, f1, b1, f2, b2, f3, b3, f4, b4, xf1, xb1, xf2, xb2, xf3, xb3, xf4, xb4 = refs[:17]
    d_qkv, g_qkv, h_all = refs[17:]
    me = lax.axis_index("blk")
    core = lax.axis_index("head") % 2
    place = place_of(me)
    rows = own.shape[0]
    half, quarter = rows // 2, rows // 4

    def put(owner, start, ref):
        n = ref.shape[0]
        h_all[pl.ds(pl.multiple_of(owner * rows + start, n), n), :] = ref[...]

    put(me, 0, own)
    for step, (f, b, xf, xb) in enumerate(
        ((f1, b1, xf1, xb1), (f2, b2, xf2, xb2), (f3, b3, xf3, xb3)), 1
    ):
        for owner, a, o in (
            (ring_of((place + 8 - step) % 8), f, xf),
            (ring_of((place + step) % 8), b, xb),
        ):
            put(owner, core * half, a)
            put(owner, (1 - core) * half, o)
    far = ring_of((place + 4) % 8)
    put(far, core * half, f4)
    put(far, (1 - core) * half, xf4)
    put(far, core * half + quarter, b4)
    put(far, (1 - core) * half + quarter, xb4)
    out = dot_tn(h_all[...], d_qkv[...])
    width = g_qkv.shape[2]
    for i in range(3):
        g_qkv[:, i, :] = out[:, i * width : (i + 1) * width]


def input_kernel(dq_a, dq_b, w_a, w_b, flat_a, flat_b, sort_a, sort_b, d_h, dq_full, w_full, flat_full, sort_full):
    row = lax.axis_index("head") // 2
    width = dq_a.shape[1]
    for j, (g, w) in enumerate(((dq_a, w_a), (dq_b, w_b))):
        at = pl.multiple_of((row ^ j) * width, width)
        dq_full[:, pl.ds(at, width)] = g[...]
        w_full[:, pl.ds(at, width)] = w[...]
    part = dot_nt(dq_full[...], w_full[...])
    nb = flat_a.shape[1]
    for j, (flat, sort) in enumerate(((flat_a, sort_a), (flat_b, sort_b))):
        at = pl.multiple_of((row ^ j) * nb, nb)
        flat_full[:, pl.ds(at, nb)] = flat[...]
        sort_full[:, pl.ds(at, nb)] = sort[...]
    d_sum = sum(dot_nt(p, sort_full[...]) for p in three_parts(flat_full[...])[::-1]) / BLOCK
    blocks = d_sum.shape[0]
    for i in range(blocks):
        sl = slice(i * BLOCK, (i + 1) * BLOCK)
        d_h[sl, :] = part[sl, :] + d_sum[i : i + 1, :]


def end_kernel(tokens, gain, own, other, d_middle, d_tokens, g_gain):
    f32 = jnp.float32
    normed, inv = norm_parts(tokens[...].astype(f32))
    d_h = own[...] + other[...]
    g_gain[...] = jnp.broadcast_to(jnp.sum(d_h * normed, 0, keepdims=True), g_gain.shape)
    d_tokens[...] = d_middle[...] + norm_back(d_h, normed, inv, gain[...].astype(f32))


VMEM_SPEC = pl.BlockSpec(memory_space=pltpu.VMEM)
SMEM_SPEC = pl.BlockSpec(memory_space=pltpu.SMEM)


def call(kernel, outs, *args, scratch=(), smem=(), flops=0, name=None):
    shapes = [jax.ShapeDtypeStruct(s, d) for s, d in outs]
    moved = sum(a.size * a.dtype.itemsize for a in args) + sum(
        math.prod(s) * jnp.dtype(d).itemsize for s, d in outs
    )
    result = pl.pallas_call(
        kernel,
        out_shape=shapes,
        in_specs=[SMEM_SPEC if i in smem else VMEM_SPEC for i in range(len(args))],
        out_specs=[VMEM_SPEC] * len(shapes),
        scratch_shapes=[pltpu.VMEM(s, d) for s, d in scratch],
        compiler_params=pltpu.CompilerParams(vmem_limit_bytes=VMEM_LIMIT),

        name=name,
    )(*args)
    return result[0] if len(shapes) == 1 else result


RING = (0, 2, 4, 6, 7, 5, 3, 1)


def local_eight(
    tokens, gain_attn, gain_ffn, w_qkv, w_out, w_sort, w_up, w_down, gumbel_noise, partner, cotangent
):
    f32, bf16 = jnp.float32, jnp.bfloat16
    rows = tokens.shape[0]
    blocks = rows // BLOCK
    width = w_out.shape[0]
    ff = w_up.shape[1]
    nb = partner.shape[0]
    total = nb * BLOCK
    half, quarter = rows // 2, rows // 4
    core = lax.axis_index("head") % 2

    def ahead(v):
        return lax.ppermute(v, "blk", [(RING[i], RING[(i + 1) % 8]) for i in range(8)])

    def behind(v):
        return lax.ppermute(v, "blk", [(RING[i], RING[(i - 1) % 8]) for i in range(8)])

    def swap_head(v, j):
        return lax.ppermute(v, "head", [(i, i ^ j) for i in range(4)])

    def swap_blk(v, j):
        return lax.ppermute(v, "blk", [(i, i ^ j) for i in range(8)])

    gain_one = gain_attn.reshape(1, D)
    gain_two = gain_ffn.reshape(1, D)
    w_in = w_qkv.reshape(D, 3 * width)

    h_one, payload = call(
        head_kernel, [((rows, D), bf16), ((blocks, D + 2 * nb), f32)], tokens, gain_one, gumbel_noise,
        name="norm_one",
    )
    mine = lax.dynamic_slice_in_dim(h_one, core * half, half, 0)
    ring_f, ring_b = [mine], [mine]
    for step in range(3):
        ring_f.append(ahead(ring_f[-1]))
        ring_b.append(behind(ring_b[-1]))
    ring_f.append(ahead(ring_f[-1][:quarter]))
    ring_b.append(behind(ring_b[-1][quarter:]))
    ring_f, ring_b = ring_f[1:], ring_b[1:]
    other_f = [swap_head(v, 1) for v in ring_f]
    other_b = [swap_head(v, 1) for v in ring_b]

    pay = jnp.concatenate([payload, swap_blk(payload, 1)], 0)
    pay = jnp.concatenate([pay, swap_blk(pay, 2)], 0)
    pay_far = swap_blk(pay, 4)

    wo_y = swap_head(w_out, 2)
    wo_c = swap_head(w_out, 1)
    wo_yc = swap_head(wo_y, 1)
    up_y = swap_head(w_up, 2)
    down_y = swap_head(w_down, 2)
    in_y = swap_head(w_in, 2)
    sort_y = swap_head(w_sort, 2)

    project = lambda *v: call(
        project_kernel, [((sum(x.shape[0] for x in v), 3 * width), bf16)], *v, w_in, name="project",
        flops=2 * sum(x.shape[0] for x in v) * 3 * width * D,
    )
    qkv_own = project(h_one)
    qkv_steps = [
        project(ring_f[s], other_f[s], ring_b[s], other_b[s]) for s in range(4)
    ]
    summary, steps, scale_rows, weight_rows = call(
        sink_kernel,
        [
            ((nb, D), f32),
            ((2 * SINK, 2, nb, nb), f32),
            ((nb, 4 * DH), f32),
            ((nb, 2 * DH), f32),
        ],
        pay, pay_far, w_sort, partner, name="sinkhorn",
    )
    qkv, context = call(
        attend_kernel,
        [((total, 3 * width), bf16), ((rows, width), bf16)],
        qkv_own, *qkv_steps, partner, scale_rows, weight_rows, smem=(5,), name="attend",
    )
    ctx_y = swap_head(context, 2)
    ctx_c = swap_head(context, 1)
    ctx_yc = swap_head(ctx_y, 1)
    middle, h_two, active, d_hidden, ffn, d_h_two = call(
        feed_kernel,
        [
            ((rows, D), f32),
            ((rows, D), bf16),
            ((rows, ff), bf16),
            ((rows, ff), bf16),
            ((rows, D), f32),
            ((rows, D), f32),
        ],
        tokens, cotangent, gain_two, context, ctx_c, ctx_y, ctx_yc, w_out, wo_c, wo_y, wo_yc,
        w_up, up_y, w_down, down_y,
        scratch=[((rows, 4 * width), bf16), ((4 * width, D), bf16), ((D, 2 * ff), bf16), ((2 * ff, D), bf16)],
        name="feed", flops=18 * rows * D * ff,
    )
    d_h_two_other = swap_head(d_h_two, 1)
    ffn_other = swap_head(ffn, 1)
    d_middle, d_low, d_ctx, g_two = call(
        back_kernel,
        [((rows, D), f32), ((rows, D), bf16), ((rows, width), bf16), ((8, D), f32)],
        middle, d_h_two, d_h_two_other, cotangent, gain_two, w_out, name="back",
    )
    out_f, out_b = [d_ctx], [d_ctx]
    for step in range(3):
        out_f.append(ahead(out_f[-1]))
        out_b.append(behind(out_b[-1]))
    out_f.append(ahead(out_f[-1][:half]))
    out_b.append(behind(out_b[-1][half:]))
    stack = D + ff + width
    keep, send = call(
        grads_kernel,
        [((stack // 2, D), f32), ((stack // 2, D), bf16)],
        h_two, d_hidden, active, cotangent, context, d_low,
        scratch=[((stack, D), f32)], name="grads", flops=2 * rows * D * stack,
    )
    for shift in (1, 2):
        n = keep.shape[0]
        keep, send = call(
            functools.partial(merge_kernel, shift),
            [((n // 2, D), f32), ((n // 2, D), bf16)],
            keep, swap_blk(send, 1 << (shift - 1)), scratch=[((n, D), f32)], name="merge",
        )
    owned = (keep + swap_blk(send, 4).astype(f32)).astype(bf16)
    owned = jnp.concatenate([owned, swap_blk(owned, 4)], 0)
    owned = jnp.concatenate([owned, swap_blk(owned, 2)], 0)
    g_up, g_down, g_out = call(
        lay_kernel,
        [((D, ff), f32), ((ff, D), f32), ((width, D), f32)],
        owned, swap_blk(owned, 1), scratch=[((stack, D), bf16)], name="lay",
    )
    output = middle + (ffn + ffn_other)
    d_qkv, d_weight = call(
        pull_kernel,
        [((total, 3 * width), bf16), ((nb, 4 * DH), f32)],
        qkv, d_ctx, out_f[1], out_b[1], out_f[2], out_b[2], out_f[3], out_b[3], out_f[4], out_b[4],
        partner, scale_rows, weight_rows, smem=(10,),
        scratch=[((total, width), bf16), ((total, width), f32), ((total, width), f32)],
        name="pull",
    )
    d_flat, g_sort = call(
        sink_back_kernel,
        [((nb, 2 * nb), f32), ((D, 2 * nb), f32)],
        d_weight, steps, partner, summary, name="sinkhorn_back",
    )
    me = lax.axis_index("blk")
    d_mine = lax.dynamic_slice_in_dim(d_qkv, me * rows, rows, 0)
    flat_mine = lax.dynamic_slice_in_dim(d_flat, me * blocks, blocks, 0)
    d_mine_y = swap_head(d_mine, 2)
    flat_y = swap_head(flat_mine, 2)
    d_h = call(
        input_kernel, [((rows, D), f32)],
        d_mine, d_mine_y, w_in, in_y, flat_mine, flat_y, w_sort, sort_y,
        scratch=[
            ((rows, 6 * width), bf16), ((D, 6 * width), bf16), ((blocks, 4 * nb), f32), ((D, 4 * nb), bf16),
        ],
        name="input_back",
    )
    d_tokens, g_one = call(
        end_kernel, [((rows, D), f32), ((8, D), f32)],
        tokens, gain_one, d_h, swap_head(d_h, 1), d_middle, name="norm_one_back",
    )
    gains = jnp.concatenate([g_one, g_two], 1)
    for j in (1, 2, 4):
        gains = gains + swap_blk(gains, j)
    g_qkv = call(
        weight_kernel, [((D, 3, width), f32)],
        h_one, ring_f[0], ring_b[0], ring_f[1], ring_b[1], ring_f[2], ring_b[2], ring_f[3], ring_b[3],
        other_f[0], other_b[0], other_f[1], other_b[1], other_f[2], other_b[2], other_f[3], other_b[3],
        d_qkv, scratch=[((total, D), bf16)], name="weights",
    )
    return output, d_tokens, gains[0, :D], gains[0, D:], g_qkv, g_out, g_sort, g_up, g_down


def solution(mesh):
    in_specs = (
        P("blk", None),
        P(),
        P(),
        P(None, None, "head"),
        P("head", None),
        P(None, "head"),
        P(None, "head"),
        P("head", None),
        P("blk", "head", None),
        P(None, "head"),
        P("blk", None),
    )
    out_specs = (
        P("blk", None),
        P("blk", None),
        P(),
        P(),
        P(None, None, "head"),
        P("head", None),
        P(None, "head"),
        P(None, "head"),
        P("head", None),
    )
    plan = local_eight if mesh.shape["blk"] == 8 and mesh.shape["head"] == 4 else local
    return jax.shard_map(plan, mesh=mesh, in_specs=in_specs, out_specs=out_specs, check_vma=False)
```

```python
import functools
import math

import jax
import jax.numpy as jnp
from jax import lax
from jax.experimental import pallas as pl
from jax.experimental.pallas import tpu as pltpu
from jax.sharding import PartitionSpec as P

D = 512
DH = 64
BLOCK = 64
SINK = 8


EPS = 1e-05
TEMPER = 0.75
ROOT_HALF = 0.7071067811865476
INV_ROOT_TWO_PI = 0.3989422804014327
HIGHEST = lax.Precision.HIGHEST


def normalize(values, norm_gain):
    average = jnp.mean(values, -1, keepdims=True)
    centred = values - average
    inv_std = lax.rsqrt(jnp.mean(centred * centred, -1, keepdims=True) + EPS)
    normed = centred * inv_std
    return (normed * norm_gain, normed, inv_std)


def norm_back(d_out, normed, inv_std, norm_gain):
    d_normed = d_out * norm_gain
    return inv_std * (
        d_normed
        - jnp.mean(d_normed, -1, keepdims=True)
        - normed * jnp.mean(d_normed * normed, -1, keepdims=True)
    )


def log_total(values, axis):
    highest = jnp.max(values, axis=axis, keepdims=True)
    return highest + jnp.log(jnp.sum(jnp.exp(values - highest), axis=axis, keepdims=True))


def balancing_log_space(sort_logits):
    for sweep in range(SINK):
        sort_logits = sort_logits - log_total(sort_logits, 2)
        sort_logits = sort_logits - log_total(sort_logits, 1)
    return sort_logits


def gelu_value(values):
    return 0.5 * values * (1.0 + lax.erf(values * ROOT_HALF))


def gelu_slope(values):
    return (
        0.5 * (1.0 + lax.erf(values * ROOT_HALF))
        + values * jnp.exp(-0.5 * values * values) * INV_ROOT_TWO_PI
    )


def local(
    tokens,
    gain_attn,
    gain_ffn,
    w_qkv,
    w_out,
    w_sort,
    w_up,
    w_down,
    gumbel_noise,
    partner,
    cotangent,
):
    f32 = jnp.float32
    bf16 = jnp.bfloat16
    tok_rows = tokens.shape[0]
    blocks_dev = tok_rows // BLOCK
    heads_dev = w_out.shape[0] // DH
    width_dev = heads_dev * DH
    requests = blocks_dev * heads_dev
    dev_count = lax.axis_size("blk")
    my_index = lax.axis_index("blk")
    first_block = my_index * blocks_dev
    seq_blocks = partner.shape[0]
    scale = DH ** (-0.5)
    gain_one = gain_attn.astype(f32)
    gain_two = gain_ffn.astype(f32)
    inputs = tokens.astype(f32)
    h_one, normed_one, inv_one = normalize(inputs, gain_one)
    h_one_low = h_one.astype(bf16)
    qkv = jnp.einsum("td,dcf->tcf", h_one_low, w_qkv, preferred_element_type=f32).astype(bf16)
    summary = jnp.mean(h_one.reshape(blocks_dev, BLOCK, D), axis=1)
    sort_mat = w_sort.astype(f32)
    own_rows = (
        jnp.dot(summary, sort_mat, precision=HIGHEST).reshape(blocks_dev, heads_dev, seq_blocks)
        + gumbel_noise
    ) / TEMPER
    every_rows = lax.all_gather(own_rows, "blk", axis=0, tiled=True)
    my_partner = lax.dynamic_slice_in_dim(partner, first_block, blocks_dev, 0)

    def own_weights(sequence_rows):
        balanced_plan = balancing_log_space(sequence_rows.transpose(1, 0, 2))
        mine = lax.dynamic_slice_in_dim(jnp.exp(balanced_plan), first_block, blocks_dev, 1)
        return seq_blocks * jnp.take_along_axis(mine, my_partner.T[:, :, None], axis=2)[:, :, 0]

    weight_hb, sink_pull = jax.vjp(own_weights, every_rows)
    weight_matrix = weight_hb.T
    owner_all = (partner // blocks_dev).reshape(dev_count, requests)
    slot_all = (
        partner % blocks_dev * heads_dev + jnp.arange(heads_dev, dtype=jnp.int32)[None, :]
    ).reshape(dev_count, requests)
    owner_mine = lax.dynamic_index_in_dim(owner_all, my_index, 0, keepdims=False)
    tile_ids = jnp.arange(requests, dtype=jnp.int32)
    key_value = (
        qkv[:, 1:3]
        .reshape(blocks_dev, BLOCK, 2, heads_dev, DH)
        .transpose(0, 3, 1, 2, 4)
        .reshape(requests, BLOCK, 2 * DH)
    )
    empty_tile = jnp.zeros((), bf16)
    wanted = owner_all == my_index
    outgoing = jnp.where(
        wanted[:, :, None, None], jnp.take(key_value, slot_all, axis=0), empty_tile
    )
    incoming = lax.all_to_all(outgoing, "blk", split_axis=0, concat_axis=0, tiled=True)
    partner_tiles = jnp.sum(incoming, axis=0, dtype=f32).astype(bf16)
    far_tiles = partner_tiles.reshape(blocks_dev, heads_dev, BLOCK, 2, DH)
    key_far = far_tiles[:, :, :, 0]
    value_far = far_tiles[:, :, :, 1]
    query_b = qkv[:, 0].reshape(blocks_dev, BLOCK, heads_dev, DH)
    key_b = qkv[:, 1].reshape(blocks_dev, BLOCK, heads_dev, DH)
    value_b = qkv[:, 2].reshape(blocks_dev, BLOCK, heads_dev, DH)
    weight_s = weight_matrix[:, :, None, None]

    def score_parts():
        near_z = scale * jnp.einsum("bqhd,bkhd->bhqk", query_b, key_b, preferred_element_type=f32)
        far_z = scale * jnp.einsum("bqhd,bhkd->bhqk", query_b, key_far, preferred_element_type=f32)
        return (near_z, far_z, jnp.concatenate([near_z, weight_s * far_z], -1))

    near_z, far_z, scores = score_parts()
    highest = jnp.max(scores, -1, keepdims=True)
    expo = jnp.exp(scores - highest)
    row_total = jnp.sum(expo, -1, keepdims=True)
    log_sum = highest + jnp.log(row_total)
    probs_low = (expo / row_total).astype(bf16)
    near_ctx = jnp.einsum(
        "bhqk,bkhd->bqhd", probs_low[..., :BLOCK], value_b, preferred_element_type=f32
    )
    far_ctx = jnp.einsum(
        "bhqk,bhkd->bqhd", probs_low[..., BLOCK:], value_far, preferred_element_type=f32
    )
    context = near_ctx + weight_matrix[:, None, :, None] * far_ctx
    context_low = context.reshape(tok_rows, width_dev).astype(bf16)
    attn = lax.psum(jnp.dot(context_low, w_out, preferred_element_type=f32), "head")
    middle = inputs + attn
    h_two, normed_two, inv_two = normalize(middle, gain_two)
    h_two_low = h_two.astype(bf16)
    hidden_pre = jnp.dot(h_two_low, w_up, preferred_element_type=f32)
    active_low = gelu_value(hidden_pre).astype(bf16)
    ffn = lax.psum(
        jnp.dot(active_low, w_down, preferred_element_type=f32).astype(jnp.bfloat16), "head"
    ).astype(jnp.float32)
    output = middle + ffn
    g_down = jnp.einsum("tf,td->fd", active_low, cotangent, preferred_element_type=f32)
    d_active = jnp.einsum("td,fd->tf", cotangent, w_down, preferred_element_type=f32)
    d_hidden = (d_active * gelu_slope(hidden_pre)).astype(bf16)
    g_up = jnp.einsum("td,tf->df", h_two_low, d_hidden, preferred_element_type=f32)
    d_h_two = lax.psum(jnp.einsum("tf,df->td", d_hidden, w_up, preferred_element_type=f32), "head")
    g_gain_two = jnp.sum(d_h_two * normed_two, 0)
    d_middle = cotangent.astype(f32) + norm_back(d_h_two, normed_two, inv_two, gain_two)
    d_attn_low = d_middle.astype(bf16)
    g_out = jnp.einsum("tf,td->fd", context_low, d_attn_low, preferred_element_type=f32)
    d_context = jnp.einsum("td,fd->tf", d_attn_low, w_out, preferred_element_type=f32).astype(bf16)
    d_context = d_context.reshape(blocks_dev, BLOCK, heads_dev, DH)
    near_z, far_z, scores = score_parts()
    probs = jnp.exp(scores - log_sum)
    probs_low = probs.astype(bf16)
    far_ctx = jnp.einsum(
        "bhqk,bhkd->bqhd", probs_low[..., BLOCK:], value_far, preferred_element_type=f32
    )
    d_probs_near = jnp.einsum("bqhd,bkhd->bhqk", d_context, value_b, preferred_element_type=f32)
    d_probs_far = weight_s * jnp.einsum(
        "bqhd,bhkd->bhqk", d_context, value_far, preferred_element_type=f32
    )
    d_probs = jnp.concatenate([d_probs_near, d_probs_far], -1)
    d_scores = probs * (d_probs - jnp.sum(d_probs * probs, -1, keepdims=True))
    d_near = d_scores[..., :BLOCK].astype(bf16)
    d_far_raw = d_scores[..., BLOCK:]
    d_far = (weight_s * d_far_raw).astype(bf16)
    d_weight = jnp.sum(d_far_raw * far_z, (2, 3)) + jnp.sum(d_context.astype(f32) * far_ctx, (1, 3))
    d_query = scale * (
        jnp.einsum("bhqk,bkhd->bqhd", d_near, key_b, preferred_element_type=f32)
        + jnp.einsum("bhqk,bhkd->bqhd", d_far, key_far, preferred_element_type=f32)
    )
    d_key = scale * jnp.einsum("bhqk,bqhd->bkhd", d_near, query_b, preferred_element_type=f32)
    d_value = jnp.einsum(
        "bhqk,bqhd->bkhd", probs_low[..., :BLOCK], d_context, preferred_element_type=f32
    )
    d_key_far = scale * jnp.einsum("bhqk,bqhd->bhkd", d_far, query_b, preferred_element_type=f32)
    d_value_far = weight_s * jnp.einsum(
        "bhqk,bqhd->bhkd", probs_low[..., BLOCK:], d_context, preferred_element_type=f32
    )
    grad_tiles = jnp.stack([d_key_far.astype(bf16), d_value_far.astype(bf16)], 3).reshape(
        requests, BLOCK * 2 * DH
    )
    peers = jnp.arange(dev_count, dtype=jnp.int32)
    outgoing_grads = jnp.where(
        (owner_mine[None, :] == peers[:, None])[:, :, None], grad_tiles[None], empty_tile
    )
    returned = lax.all_to_all(outgoing_grads, "blk", split_axis=0, concat_axis=0, tiled=True)
    selector = (owner_all == my_index)[:, :, None] & (
        slot_all[:, :, None] == tile_ids[None, None, :]
    )
    selector = selector.reshape(dev_count * requests, requests).astype(bf16)
    remote = jnp.einsum(
        "st,sf->tf",
        selector,
        returned.reshape(dev_count * requests, BLOCK * 2 * DH),
        preferred_element_type=f32,
    )
    remote = (
        remote.reshape(blocks_dev, heads_dev, BLOCK, 2, DH)
        .transpose(0, 2, 3, 1, 4)
        .reshape(tok_rows, 2, width_dev)
    )
    near_kv = (
        jnp.stack([d_key.reshape(tok_rows, width_dev), d_value.reshape(tok_rows, width_dev)], 1)
        + remote
    )
    d_qkv = jnp.concatenate([d_query.reshape(tok_rows, 1, width_dev), near_kv], 1).astype(bf16)
    g_qkv = jnp.einsum("td,tcf->dcf", h_one_low, d_qkv, preferred_element_type=f32)
    d_h_part = jnp.einsum("tcf,dcf->td", d_qkv, w_qkv, preferred_element_type=f32)
    (d_every,) = sink_pull(d_weight.T)
    d_own = lax.psum_scatter(d_every, "blk", scatter_dimension=0, tiled=True) / TEMPER
    d_flat = d_own.reshape(blocks_dev, heads_dev * seq_blocks)
    g_sort = jnp.dot(summary.T, d_flat, precision=HIGHEST)
    d_summary = jnp.dot(d_flat, sort_mat.T, precision=HIGHEST)
    d_h_part = (d_h_part.reshape(blocks_dev, BLOCK, D) + d_summary[:, None, :] / BLOCK).reshape(
        tok_rows, D
    )
    d_h_one = lax.psum(d_h_part, "head")
    g_gain_one = jnp.sum(d_h_one * normed_one, 0)
    d_tokens = d_middle + norm_back(d_h_one, normed_one, inv_one, gain_one)
    summed = lax.psum((g_gain_one, g_gain_two, g_qkv, g_out, g_sort, g_up, g_down), "blk")
    return (
        output,
        d_tokens,
        summed[0],
        summed[1],
        summed[2],
        summed[3],
        summed[4],
        summed[5],
        summed[6],
    )


def mask_pair(values, near):
    zero = jnp.zeros_like(values)
    return jnp.where(near, values, zero), jnp.where(near, zero, values)


def first_lanes():
    return lax.broadcasted_iota(jnp.int32, (1, 2 * DH), 1) < DH


def dot_nn(a, b):
    return lax.dot_general(a, b, (((1,), (0,)), ((), ())), preferred_element_type=jnp.float32)


def dot_nt(a, b):
    return lax.dot_general(a, b, (((1,), (1,)), ((), ())), preferred_element_type=jnp.float32)


def dot_tn(a, b):
    return lax.dot_general(a, b, (((0,), (0,)), ((), ())), preferred_element_type=jnp.float32)


def three_parts(values):
    high = values.astype(jnp.bfloat16)
    rest = values - high.astype(jnp.float32)
    mid = rest.astype(jnp.bfloat16)
    low = (rest - mid.astype(jnp.float32)).astype(jnp.bfloat16)
    return high, mid, low


def norm_parts(values):
    centred = values - jnp.mean(values, -1, keepdims=True)
    inv_std = lax.rsqrt(jnp.mean(centred * centred, -1, keepdims=True) + EPS)
    return centred * inv_std, inv_std


def head_kernel(tokens, gain, noise, h_one, packed, summary, own_noise):
    f32, bf16 = jnp.float32, jnp.bfloat16
    core = lax.axis_index("head") % 2
    rows = tokens.shape[0]
    half, quarter = rows // 2, rows // 4
    normed, _ = norm_parts(tokens[...].astype(f32))
    h = normed * gain[...].astype(f32)
    h_one[...] = h.astype(bf16)
    summary[...] = jnp.mean(h.reshape(rows // BLOCK, BLOCK, D), axis=1)
    blocks = half // BLOCK
    mine = jnp.where(core == 0, summary[:blocks, :], summary[blocks:, :])
    lines = []
    for r in range(2):
        few = noise.shape[0] // 2
        lines.append(
            jnp.concatenate(
                [noise[r * few + i, h : h + 1, :] for i in range(few) for h in range(2)], 1
            )
        )
    for at, values in ((0, mine), (quarter + EXTRA, jnp.concatenate(lines, 0))):
        start = pl.multiple_of(core * half + (0 if at == 0 else quarter), quarter)
        packed[at : at + quarter, :] = h_one[pl.ds(start, quarter), :]
        if at:
            own_noise[...] = values
        parts = [p.astype(f32) for p in three_parts(values)]
        empty = jnp.zeros((EXTRA - 3 * values.shape[0], D), f32)
        packed[at + quarter : at + quarter + EXTRA, :] = jnp.concatenate(parts + [empty], 0).astype(bf16)


def wide(weight):
    return jnp.concatenate([weight[i] for i in range(3)], 1)


def project_own_kernel(h_one, weight, out):
    for start in range(0, h_one.shape[0], 2 * BLOCK):
        sl = slice(start, start + 2 * BLOCK)
        out[sl, :] = dot_nn(h_one[sl, :], wide(weight)).astype(jnp.bfloat16)


def project_kernel(f, xf, b, xb, weight, out, extra):
    quarter = f.shape[0] // 2 - EXTRA
    to = 0
    for piece in (f, xf, b, xb):
        for at in (0, quarter + EXTRA):
            out[to : to + quarter, :] = dot_nn(
                piece[at : at + quarter, :], wide(weight)
            ).astype(jnp.bfloat16)
            to += quarter
    to = 0
    for piece in (f, xf, b, xb):
        for at in (quarter, 2 * quarter + EXTRA):
            extra[to : to + EXTRA, :] = piece[at : at + EXTRA, :]
            to += EXTRA


def ring_of(position):
    return jnp.where(position < 4, 2 * position, 2 * (7 - position) + 1)


def place_of(index):
    return jnp.where(index % 2 == 0, index // 2, 7 - index // 2)


def far_near(table, at, lanes):
    return table[pl.ds(pl.multiple_of(at * BLOCK, BLOCK), BLOCK), lanes]


def block_operands(qkv, block, first, second, near):
    k_lanes, v_lanes = slice(2 * DH, 4 * DH), slice(4 * DH, 6 * DH)
    query = far_near(qkv, block, slice(0, 2 * DH))
    keys, values = [], []
    for lanes, store in ((k_lanes, keys), (v_lanes, values)):
        own0, own1 = mask_pair(far_near(qkv, block, lanes), near)
        far0, _ = mask_pair(far_near(qkv, first, lanes), near)
        _, far1 = mask_pair(far_near(qkv, second, lanes), near)
        store.extend([own0, far0, own1, far1])
    return query, keys, values


def block_probs(scores):
    probs = []
    for h in range(2):
        part = scores[:, h * 2 * DH : (h + 1) * 2 * DH]
        expo = jnp.exp(part - jnp.max(part, -1, keepdims=True))
        probs.append(expo / jnp.sum(expo, -1, keepdims=True))
    return probs


def choices(partner, h):
    nb = partner.shape[1]
    sides = lax.broadcasted_iota(jnp.int32, (nb, nb), 0)
    hot = (sides == partner[h : h + 1, :]).astype(jnp.bfloat16)
    same = sides == lax.broadcasted_iota(jnp.int32, (nb, nb), 1)
    return dot_nt(same.astype(jnp.bfloat16), hot)


def joined(rows, count):
    parts = rows.astype(jnp.float32)
    return (parts[:count] + parts[count : 2 * count]) + parts[2 * count : 3 * count]


def attend_kernel(
    own, step1, step2, step3, extra1, extra2, extra3, f4, b4, xf4, xb4, weight, w_sort,
    own_summary, own_noise, partner, partner_rows,
    qkv, context, summary, steps, scale_rows, weight_rows, noise,
):
    f32, bf16 = jnp.float32, jnp.bfloat16
    me = lax.axis_index("blk")
    core = lax.axis_index("head") % 2
    place = place_of(me)
    nb = partner_rows.shape[1]
    rows = own.shape[0]
    half, quarter = rows // 2, rows // 4
    blocks = rows // BLOCK
    few = blocks // 2

    def put_noise(owner, values):
        lines = [
            values[r : r + 1, i * 2 * nb : (i + 1) * 2 * nb] for r in range(2) for i in range(few)
        ]
        at = pl.multiple_of(owner * blocks, blocks)
        noise[pl.ds(at, blocks), :] = jnp.concatenate(lines, 0)

    def put_summary(owner, mine, other):
        both = jnp.where(
            core == 0, jnp.concatenate([mine, other], 0), jnp.concatenate([other, mine], 0)
        )
        summary[pl.ds(pl.multiple_of(owner * blocks, blocks), blocks), :] = both

    summary[pl.ds(pl.multiple_of(me * blocks, blocks), blocks), :] = own_summary[...]
    put_noise(me, own_noise[...])
    qkv[pl.ds(pl.multiple_of(me * rows, rows), rows), :] = own[...]
    for step, ref, extra in ((1, step1, extra1), (2, step2, extra2), (3, step3, extra3)):
        owners = (ring_of((place + 8 - step) % 8), ring_of((place + step) % 8))
        for way, owner in enumerate(owners):
            for side, number in ((core, 0), (1 - core, 1)):
                at = pl.multiple_of(owner * rows + side * half, half)
                slot = 2 * way + number
                qkv[pl.ds(at, half), :] = ref[slot * half : (slot + 1) * half, :]
            lines = [extra[(4 * way + k) * EXTRA : (4 * way + k + 1) * EXTRA, :] for k in range(3)]
            put_summary(owner, joined(lines[0], few), joined(lines[2], few))
            put_noise(owner, joined(lines[1], 2))
    owner = ring_of((place + 4) % 8)
    for side, front, back in ((core, f4, b4), (1 - core, xf4, xb4)):
        for k, piece in enumerate((front, back)):
            at = pl.multiple_of(owner * rows + side * half + k * quarter, quarter)
            qkv[pl.ds(at, quarter), :] = dot_nn(piece[:quarter, :], wide(weight)).astype(bf16)
    put_summary(owner, joined(f4[quarter:, :], few), joined(xf4[quarter:, :], few))
    put_noise(owner, joined(b4[quarter:, :], 2))

    parts = three_parts(summary[...])
    logits = sum(dot_nn(part, w_sort[...]) for part in parts[::-1])
    logits = (logits + noise[...]) / TEMPER
    plan = jnp.stack([logits[:, :nb], logits[:, nb:]])
    for sweep in range(SINK):
        for k, axis in enumerate((2, 1)):
            plan = plan - log_total(plan, axis)
            steps[2 * sweep + k] = jnp.exp(plan)
    final = jnp.exp(plan)
    picked = []
    for h in range(2):
        chosen = choices(partner_rows, h)
        picked.append(nb * jnp.sum(chosen * final[h], axis=1, keepdims=True))
    ones = jnp.ones((nb, DH), f32)
    scale_rows[...] = jnp.concatenate([ones, picked[0] * ones, ones, picked[1] * ones], 1)
    weight_rows[...] = jnp.concatenate([picked[0] * ones, picked[1] * ones], 1)

    near = first_lanes()
    work = []
    for i in range(blocks):
        block = me * blocks + i
        query, keys, values = block_operands(
            qkv, block, partner[0, block], partner[1, block], near
        )
        none = jnp.zeros_like(values[0])
        table = jnp.concatenate(
            [
                jnp.concatenate([values[0], none, values[2], none], 0),
                jnp.concatenate([none, values[1], none, values[3]], 0),
            ],
            1,
        )
        z = dot_nt(query, jnp.concatenate(keys, 0)) * (DH**-0.5)
        work.append((block, z, table))
    probs = [block_probs(z * scale_rows[pl.ds(block, 1), :]) for block, z, _ in work]
    outs = [
        dot_nn(jnp.concatenate([p.astype(bf16) for p in prob], 1), table)
        for prob, (_, _, table) in zip(probs, work)
    ]
    for i, (out, (block, _, _)) in enumerate(zip(outs, work)):
        ctx = out[:, : 2 * DH] + weight_rows[pl.ds(block, 1), :] * out[:, 2 * DH :]
        context[i * BLOCK : (i + 1) * BLOCK, :] = ctx.astype(bf16)


def feed_kernel(
    tokens, cotangent, gain, ctx0, ctx1, ctx2, ctx3, wo0, wo1, wo2, wo3, up_a, up_b, down_a, down_b,
    middle, h_two, active, d_hidden, ffn, d_h_two,
    ctx_full, wo_full, up_full, down_full, act_full, d_full,
):
    f32, bf16 = jnp.float32, jnp.bfloat16
    hd = lax.axis_index("head")
    row = hd // 2
    width = ctx0.shape[1]
    ff = up_a.shape[1]
    for j, (c, w) in enumerate(((ctx0, wo0), (ctx1, wo1), (ctx2, wo2), (ctx3, wo3))):
        at = pl.multiple_of((hd ^ j) * width, width)
        ctx_full[:, pl.ds(at, width)] = c[...]
        wo_full[pl.ds(at, width), :] = w[...]
    for j, (u, w) in enumerate(((up_a, down_a), (up_b, down_b))):
        at = pl.multiple_of((row ^ j) * ff, ff)
        up_full[:, pl.ds(at, ff)] = u[...]
        down_full[pl.ds(at, ff), :] = w[...]
    chunk = 256
    for start in range(0, tokens.shape[0], chunk):
        sl = slice(start, start + chunk)
        mid = tokens[sl, :].astype(f32) + dot_nn(ctx_full[sl, :], wo_full[...])
        middle[sl, :] = mid
        normed, _ = norm_parts(mid)
        low = (normed * gain[...].astype(f32)).astype(bf16)
        h_two[sl, :] = low
        ffn_sum = None
        back_sum = None
        for j in range(2):
            cols = slice(j * ff, (j + 1) * ff)
            pre = dot_nn(low, up_full[:, cols])
            d_act = dot_nt(cotangent[sl, :], down_full[cols, :])
            bell = 0.5 * (1.0 + lax.erf(pre * ROOT_HALF))
            act = (pre * bell).astype(bf16)
            slope = bell + pre * jnp.exp(-0.5 * pre * pre) * INV_ROOT_TWO_PI
            d_pre = (d_act * slope).astype(bf16)
            act_full[sl, cols] = act
            d_full[sl, cols] = d_pre
            f = dot_nn(act, down_full[cols, :])
            b = dot_nt(d_pre, up_full[:, cols])
            ffn_sum = f if ffn_sum is None else ffn_sum + f
            back_sum = b if back_sum is None else back_sum + b
        ffn[sl, :] = ffn_sum
        d_h_two[sl, :] = back_sum
    mine = pl.ds(pl.multiple_of(row * ff, ff), ff)
    active[...] = act_full[:, mine]
    d_hidden[...] = d_full[:, mine]


def back_kernel(middle, own, other, cotangent, gain, w_out, d_middle, d_low, d_ctx, g_gain):
    f32, bf16 = jnp.float32, jnp.bfloat16
    normed, inv = norm_parts(middle[...])
    d_h = own[...] + other[...]
    g_gain[...] = jnp.broadcast_to(jnp.sum(d_h * normed, 0, keepdims=True), g_gain.shape)
    d_mid = cotangent[...].astype(f32) + norm_back(d_h, normed, inv, gain[...].astype(f32))
    d_middle[...] = d_mid
    low = d_mid.astype(bf16)
    d_low[...] = low
    d_ctx[...] = dot_nt(low, w_out[...]).astype(bf16)


def grads_kernel(h_two, d_hidden, active, cotangent, *refs):
    keeps, sends, (own, other) = refs[:4], refs[4:8], refs[8:]
    me = lax.axis_index("blk")
    bit, z = me & 1, me >> 1
    up = dot_tn(h_two[...], d_hidden[...])
    down = dot_tn(active[...], cotangent[...])
    own[...] = jnp.where(bit == 0, up, down)
    other[...] = jnp.where(bit == 0, down, up)
    n = keeps[0].shape[0]
    for j in range(4):
        at = pl.ds(pl.multiple_of((z ^ j) * n, n), n)
        keeps[j][...] = own[at, :]
        sends[j][...] = other[at, :].astype(jnp.bfloat16)


def out_grad_kernel(context, d_low, keep, send, total):
    bit = lax.axis_index("blk") & 1
    total[...] = dot_tn(context[...], d_low[...])
    half = keep.shape[0]
    keep[...] = total[pl.ds(pl.multiple_of(bit * half, half), half), :]
    send[...] = total[pl.ds(pl.multiple_of((1 - bit) * half, half), half), :].astype(jnp.bfloat16)


def out_part(j, keep_out, arrived_out, total):
    total[...] = keep_out[...] + arrived_out[...].astype(jnp.float32)
    n = total.shape[0] // 4
    z = lax.axis_index("blk") >> 1
    return total[pl.ds(pl.multiple_of((z ^ j) * n, n), n), :]


def join_kernel(j, keep, arrived, keep_out, arrived_out, out, total):
    n = keep.shape[0]
    out[:n, :] = (keep[...] + arrived[...].astype(jnp.float32)).astype(jnp.bfloat16)
    out[n:, :] = out_part(j, keep_out, arrived_out, total).astype(jnp.bfloat16)


def total_kernel(keep, arrived, keep_out, arrived_out, one, two, three, out, total):
    f32 = jnp.float32
    n = keep.shape[0]
    own = jnp.concatenate(
        [keep[...] + arrived[...].astype(f32), out_part(0, keep_out, arrived_out, total)], 0
    )
    own = (own + one[...].astype(f32)) + (two[...].astype(f32) + three[...].astype(f32))
    out[...] = own.astype(jnp.bfloat16)


def lay_kernel(own, z1, z2, z3, x0, x1, x2, x3, g_up, g_down, g_out):
    f32 = jnp.float32
    me = lax.axis_index("blk")
    z = me >> 1
    n = g_up.shape[0] // 4
    few = g_out.shape[0] // 8
    for j in range(4):
        at = pl.ds(pl.multiple_of((z ^ j) * n, n), n)
        mine, other = ((own, x0), (z1, x1), (z2, x2), (z3, x3))[j]
        first = jnp.where(me & 1 == 0, mine[...].astype(f32), other[...].astype(f32))
        second = jnp.where(me & 1 == 0, other[...].astype(f32), mine[...].astype(f32))
        g_up[at, :] = first[:n]
        g_down[at, :] = second[:n]
        to = pl.multiple_of((z ^ j) * few, few)
        g_out[pl.ds(to, few), :] = first[n:]
        g_out[pl.ds(pl.multiple_of(to + 4 * few, few), few), :] = second[n:]


def halve_kernel(f, b, front, back):
    n = front.shape[0]
    front[...] = f[:n, :]
    back[...] = b[n:, :]


def add_kernel(*refs):
    *terms, out = refs
    total = terms[0][...]
    for term in terms[1:]:
        total = total + term[...]
    out[...] = total


def gains_kernel(here, one, two, three, first, second):
    total = (here[...] + one[...]) + (two[...] + three[...])
    first[...] = total[0, :]
    second[...] = total[8, :]


def pull_kernel(pieces, *refs):
    f32, bf16 = jnp.float32, jnp.bfloat16
    count = len(pieces)
    outs = refs[:count]
    qkv, partner, scale_rows, weight_rows, near_out, low_out, d_weight = refs[count:]
    place = place_of(lax.axis_index("blk"))
    near = first_lanes()
    scale = DH**-0.5
    to = 0
    for (step, start), d_ctx in zip(pieces, outs):
        owner = ring_of((place + 8 - step) % 8)
        for group in range(0, d_ctx.shape[0] // BLOCK, 4):
            work = []
            for i in range(group, group + 4):
                block = owner * (SHARD // BLOCK) + start // BLOCK + i
                query, keys, values = block_operands(
                    qkv, block, partner[0, block], partner[1, block], near
                )
                work.append(
                    dict(
                        query=query,
                        keys=jnp.concatenate(keys, 0),
                        values=jnp.concatenate(values, 0),
                        scale=scale_rows[pl.ds(block, 1), :],
                        weight=weight_rows[pl.ds(block, 1), :],
                        d_out=d_ctx[i * BLOCK : (i + 1) * BLOCK, :],
                    )
                )
            for w in work:
                w["z"] = dot_nt(w["query"], w["keys"]) * scale
            for w in work:
                w["raw"] = dot_nt(w["d_out"], w["values"])
            for w in work:
                w["probs"] = block_probs(w["z"] * w["scale"])
            for w in work:
                d_z, low, d_w = [], [], []
                for h in range(2):
                    sl = slice(h * 2 * DH, (h + 1) * 2 * DH)
                    probs = w["probs"][h]
                    d_probs = w["raw"][:, sl] * w["scale"][:, sl]
                    d_scores = probs * (d_probs - jnp.sum(d_probs * probs, -1, keepdims=True))
                    d_z.append((d_scores * w["scale"][:, sl]).astype(bf16))
                    low.append(probs.astype(bf16))
                    d_w.append(
                        jnp.sum(
                            d_scores * w["z"][:, sl] + low[h].astype(f32) * w["raw"][:, sl],
                            0,
                            keepdims=True,
                        )
                    )
                w["d_z"], w["low"] = jnp.concatenate(d_z, 1), jnp.concatenate(low, 1)
                w["d_w"] = jnp.concatenate(d_w, 1)
            for w in work:
                w["d_query"] = dot_nn(w["d_z"], w["keys"]) * scale
            for w in work:
                w["d_keys"] = dot_tn(w["d_z"], w["query"]) * scale
            for w in work:
                w["d_values"] = dot_tn(w["low"], w["d_out"])
            for w in work:
                at = slice(to * BLOCK, (to + 1) * BLOCK)
                d_weight[to : to + 1, :] = w["d_w"]
                low_out[at, : 2 * DH] = w["d_query"].astype(bf16)
                for k, name in enumerate(("d_keys", "d_values")):
                    parts = [w[name][i * BLOCK : (i + 1) * BLOCK, :] for i in range(4)]
                    near_out[at, k * 2 * DH : (k + 1) * 2 * DH] = jnp.where(near, parts[0], parts[2])
                    far = jnp.where(near, parts[1], parts[3])
                    if k == 1:
                        far = far * w["weight"]
                    low_out[at, (k + 1) * 2 * DH : (k + 2) * 2 * DH] = far.astype(bf16)
                to += 1


def collect_kernel(pieces, *refs):
    f32, bf16 = jnp.float32, jnp.bfloat16
    count = len(pieces)
    nears, lows, d_weights = refs[:count], refs[count : 2 * count], refs[2 * count : 3 * count]
    partner, d_qkv, d_mine, d_weight, acc, far = refs[3 * count :]
    me = lax.axis_index("blk")
    place = place_of(me)
    for parts, near_ref, low_ref, w_ref in zip(pieces, nears, lows, d_weights):
        at = 0
        for step, start, n in parts:
            owner = ring_of((place + 8 - step) % 8)
            to = pl.ds(pl.multiple_of(owner * SHARD + start, n), n)
            acc[to, :] = near_ref[at : at + n, :]
            far[to, :] = low_ref[at : at + n, 2 * DH :]
            d_qkv[to, : 2 * DH] = low_ref[at : at + n, : 2 * DH]
            if start == 0:
                nb = SHARD // BLOCK
                first = pl.multiple_of(owner * nb, nb)
                d_weight[pl.ds(first, nb), :] = w_ref[at // BLOCK : at // BLOCK + nb, :]
            at += n
    near = first_lanes()
    both = jnp.concatenate([near, near], 1)

    def body(block, _):
        tile = far[pl.ds(pl.multiple_of(block * BLOCK, BLOCK), BLOCK), :].astype(f32)
        for h, kept in ((0, jnp.where(both, tile, 0.0)), (1, jnp.where(both, 0.0, tile))):
            to = pl.ds(pl.multiple_of(partner[h, block] * BLOCK, BLOCK), BLOCK)
            acc[to, :] += kept
        return 0

    lax.fori_loop(0, partner.shape[1], body, 0, unroll=4)
    d_qkv[:, 2 * DH :] = acc[...].astype(bf16)
    d_mine[...] = d_qkv[pl.ds(pl.multiple_of(me * SHARD, SHARD), SHARD), :]


def sink_back_kernel(d_weight, steps, partner, summary, d_mine, g_sort, d_flat):
    nb = partner.shape[1]
    grads = []
    for h in range(2):
        total = jnp.sum(
            d_weight[:, (2 * h + 1) * DH : (2 * h + 2) * DH], axis=1, keepdims=True
        )
        grads.append(choices(partner, h) * (nb * total))
    last = steps.shape[0] - 1
    grad = jnp.stack(grads) * steps[last]
    for t in range(last, -1, -1):
        grad = grad - steps[t] * jnp.sum(grad, axis=1 if t % 2 else 2, keepdims=True)
    flat = jnp.concatenate([grad[0], grad[1]], 1) / TEMPER
    d_flat[...] = flat
    n = d_mine.shape[0]
    d_mine[...] = d_flat[pl.ds(pl.multiple_of(lax.axis_index("blk") * n, n), n), :]
    g_sort[...] = lax.dot_general(
        summary[...],
        flat,
        (((0,), (0,)), ((), ())),
        precision=HIGHEST,
        preferred_element_type=jnp.float32,
    )


def weight_kernel(*refs):
    own, f1, b1, f2, b2, f3, b3, f4, b4, xf1, xb1, xf2, xb2, xf3, xb3, xf4, xb4 = refs[:17]
    d_qkv, g_qkv, h_all = refs[17:]
    me = lax.axis_index("blk")
    core = lax.axis_index("head") % 2
    place = place_of(me)
    rows = own.shape[0]
    half, quarter = rows // 2, rows // 4

    def put(owner, start, ref):
        for at in range(0, ref.shape[0], quarter + EXTRA):
            to = pl.multiple_of(owner * rows + start + (quarter if at else 0), quarter)
            h_all[pl.ds(to, quarter), :] = ref[at : at + quarter, :]

    h_all[pl.ds(pl.multiple_of(me * rows, rows), rows), :] = own[...]
    for step, (f, b, xf, xb) in enumerate(
        ((f1, b1, xf1, xb1), (f2, b2, xf2, xb2), (f3, b3, xf3, xb3)), 1
    ):
        for owner, a, o in (
            (ring_of((place + 8 - step) % 8), f, xf),
            (ring_of((place + step) % 8), b, xb),
        ):
            put(owner, core * half, a)
            put(owner, (1 - core) * half, o)
    far = ring_of((place + 4) % 8)
    put(far, core * half, f4)
    put(far, (1 - core) * half, xf4)
    put(far, core * half + quarter, b4)
    put(far, (1 - core) * half + quarter, xb4)
    out = dot_tn(h_all[...], d_qkv[...])
    width = g_qkv.shape[2]
    for i in range(3):
        g_qkv[i] = out[:, i * width : (i + 1) * width]


def input_kernel(dq_a, dq_b, w_a, w_b, flat_a, flat_b, sort_a, sort_b, d_h, dq_full, w_full, flat_full, sort_full):
    row = lax.axis_index("head") // 2
    width = dq_a.shape[1]
    for j, (g, w) in enumerate(((dq_a, w_a), (dq_b, w_b))):
        at = pl.multiple_of((row ^ j) * width, width)
        dq_full[:, pl.ds(at, width)] = g[...]
        w_full[:, pl.ds(at, width)] = wide(w)
    part = dot_nt(dq_full[...], w_full[...])
    nb = flat_a.shape[1]
    for j, (flat, sort) in enumerate(((flat_a, sort_a), (flat_b, sort_b))):
        at = pl.multiple_of((row ^ j) * nb, nb)
        flat_full[:, pl.ds(at, nb)] = flat[...]
        sort_full[:, pl.ds(at, nb)] = sort[...]
    d_sum = sum(dot_nt(p, sort_full[...]) for p in three_parts(flat_full[...])[::-1]) / BLOCK
    blocks = d_sum.shape[0]
    for i in range(blocks):
        sl = slice(i * BLOCK, (i + 1) * BLOCK)
        d_h[sl, :] = part[sl, :] + d_sum[i : i + 1, :]


def end_kernel(tokens, gain, own, other, d_middle, g_two, d_tokens, g_gain):
    f32 = jnp.float32
    normed, inv = norm_parts(tokens[...].astype(f32))
    d_h = own[...] + other[...]
    g_gain[:8, :] = jnp.broadcast_to(jnp.sum(d_h * normed, 0, keepdims=True), g_two.shape)
    g_gain[8:, :] = g_two[...]
    d_tokens[...] = d_middle[...] + norm_back(d_h, normed, inv, gain[...].astype(f32))


VMEM_SPEC = pl.BlockSpec(memory_space=pltpu.VMEM)
SMEM_SPEC = pl.BlockSpec(memory_space=pltpu.SMEM)


def call(kernel, outs, *args, scratch=(), smem=(), limit=16, name=None):
    shapes = [jax.ShapeDtypeStruct(s, d) for s, d in outs]
    result = pl.pallas_call(
        kernel,
        out_shape=shapes,
        in_specs=[SMEM_SPEC if i in smem else VMEM_SPEC for i in range(len(args))],
        out_specs=[VMEM_SPEC] * len(shapes),
        scratch_shapes=[pltpu.VMEM(s, d) for s, d in scratch],
        compiler_params=pltpu.CompilerParams(vmem_limit_bytes=limit * 1024 * 1024),
        name=name,
    )(*args)
    return result[0] if len(shapes) == 1 else result


def tie(*values):
    return lax.optimization_barrier(values)


def after(value, *others):
    return lax.optimization_barrier((value,) + others)[0]


RING = (0, 2, 4, 6, 7, 5, 3, 1)
SHARD = 512
EXTRA = 16


def local_eight(
    tokens, gain_attn, gain_ffn, w_qkv, w_out, w_sort, w_up, w_down, gumbel_noise, partner, cotangent
):
    f32, bf16 = jnp.float32, jnp.bfloat16
    rows = tokens.shape[0]
    blocks = rows // BLOCK
    width = w_out.shape[0]
    ff = w_up.shape[1]
    nb = partner.shape[0]
    total = nb * BLOCK
    half, quarter = rows // 2, rows // 4
    core = lax.axis_index("head") % 2

    def ahead(v):
        return lax.ppermute(v, "blk", [(RING[i], RING[(i + 1) % 8]) for i in range(8)])

    def behind(v):
        return lax.ppermute(v, "blk", [(RING[i], RING[(i - 1) % 8]) for i in range(8)])

    def swap_head(v, j):
        return lax.ppermute(v, "head", [(i, i ^ j) for i in range(4)])

    def swap_blk(v, j):
        return lax.ppermute(v, "blk", [(i, i ^ j) for i in range(8)])

    w_in = w_qkv.transpose(1, 0, 2)
    partner_s = partner.T

    h_one, packed, own_summary, noise = call(
        head_kernel,
        [((rows, D), bf16), ((half + 2 * EXTRA, D), bf16), ((blocks, D), f32), ((2, D), f32)],
        tokens, gain_attn, gumbel_noise, name="norm_one",
    )

    def project(pieces):
        return call(
            project_kernel, [((2 * rows, 3 * width), bf16), ((8 * EXTRA, D), bf16)],
            *pieces, w_in, name="project",
        )

    f, b = ahead(packed), behind(packed)
    up_y = swap_head(after(w_up, packed), 2)
    qkv_own = call(project_own_kernel, [((rows, 3 * width), bf16)], h_one, w_in, name="project_own")
    f1, b1, _ = tie(f, b, qkv_own)
    f, b = ahead(f1), behind(b1)
    wo_y = swap_head(after(w_out, f1, b1), 2)
    f2, b2, _ = tie(f, b, up_y)
    f, b = ahead(f2), behind(b2)
    down_y = swap_head(after(w_down, f2, b2), 2)
    f3, b3, _ = tie(f, b, wo_y)
    f, b = call(
        halve_kernel, [((quarter + EXTRA, D), bf16)] * 2, f3, b3, name="halve"
    )
    f4, b4 = ahead(f), behind(b)
    cross = [swap_head(after(v, f), 1) for v in (f1, b1, f2, b2, f3, b3)]
    wo_c = swap_head(after(w_out, f), 1)
    wo_yc = swap_head(after(wo_y, f), 1)
    xf1, xb1, xf2, xb2, xf3, xb3 = cross
    projected = [
        project((f1, xf1, b1, xb1)), project((f2, xf2, b2, xb2)), project((f3, xf3, b3, xb3)),
    ]
    f4, b4 = tie(f4, b4, wo_c, wo_yc, *[p[0] for p in projected])[:2]
    xf4, xb4 = swap_head(f4, 1), swap_head(b4, 1)
    qkv, context, summary, steps, scale_rows, weight_rows = call(
        attend_kernel,
        [
            ((total, 3 * width), bf16),
            ((rows, width), bf16),
            ((nb, D), f32),
            ((2 * SINK, 2, nb, nb), f32),
            ((nb, 4 * DH), f32),
            ((nb, 2 * DH), f32),
        ],
        qkv_own, *[p[0] for p in projected], *[p[1] for p in projected],
        f4, b4, xf4, xb4, w_in, w_sort, own_summary, noise, partner_s, partner_s,
        smem=(15,), scratch=[((nb, 2 * nb), f32)], name="attend",
    )
    ctx_y, ctx_c = swap_head(context, 2), swap_head(context, 1)
    ctx_yc = swap_head(ctx_y, 1)
    middle, h_two, active, d_hidden, ffn, d_h_two = call(
        feed_kernel,
        [
            ((rows, D), f32),
            ((rows, D), bf16),
            ((rows, ff), bf16),
            ((rows, ff), bf16),
            ((rows, D), f32),
            ((rows, D), f32),
        ],
        tokens, cotangent, gain_ffn, context, ctx_c, ctx_y, ctx_yc, w_out, wo_c, wo_y, wo_yc,
        w_up, up_y, w_down, down_y,
        scratch=[
            ((rows, 4 * width), bf16), ((4 * width, D), bf16), ((D, 2 * ff), bf16), ((2 * ff, D), bf16),
            ((rows, 2 * ff), bf16), ((rows, 2 * ff), bf16),
        ],
        name="feed",
    )
    d_h_two_other = swap_head(d_h_two, 1)
    piece, few = D // 4, width // 8
    parts = call(
        grads_kernel,
        [((piece, D), f32)] * 4 + [((piece, D), bf16)] * 4,
        h_two, d_hidden, active, cotangent, scratch=[((D, D), f32), ((D, D), f32)], name="grads",
    )
    keeps, sends = parts[:4], parts[4:]
    d_h_two_other, _ = tie(d_h_two_other, keeps[0])
    d_middle, d_low, d_ctx, g_two = call(
        back_kernel,
        [((rows, D), f32), ((rows, D), bf16), ((rows, width), bf16), ((8, D), f32)],
        middle, d_h_two, d_h_two_other, cotangent, gain_ffn, w_out, name="back",
    )

    plans = [[(0, 0)]] + [[(k, 0), (-k, 0)] for k in (1, 2, 3)] + [[(4, 0), (4, half)]]
    pulled = []

    def pull(given):
        plan = plans[len(pulled)]
        n = sum(a.shape[0] for a in given)
        pulled.append(
            call(
                functools.partial(pull_kernel, tuple(plan)),
                [((n, 4 * DH), f32), ((n, 6 * DH), bf16), ((n // BLOCK, 4 * DH), f32)],
                *given, qkv, partner_s, scale_rows, weight_rows, smem=(len(given) + 1,), name="pull",
            )
        )
        return pulled[-1][0]

    f, b = ahead(d_ctx), behind(d_ctx)
    keep_out, send_out = call(
        out_grad_kernel, [((width // 2, D), f32), ((width // 2, D), bf16)], context, d_low,
        scratch=[((width, D), f32)], name="out_grad",
    )
    arrived_out = swap_blk(send_out, 1)
    arrived = [None] * 4
    sent = []
    order = (1, 2, 3, 0)
    given = [d_ctx]
    arrays = [given]
    ready = (d_ctx,)
    for step in range(4):
        j = order[step]
        arrived[j] = swap_blk(after(sends[j], *ready), 1)
        extra = []
        if step:
            j = order[step - 1]
            summed = call(
                functools.partial(join_kernel, j), [((piece + few, D), bf16)],
                keeps[j], arrived[j], keep_out, arrived_out, scratch=[((4 * few, D), f32)], name="join",
            )
            sent.append(swap_blk(summed, 2 * j))
            extra.append(summed)
        done = pull(given)
        if step == 0:
            in_y = swap_head(after(w_in, d_ctx), 2)
        if step == 1:
            sort_y = swap_head(after(w_sort, f), 2)
            ffn_other = swap_head(after(ffn, f), 1)
            extra.append(in_y)
        if step < 3:
            extra.append(arrived[order[step]])
        if step == 0:
            extra.append(arrived_out)
        f, b = tie(f, b, done, *extra)[:2]
        given = [f, b]
        arrays.append(given)
        ready = (f, b)
        if step < 2:
            f, b = ahead(f), behind(b)
        elif step == 2:
            f, b = call(halve_kernel, [((half, width), bf16)] * 2, f, b, name="halve")
            f, b = ahead(f), behind(b)
    pull(given)
    spans = tuple(
        tuple((step, start, a.shape[0]) for (step, start), a in zip(plan, given))
        for plan, given in zip(plans, arrays)
    )
    d_qkv, d_mine, d_weight = call(
        functools.partial(collect_kernel, spans),
        [((total, 3 * width), bf16), ((rows, 3 * width), bf16), ((nb, 4 * DH), f32)],
        *[p[k] for k in range(3) for p in pulled], partner_s, smem=(15,),
        scratch=[((total, 4 * DH), f32), ((total, 4 * DH), bf16)], name="collect",
    )
    d_mine_y = swap_head(d_mine, 2)
    owned = call(
        total_kernel, [((piece + few, D), bf16)],
        keeps[0], arrived[0], keep_out, arrived_out, *sent, scratch=[((4 * few, D), f32)], name="total",
    )
    own_x, z1, z2, z3 = swap_blk(owned, 1), swap_blk(owned, 2), swap_blk(owned, 4), swap_blk(owned, 6)
    flat_mine, g_sort = call(
        sink_back_kernel,
        [((blocks, 2 * nb), f32), ((D, 2 * nb), f32)],
        after(d_weight, owned), steps, partner_s, summary, scratch=[((nb, 2 * nb), f32)],
        name="sinkhorn_back",
    )
    flat_y = swap_head(flat_mine, 2)
    d_h = call(
        input_kernel, [((rows, D), f32)],
        d_mine, d_mine_y, w_in, in_y, flat_mine, flat_y, w_sort, sort_y,
        scratch=[
            ((rows, 6 * width), bf16), ((D, 6 * width), bf16), ((blocks, 4 * nb), f32), ((D, 4 * nb), bf16),
        ],
        name="input_back",
    )
    d_h_other = swap_head(d_h, 1)
    g_qkv = call(
        weight_kernel, [((3, D, width), f32)],
        h_one, f1, b1, f2, b2, f3, b3, f4, b4, xf1, xb1, xf2, xb2, xf3, xb3, xf4, xb4,
        after(d_qkv, flat_mine), scratch=[((total, D), bf16)], limit=24, name="weights",
    )
    d_h_other, g_qkv, z1 = tie(d_h_other, g_qkv, z1)
    d_tokens, gains = call(
        end_kernel, [((rows, D), f32), ((16, D), f32)],
        tokens, gain_attn, d_h, d_h_other, d_middle, g_two, name="norm_one_back",
    )
    gains = call(add_kernel, [((16, D), f32)], gains, swap_blk(gains, 1), name="add_gains")
    gains1, gains2, gains3 = swap_blk(gains, 2), swap_blk(gains, 4), swap_blk(gains, 6)
    x1, x2, x3 = swap_blk(z1, 1), swap_blk(z2, 1), swap_blk(z3, 1)
    output = call(add_kernel, [((rows, D), f32)], after(ffn, d_h_other), ffn_other, middle, name="output")
    g_up, g_down, g_out = call(
        lay_kernel,
        [((D, ff), f32), ((ff, D), f32), ((width, D), f32)],
        owned, z1, z2, z3, own_x, x1, x2, x3, name="lay",
    )
    g_one, g_two = call(
        gains_kernel, [((D,), f32), ((D,), f32)], gains, gains1, gains2, gains3, name="gains"
    )
    return output, d_tokens, g_one, g_two, g_qkv.transpose(1, 0, 2), g_out, g_sort, g_up, g_down


def solution(mesh):
    in_specs = (
        P("blk", None),
        P(),
        P(),
        P(None, None, "head"),
        P("head", None),
        P(None, "head"),
        P(None, "head"),
        P("head", None),
        P("blk", "head", None),
        P(None, "head"),
        P("blk", None),
    )
    out_specs = (
        P("blk", None),
        P("blk", None),
        P(),
        P(),
        P(None, None, "head"),
        P("head", None),
        P(None, "head"),
        P(None, "head"),
        P("head", None),
    )
    plan = local_eight if mesh.shape["blk"] == 8 and mesh.shape["head"] == 4 else local
    return jax.shard_map(plan, mesh=mesh, in_specs=in_specs, out_specs=out_specs, check_vma=False)
```

```python
import functools
import math

import jax
import jax.numpy as jnp
from jax import lax
from jax.experimental import pallas as pl
from jax.experimental.pallas import tpu as pltpu
from jax.sharding import PartitionSpec as P

D = 512
DH = 64
BLOCK = 64
SINK = 8


EPS = 1e-05
TEMPER = 0.75
ROOT_HALF = 0.7071067811865476
INV_ROOT_TWO_PI = 0.3989422804014327
HIGHEST = lax.Precision.HIGHEST


def normalize(values, norm_gain):
    average = jnp.mean(values, -1, keepdims=True)
    centred = values - average
    inv_std = lax.rsqrt(jnp.mean(centred * centred, -1, keepdims=True) + EPS)
    normed = centred * inv_std
    return (normed * norm_gain, normed, inv_std)


def norm_back(d_out, normed, inv_std, norm_gain):
    d_normed = d_out * norm_gain
    return inv_std * (
        d_normed
        - jnp.mean(d_normed, -1, keepdims=True)
        - normed * jnp.mean(d_normed * normed, -1, keepdims=True)
    )


def log_total(values, axis):
    highest = jnp.max(values, axis=axis, keepdims=True)
    return highest + jnp.log(jnp.sum(jnp.exp(values - highest), axis=axis, keepdims=True))


def balancing_log_space(sort_logits):
    for sweep in range(SINK):
        sort_logits = sort_logits - log_total(sort_logits, 2)
        sort_logits = sort_logits - log_total(sort_logits, 1)
    return sort_logits


def gelu_value(values):
    return 0.5 * values * (1.0 + lax.erf(values * ROOT_HALF))


def gelu_slope(values):
    return (
        0.5 * (1.0 + lax.erf(values * ROOT_HALF))
        + values * jnp.exp(-0.5 * values * values) * INV_ROOT_TWO_PI
    )


def local(
    tokens,
    gain_attn,
    gain_ffn,
    w_qkv,
    w_out,
    w_sort,
    w_up,
    w_down,
    gumbel_noise,
    partner,
    cotangent,
):
    f32 = jnp.float32
    bf16 = jnp.bfloat16
    tok_rows = tokens.shape[0]
    blocks_dev = tok_rows // BLOCK
    heads_dev = w_out.shape[0] // DH
    width_dev = heads_dev * DH
    requests = blocks_dev * heads_dev
    dev_count = lax.axis_size("blk")
    my_index = lax.axis_index("blk")
    first_block = my_index * blocks_dev
    seq_blocks = partner.shape[0]
    scale = DH ** (-0.5)
    gain_one = gain_attn.astype(f32)
    gain_two = gain_ffn.astype(f32)
    inputs = tokens.astype(f32)
    h_one, normed_one, inv_one = normalize(inputs, gain_one)
    h_one_low = h_one.astype(bf16)
    qkv = jnp.einsum("td,dcf->tcf", h_one_low, w_qkv, preferred_element_type=f32).astype(bf16)
    summary = jnp.mean(h_one.reshape(blocks_dev, BLOCK, D), axis=1)
    sort_mat = w_sort.astype(f32)
    own_rows = (
        jnp.dot(summary, sort_mat, precision=HIGHEST).reshape(blocks_dev, heads_dev, seq_blocks)
        + gumbel_noise
    ) / TEMPER
    every_rows = lax.all_gather(own_rows, "blk", axis=0, tiled=True)
    my_partner = lax.dynamic_slice_in_dim(partner, first_block, blocks_dev, 0)

    def own_weights(sequence_rows):
        balanced_plan = balancing_log_space(sequence_rows.transpose(1, 0, 2))
        mine = lax.dynamic_slice_in_dim(jnp.exp(balanced_plan), first_block, blocks_dev, 1)
        return seq_blocks * jnp.take_along_axis(mine, my_partner.T[:, :, None], axis=2)[:, :, 0]

    weight_hb, sink_pull = jax.vjp(own_weights, every_rows)
    weight_matrix = weight_hb.T
    owner_all = (partner // blocks_dev).reshape(dev_count, requests)
    slot_all = (
        partner % blocks_dev * heads_dev + jnp.arange(heads_dev, dtype=jnp.int32)[None, :]
    ).reshape(dev_count, requests)
    owner_mine = lax.dynamic_index_in_dim(owner_all, my_index, 0, keepdims=False)
    tile_ids = jnp.arange(requests, dtype=jnp.int32)
    key_value = (
        qkv[:, 1:3]
        .reshape(blocks_dev, BLOCK, 2, heads_dev, DH)
        .transpose(0, 3, 1, 2, 4)
        .reshape(requests, BLOCK, 2 * DH)
    )
    empty_tile = jnp.zeros((), bf16)
    wanted = owner_all == my_index
    outgoing = jnp.where(
        wanted[:, :, None, None], jnp.take(key_value, slot_all, axis=0), empty_tile
    )
    incoming = lax.all_to_all(outgoing, "blk", split_axis=0, concat_axis=0, tiled=True)
    partner_tiles = jnp.sum(incoming, axis=0, dtype=f32).astype(bf16)
    far_tiles = partner_tiles.reshape(blocks_dev, heads_dev, BLOCK, 2, DH)
    key_far = far_tiles[:, :, :, 0]
    value_far = far_tiles[:, :, :, 1]
    query_b = qkv[:, 0].reshape(blocks_dev, BLOCK, heads_dev, DH)
    key_b = qkv[:, 1].reshape(blocks_dev, BLOCK, heads_dev, DH)
    value_b = qkv[:, 2].reshape(blocks_dev, BLOCK, heads_dev, DH)
    weight_s = weight_matrix[:, :, None, None]

    def score_parts():
        near_z = scale * jnp.einsum("bqhd,bkhd->bhqk", query_b, key_b, preferred_element_type=f32)
        far_z = scale * jnp.einsum("bqhd,bhkd->bhqk", query_b, key_far, preferred_element_type=f32)
        return (near_z, far_z, jnp.concatenate([near_z, weight_s * far_z], -1))

    near_z, far_z, scores = score_parts()
    highest = jnp.max(scores, -1, keepdims=True)
    expo = jnp.exp(scores - highest)
    row_total = jnp.sum(expo, -1, keepdims=True)
    log_sum = highest + jnp.log(row_total)
    probs_low = (expo / row_total).astype(bf16)
    near_ctx = jnp.einsum(
        "bhqk,bkhd->bqhd", probs_low[..., :BLOCK], value_b, preferred_element_type=f32
    )
    far_ctx = jnp.einsum(
        "bhqk,bhkd->bqhd", probs_low[..., BLOCK:], value_far, preferred_element_type=f32
    )
    context = near_ctx + weight_matrix[:, None, :, None] * far_ctx
    context_low = context.reshape(tok_rows, width_dev).astype(bf16)
    attn = lax.psum(jnp.dot(context_low, w_out, preferred_element_type=f32), "head")
    middle = inputs + attn
    h_two, normed_two, inv_two = normalize(middle, gain_two)
    h_two_low = h_two.astype(bf16)
    hidden_pre = jnp.dot(h_two_low, w_up, preferred_element_type=f32)
    active_low = gelu_value(hidden_pre).astype(bf16)
    ffn = lax.psum(
        jnp.dot(active_low, w_down, preferred_element_type=f32).astype(jnp.bfloat16), "head"
    ).astype(jnp.float32)
    output = middle + ffn
    g_down = jnp.einsum("tf,td->fd", active_low, cotangent, preferred_element_type=f32)
    d_active = jnp.einsum("td,fd->tf", cotangent, w_down, preferred_element_type=f32)
    d_hidden = (d_active * gelu_slope(hidden_pre)).astype(bf16)
    g_up = jnp.einsum("td,tf->df", h_two_low, d_hidden, preferred_element_type=f32)
    d_h_two = lax.psum(jnp.einsum("tf,df->td", d_hidden, w_up, preferred_element_type=f32), "head")
    g_gain_two = jnp.sum(d_h_two * normed_two, 0)
    d_middle = cotangent.astype(f32) + norm_back(d_h_two, normed_two, inv_two, gain_two)
    d_attn_low = d_middle.astype(bf16)
    g_out = jnp.einsum("tf,td->fd", context_low, d_attn_low, preferred_element_type=f32)
    d_context = jnp.einsum("td,fd->tf", d_attn_low, w_out, preferred_element_type=f32).astype(bf16)
    d_context = d_context.reshape(blocks_dev, BLOCK, heads_dev, DH)
    near_z, far_z, scores = score_parts()
    probs = jnp.exp(scores - log_sum)
    probs_low = probs.astype(bf16)
    far_ctx = jnp.einsum(
        "bhqk,bhkd->bqhd", probs_low[..., BLOCK:], value_far, preferred_element_type=f32
    )
    d_probs_near = jnp.einsum("bqhd,bkhd->bhqk", d_context, value_b, preferred_element_type=f32)
    d_probs_far = weight_s * jnp.einsum(
        "bqhd,bhkd->bhqk", d_context, value_far, preferred_element_type=f32
    )
    d_probs = jnp.concatenate([d_probs_near, d_probs_far], -1)
    d_scores = probs * (d_probs - jnp.sum(d_probs * probs, -1, keepdims=True))
    d_near = d_scores[..., :BLOCK].astype(bf16)
    d_far_raw = d_scores[..., BLOCK:]
    d_far = (weight_s * d_far_raw).astype(bf16)
    d_weight = jnp.sum(d_far_raw * far_z, (2, 3)) + jnp.sum(d_context.astype(f32) * far_ctx, (1, 3))
    d_query = scale * (
        jnp.einsum("bhqk,bkhd->bqhd", d_near, key_b, preferred_element_type=f32)
        + jnp.einsum("bhqk,bhkd->bqhd", d_far, key_far, preferred_element_type=f32)
    )
    d_key = scale * jnp.einsum("bhqk,bqhd->bkhd", d_near, query_b, preferred_element_type=f32)
    d_value = jnp.einsum(
        "bhqk,bqhd->bkhd", probs_low[..., :BLOCK], d_context, preferred_element_type=f32
    )
    d_key_far = scale * jnp.einsum("bhqk,bqhd->bhkd", d_far, query_b, preferred_element_type=f32)
    d_value_far = weight_s * jnp.einsum(
        "bhqk,bqhd->bhkd", probs_low[..., BLOCK:], d_context, preferred_element_type=f32
    )
    grad_tiles = jnp.stack([d_key_far.astype(bf16), d_value_far.astype(bf16)], 3).reshape(
        requests, BLOCK * 2 * DH
    )
    peers = jnp.arange(dev_count, dtype=jnp.int32)
    outgoing_grads = jnp.where(
        (owner_mine[None, :] == peers[:, None])[:, :, None], grad_tiles[None], empty_tile
    )
    returned = lax.all_to_all(outgoing_grads, "blk", split_axis=0, concat_axis=0, tiled=True)
    selector = (owner_all == my_index)[:, :, None] & (
        slot_all[:, :, None] == tile_ids[None, None, :]
    )
    selector = selector.reshape(dev_count * requests, requests).astype(bf16)
    remote = jnp.einsum(
        "st,sf->tf",
        selector,
        returned.reshape(dev_count * requests, BLOCK * 2 * DH),
        preferred_element_type=f32,
    )
    remote = (
        remote.reshape(blocks_dev, heads_dev, BLOCK, 2, DH)
        .transpose(0, 2, 3, 1, 4)
        .reshape(tok_rows, 2, width_dev)
    )
    near_kv = (
        jnp.stack([d_key.reshape(tok_rows, width_dev), d_value.reshape(tok_rows, width_dev)], 1)
        + remote
    )
    d_qkv = jnp.concatenate([d_query.reshape(tok_rows, 1, width_dev), near_kv], 1).astype(bf16)
    g_qkv = jnp.einsum("td,tcf->dcf", h_one_low, d_qkv, preferred_element_type=f32)
    d_h_part = jnp.einsum("tcf,dcf->td", d_qkv, w_qkv, preferred_element_type=f32)
    (d_every,) = sink_pull(d_weight.T)
    d_own = lax.psum_scatter(d_every, "blk", scatter_dimension=0, tiled=True) / TEMPER
    d_flat = d_own.reshape(blocks_dev, heads_dev * seq_blocks)
    g_sort = jnp.dot(summary.T, d_flat, precision=HIGHEST)
    d_summary = jnp.dot(d_flat, sort_mat.T, precision=HIGHEST)
    d_h_part = (d_h_part.reshape(blocks_dev, BLOCK, D) + d_summary[:, None, :] / BLOCK).reshape(
        tok_rows, D
    )
    d_h_one = lax.psum(d_h_part, "head")
    g_gain_one = jnp.sum(d_h_one * normed_one, 0)
    d_tokens = d_middle + norm_back(d_h_one, normed_one, inv_one, gain_one)
    summed = lax.psum((g_gain_one, g_gain_two, g_qkv, g_out, g_sort, g_up, g_down), "blk")
    return (
        output,
        d_tokens,
        summed[0],
        summed[1],
        summed[2],
        summed[3],
        summed[4],
        summed[5],
        summed[6],
    )


def mask_pair(values, near):
    zero = jnp.zeros_like(values)
    return jnp.where(near, values, zero), jnp.where(near, zero, values)


def first_lanes():
    return lax.broadcasted_iota(jnp.int32, (1, 2 * DH), 1) < DH


def dot_nn(a, b):
    return lax.dot_general(a, b, (((1,), (0,)), ((), ())), preferred_element_type=jnp.float32)


def dot_nt(a, b):
    return lax.dot_general(a, b, (((1,), (1,)), ((), ())), preferred_element_type=jnp.float32)


def dot_tn(a, b):
    return lax.dot_general(a, b, (((0,), (0,)), ((), ())), preferred_element_type=jnp.float32)


def three_parts(values):
    high = values.astype(jnp.bfloat16)
    rest = values - high.astype(jnp.float32)
    mid = rest.astype(jnp.bfloat16)
    low = (rest - mid.astype(jnp.float32)).astype(jnp.bfloat16)
    return high, mid, low


def norm_parts(values):
    centred = values - jnp.mean(values, -1, keepdims=True)
    inv_std = lax.rsqrt(jnp.mean(centred * centred, -1, keepdims=True) + EPS)
    return centred * inv_std, inv_std


def noise_rows(noise):
    few = noise.shape[0] // 2
    return [
        jnp.concatenate([noise[r * few + i, h : h + 1, :] for i in range(few) for h in range(2)], 1)
        for r in range(2)
    ]


def head_kernel(tokens, gain, noise, other_noise, up, shard, summary, own_noise, up_a):
    f32, bf16 = jnp.float32, jnp.bfloat16
    rows = tokens.shape[0]
    half = rows // 2
    core = lax.axis_index("head") % 2
    normed, _ = norm_parts(tokens[...].astype(f32))
    h = normed * gain[...].astype(f32)
    low = h.astype(bf16)
    means = jnp.mean(h.reshape(rows // BLOCK, BLOCK, D), axis=1)
    summary[...] = means
    up_a[...] = up[: up_a.shape[0], :]
    mine = jnp.concatenate(noise_rows(noise), 0)
    other = jnp.concatenate(noise_rows(other_noise), 0)
    own_noise[...] = mine
    both = jnp.where(
        core == 0, jnp.concatenate([mine, other], 0), jnp.concatenate([other, mine], 0)
    )
    few = means.shape[0] // 2
    for k in range(2):
        at = k * (half + EXTRA)
        shard[at : at + half, :] = low[k * half : (k + 1) * half, :]
        parts = [p.astype(f32) for p in three_parts(means[k * few : (k + 1) * few, :])]
        parts += [p.astype(f32) for p in three_parts(both)] if k else [jnp.zeros((12, D), f32)]
        parts.append(jnp.zeros((EXTRA - 24, D), f32))
        shard[at + half : at + half + EXTRA, :] = jnp.concatenate(parts, 0).astype(bf16)


def project_rows(rows, joint):
    return dot_nn(rows, joint[:, : 6 * DH]).astype(jnp.bfloat16)


def project_own_kernel(h_one, weight, w_sort, w_out, up, down, out, joint, first, second, third):
    joint[...] = jnp.concatenate([weight[i] for i in range(3)] + [w_sort[...]], 1)
    width = w_out.shape[0]
    rest = first.shape[0] - width
    first[:rest, :] = up[up.shape[0] - rest :, :]
    first[rest:, :] = w_out[...]
    n = second.shape[0]
    second[...] = down[:n, :]
    third[...] = down[n:, :]
    project_shard(h_one, joint, out, 0)


def project_shard(shard, joint, out, to):
    half = shard.shape[0] // 2 - EXTRA
    for k in range(2):
        for start in range(0, half, 2 * BLOCK):
            at = k * (half + EXTRA) + start
            out[to : to + 2 * BLOCK, :] = project_rows(shard[at : at + 2 * BLOCK, :], joint)
            to += 2 * BLOCK


def project_kernel(mine, other, joint, out, extra):
    size = mine.shape[0] // 2
    for k, piece in enumerate((mine, other)):
        project_shard(piece, joint, out, k * 2 * (size - EXTRA))
        for m in range(2):
            to = (2 * k + m) * EXTRA
            extra[to : to + EXTRA, :] = piece[(m + 1) * size - EXTRA : (m + 1) * size, :]


def half_kernel(shard, w_out, first, half, pair):
    n, width = half.shape[0], w_out.shape[0]
    core = lax.axis_index("head") % 2
    half[...] = shard[pl.ds(pl.multiple_of(core * n, n), n), :]
    pair[:width, :] = w_out[...]
    pair[width:, :] = first[first.shape[0] - width :, :]


def owners_of(step):
    place = place_of(lax.axis_index("blk"))
    core = lax.axis_index("head") % 2
    way = jnp.where(core == 0, 8 - step, step)
    return ring_of((place + way) % 8), ring_of((place + 8 - way) % 8)


def ring_of(position):
    return jnp.where(position < 4, 2 * position, 2 * (7 - position) + 1)


def place_of(index):
    return jnp.where(index % 2 == 0, index // 2, 7 - index // 2)


def far_near(table, at, lanes):
    return table[pl.ds(pl.multiple_of(at * BLOCK, BLOCK), BLOCK), lanes]


def block_operands(qkv, block, first, second, near):
    k_lanes, v_lanes = slice(2 * DH, 4 * DH), slice(4 * DH, 6 * DH)
    query = far_near(qkv, block, slice(0, 2 * DH))
    keys, values = [], []
    for lanes, store in ((k_lanes, keys), (v_lanes, values)):
        own0, own1 = mask_pair(far_near(qkv, block, lanes), near)
        far0, _ = mask_pair(far_near(qkv, first, lanes), near)
        _, far1 = mask_pair(far_near(qkv, second, lanes), near)
        store.extend([own0, far0, own1, far1])
    return query, keys, values


def block_probs(scores):
    probs = []
    for h in range(2):
        part = scores[:, h * 2 * DH : (h + 1) * 2 * DH]
        expo = jnp.exp(part - jnp.max(part, -1, keepdims=True))
        probs.append(expo / jnp.sum(expo, -1, keepdims=True))
    return probs


def choices(partner, h):
    nb = partner.shape[1]
    sides = lax.broadcasted_iota(jnp.int32, (nb, nb), 0)
    hot = (sides == partner[h : h + 1, :]).astype(jnp.bfloat16)
    same = sides == lax.broadcasted_iota(jnp.int32, (nb, nb), 1)
    return dot_nt(same.astype(jnp.bfloat16), hot)


def joined(rows, at, count):
    parts = [rows[at + k * count : at + (k + 1) * count, :].astype(jnp.float32) for k in range(3)]
    return (parts[0] + parts[1]) + parts[2]


def attend_kernel(
    own, step1, step2, step3, extra1, extra2, extra3, mine4, other4, joint, own_summary, own_noise,
    partner, partner_rows, qkv, context, summary, steps, scale_rows, weight_rows, noise,
):
    f32, bf16 = jnp.float32, jnp.bfloat16
    me = lax.axis_index("blk")
    core = lax.axis_index("head") % 2
    nb = partner_rows.shape[1]
    rows = own.shape[0]
    half = rows // 2
    blocks = rows // BLOCK
    few = blocks // 2

    def put(owner, start, values):
        n = values.shape[0]
        qkv[pl.ds(pl.multiple_of(owner * rows + start, n), n), :] = values

    def put_noise(owner, values):
        lines = [
            values[r : r + 1, i * 2 * nb : (i + 1) * 2 * nb] for r in range(2) for i in range(few)
        ]
        at = pl.multiple_of(owner * blocks, blocks)
        noise[pl.ds(at, blocks), :] = jnp.concatenate(lines, 0)

    def put_extra(owner, first, second):
        at = pl.multiple_of(owner * blocks, blocks)
        summary[pl.ds(at, blocks), :] = jnp.concatenate(
            [joined(first, 0, few), joined(second, 0, few)], 0
        )
        both = joined(second, 3 * few, 4)
        put_noise(owner, jnp.where(core == 0, both[:2], both[2:]))

    put(me, 0, own[...])
    summary[pl.ds(pl.multiple_of(me * blocks, blocks), blocks), :] = own_summary[...]
    put_noise(me, own_noise[...])
    for step, ref, extra in ((1, step1, extra1), (2, step2, extra2), (3, step3, extra3)):
        for k, owner in enumerate(owners_of(step)):
            put(owner, 0, ref[k * rows : (k + 1) * rows, :])
            at = 2 * k * EXTRA
            put_extra(owner, extra[at : at + EXTRA, :], extra[at + EXTRA : at + 2 * EXTRA, :])
    owner, _ = owners_of(4)
    for side, ref in ((core, mine4), (1 - core, other4)):
        for start in range(0, half, 2 * BLOCK):
            values = project_rows(ref[start : start + 2 * BLOCK, :], joint)
            put(owner, side * half + start, values)
    ends = [ref[half:, :].astype(f32) for ref in (mine4, other4)]
    put_extra(
        owner, jnp.where(core == 0, ends[0], ends[1]), jnp.where(core == 0, ends[1], ends[0])
    )

    parts = three_parts(summary[...])
    logits = sum(dot_nn(part, joint[:, 6 * DH :]) for part in parts[::-1])
    logits = (logits + noise[...]) / TEMPER
    plan = jnp.stack([logits[:, :nb], logits[:, nb:]])
    for sweep in range(SINK):
        for k, axis in enumerate((2, 1)):
            plan = plan - log_total(plan, axis)
            steps[2 * sweep + k] = jnp.exp(plan)
    final = jnp.exp(plan)
    picked = []
    for h in range(2):
        picked.append(nb * jnp.sum(choices(partner_rows, h) * final[h], axis=1, keepdims=True))
    ones = jnp.ones((nb, DH), f32)
    scale_rows[...] = jnp.concatenate([ones, picked[0] * ones, ones, picked[1] * ones], 1)
    weight_rows[...] = jnp.concatenate([picked[0] * ones, picked[1] * ones], 1)

    near = first_lanes()
    work = []
    for i in range(blocks):
        block = me * blocks + i
        query, keys, values = block_operands(
            qkv, block, partner[0, block], partner[1, block], near
        )
        none = jnp.zeros_like(values[0])
        table = jnp.concatenate(
            [
                jnp.concatenate([values[0], none, values[2], none], 0),
                jnp.concatenate([none, values[1], none, values[3]], 0),
            ],
            1,
        )
        z = dot_nt(query, jnp.concatenate(keys, 0)) * (DH**-0.5)
        work.append((block, z, table))
    probs = [block_probs(z * scale_rows[pl.ds(block, 1), :]) for block, z, _ in work]
    outs = [
        dot_nn(jnp.concatenate([p.astype(bf16) for p in prob], 1), table)
        for prob, (_, _, table) in zip(probs, work)
    ]
    for i, (out, (block, _, _)) in enumerate(zip(outs, work)):
        ctx = out[:, : 2 * DH] + weight_rows[pl.ds(block, 1), :] * out[:, 2 * DH :]
        context[i * BLOCK : (i + 1) * BLOCK, :] = ctx.astype(bf16)


def feed_kernel(
    tokens, cotangent, gain, ctx0, ctx1, ctx2, ctx3, wo, wo_other, up_a, up_b, first, down_a, second, third,
    middle, h_two, active, d_hidden, ffn, d_h_two,
    ctx_full, wo_full, up_full, down_full, act_full, d_full,
):
    f32, bf16 = jnp.float32, jnp.bfloat16
    hd = lax.axis_index("head")
    row = hd // 2
    width = ctx0.shape[1]
    ff = up_a.shape[1]
    for j, c in enumerate((ctx0, ctx1, ctx2, ctx3)):
        at = pl.multiple_of((hd ^ j) * width, width)
        ctx_full[:, pl.ds(at, width)] = c[...]
        w = wo if j % 2 == 0 else wo_other
        wo_full[pl.ds(at, width), :] = w[j // 2 * width : (j // 2 + 1) * width, :]
    here, there = (pl.multiple_of((row ^ j) * ff, ff) for j in range(2))
    up_full[:, pl.ds(here, ff)] = up_a[...]
    top = up_b.shape[0]
    up_full[:top, pl.ds(there, ff)] = up_b[...]
    up_full[top:, pl.ds(there, ff)] = first[: up_a.shape[0] - top, :]
    down_full[pl.ds(here, ff), :] = down_a[...]
    n = second.shape[0]
    down_full[pl.ds(there, n), :] = second[...]
    down_full[pl.ds(pl.multiple_of(there + n, 32), ff - n), :] = third[...]
    chunk = 256
    for start in range(0, tokens.shape[0], chunk):
        sl = slice(start, start + chunk)
        mid = tokens[sl, :].astype(f32) + dot_nn(ctx_full[sl, :], wo_full[...])
        middle[sl, :] = mid
        normed, _ = norm_parts(mid)
        low = (normed * gain[...].astype(f32)).astype(bf16)
        h_two[sl, :] = low
        ffn_sum = None
        back_sum = None
        for j in range(2):
            cols = slice(j * ff, (j + 1) * ff)
            pre = dot_nn(low, up_full[:, cols])
            d_act = dot_nt(cotangent[sl, :], down_full[cols, :])
            bell = 0.5 * (1.0 + lax.erf(pre * ROOT_HALF))
            act = (pre * bell).astype(bf16)
            slope = bell + pre * jnp.exp(-0.5 * pre * pre) * INV_ROOT_TWO_PI
            d_pre = (d_act * slope).astype(bf16)
            act_full[sl, cols] = act
            d_full[sl, cols] = d_pre
            f = dot_nn(act, down_full[cols, :])
            b = dot_nt(d_pre, up_full[:, cols])
            ffn_sum = f if ffn_sum is None else ffn_sum + f
            back_sum = b if back_sum is None else back_sum + b
        ffn[sl, :] = ffn_sum
        d_h_two[sl, :] = back_sum
    mine = pl.ds(pl.multiple_of(row * ff, ff), ff)
    active[...] = act_full[:, mine]
    d_hidden[...] = d_full[:, mine]


def back_kernel(middle, own, other, cotangent, gain, w_out, d_middle, d_low, d_ctx, g_gain):
    f32, bf16 = jnp.float32, jnp.bfloat16
    normed, inv = norm_parts(middle[...])
    d_h = own[...] + other[...]
    g_gain[...] = jnp.broadcast_to(jnp.sum(d_h * normed, 0, keepdims=True), g_gain.shape)
    d_mid = cotangent[...].astype(f32) + norm_back(d_h, normed, inv, gain[...].astype(f32))
    d_middle[...] = d_mid
    low = d_mid.astype(bf16)
    d_low[...] = low
    d_ctx[...] = dot_nt(low, w_out[...]).astype(bf16)


def grads_kernel(h_two, d_hidden, active, cotangent, context, d_low, *refs):
    keeps, (front, back), (up, down, out) = refs[:7], refs[7:9], refs[9:]
    place = place_of(lax.axis_index("blk"))
    up[...] = dot_tn(h_two[...], d_hidden[...])
    down[...] = dot_tn(active[...], cotangent[...])
    out[...] = dot_tn(context[...], d_low[...])

    def rows_of(distance):
        owner = ring_of((place + distance + 8) % 8)
        parts = []
        for ref in (up, down, out):
            n = ref.shape[0] // 8
            parts.append(ref[pl.ds(pl.multiple_of(owner * n, n), n), :])
        return jnp.concatenate(parts, 0)

    for ref, distance in zip(keeps, (3, 2, 1, -3, -2, -1, 0)):
        ref[...] = rows_of(distance)
    last = rows_of(4).astype(jnp.bfloat16)
    n = front.shape[0]
    front[...] = last[:n]
    back[...] = last[n:]


def relay_kernel(keep_f, keep_b, f, b, out_f, out_b):
    f32 = jnp.float32
    n, m, size = f.shape[0], b.shape[0], keep_f.shape[0]
    out_f[...] = keep_f[...].astype(jnp.bfloat16)
    out_b[...] = keep_b[...].astype(jnp.bfloat16)
    out_f[:n, :] = (keep_f[:n, :] + f[...].astype(f32)).astype(jnp.bfloat16)
    out_b[size - m :, :] = (keep_b[size - m :, :] + b[...].astype(f32)).astype(jnp.bfloat16)


def total_kernel(keep, f, b, out):
    f32 = jnp.float32
    out[...] = (keep[...] + (f[...].astype(f32) + b[...].astype(f32))).astype(jnp.bfloat16)


def cut_kernel(f, b, front, back):
    front[...] = f[: front.shape[0], :]
    back[...] = b[b.shape[0] - back.shape[0] :, :]


def lay_kernel(own, f1, b1, f2, b2, f3, b3, f4, b4, g_up, g_down, g_out):
    f32 = jnp.float32
    place = place_of(lax.axis_index("blk"))
    last = jnp.concatenate([f4[...], b4[...]], 0)
    for distance, piece in (
        (0, own[...]), (-1, f1[...]), (1, b1[...]), (-2, f2[...]), (2, b2[...]), (-3, f3[...]), (3, b3[...]),
        (4, last),
    ):
        owner = ring_of((place + distance + 8) % 8)
        start = 0
        for ref in (g_up, g_down, g_out):
            n = ref.shape[0] // 8
            ref[pl.ds(pl.multiple_of(owner * n, n), n), :] = piece[start : start + n].astype(f32)
            start += n


def halve_kernel(f, b, front, back):
    n = front.shape[0]
    front[...] = f[:n, :]
    back[...] = b[n:, :]


def add_kernel(*refs):
    *terms, out = refs
    total = terms[0][...]
    for term in terms[1:]:
        total = total + term[...]
    out[...] = total


def four_kernel(here, one, two, three, out):
    out[...] = (here[...] + one[...]) + (two[...] + three[...])


def gains_kernel(here, other, first, second):
    total = here[...] + other[...]
    first[...] = total[0, :]
    second[...] = total[8, :]


def block_at(place, step, start, i):
    return ring_of((place + 8 - step) % 8) * (SHARD // BLOCK) + start // BLOCK + i


def prepare_kernel(pieces, qkv, partner, scale_rows, z_out, probs_out):
    place = place_of(lax.axis_index("blk"))
    near = first_lanes()
    blocks = [(step, start, i) for step, start, n in pieces for i in range(n // BLOCK)]
    for first in range(0, len(blocks), 8):
        work = []
        for step, start, i in blocks[first : first + 8]:
            block = block_at(place, step, start, i)
            query, keys, _ = block_operands(qkv, block, partner[0, block], partner[1, block], near)
            work.append((query, jnp.concatenate(keys, 0), scale_rows[pl.ds(block, 1), :]))
        z = [dot_nt(query, keys) * (DH**-0.5) for query, keys, _ in work]
        probs = [block_probs(v * w[2]) for v, w in zip(z, work)]
        for k in range(len(work)):
            at = slice((first + k) * BLOCK, (first + k + 1) * BLOCK)
            z_out[at, :] = z[k]
            probs_out[at, :] = jnp.concatenate(probs[k], 1)


def pull_kernel(pieces, offset, *refs):
    f32, bf16 = jnp.float32, jnp.bfloat16
    count = len(pieces)
    outs, refs = refs[:count], refs[count:]
    qkv, partner, scale_rows, weight_rows, refs = *refs[:4], refs[4:]
    if offset is not None:
        z_all, probs_all, refs = refs[0], refs[1], refs[2:]
    near_out, low_out, d_weight = refs
    place = place_of(lax.axis_index("blk"))
    near = first_lanes()
    scale = DH**-0.5
    blocks = [
        (step, start, d_ctx, i)
        for (step, start), d_ctx in zip(pieces, outs)
        for i in range(d_ctx.shape[0] // BLOCK)
    ]
    for first in range(0, len(blocks), 8):
        work = []
        for k, (step, start, d_ctx, i) in enumerate(blocks[first : first + 8]):
            block = block_at(place, step, start, i)
            query, keys, values = block_operands(
                qkv, block, partner[0, block], partner[1, block], near
            )
            w = dict(
                query=query,
                keys=jnp.concatenate(keys, 0),
                values=jnp.concatenate(values, 0),
                scale=scale_rows[pl.ds(block, 1), :],
                weight=weight_rows[pl.ds(block, 1), :],
                d_out=d_ctx[i * BLOCK : (i + 1) * BLOCK, :],
            )
            if offset is not None:
                at = slice((offset + first + k) * BLOCK, (offset + first + k + 1) * BLOCK)
                w["z"] = z_all[at, :]
                w["probs"] = [probs_all[at, : 2 * DH], probs_all[at, 2 * DH :]]
            work.append(w)
        if offset is None:
            for w in work:
                w["z"] = dot_nt(w["query"], w["keys"]) * scale
        for w in work:
            w["raw"] = dot_nt(w["d_out"], w["values"])
        if offset is None:
            for w in work:
                w["probs"] = block_probs(w["z"] * w["scale"])
        for w in work:
            d_z, low, d_w = [], [], []
            for h in range(2):
                sl = slice(h * 2 * DH, (h + 1) * 2 * DH)
                probs = w["probs"][h]
                d_probs = w["raw"][:, sl] * w["scale"][:, sl]
                d_scores = probs * (d_probs - jnp.sum(d_probs * probs, -1, keepdims=True))
                d_z.append((d_scores * w["scale"][:, sl]).astype(bf16))
                low.append(probs.astype(bf16))
                d_w.append(
                    jnp.sum(
                        d_scores * w["z"][:, sl] + low[h].astype(f32) * w["raw"][:, sl],
                        0,
                        keepdims=True,
                    )
                )
            w["d_z"], w["low"] = jnp.concatenate(d_z, 1), jnp.concatenate(low, 1)
            w["d_w"] = jnp.concatenate(d_w, 1)
        for w in work:
            w["d_query"] = dot_nn(w["d_z"], w["keys"]) * scale
        for w in work:
            w["d_keys"] = dot_tn(w["d_z"], w["query"]) * scale
        for w in work:
            w["d_values"] = dot_tn(w["low"], w["d_out"])
        for k, w in enumerate(work):
            to = first + k
            at = slice(to * BLOCK, (to + 1) * BLOCK)
            d_weight[to : to + 1, :] = w["d_w"]
            low_out[at, : 2 * DH] = w["d_query"].astype(bf16)
            for m, name in enumerate(("d_keys", "d_values")):
                parts = [w[name][i * BLOCK : (i + 1) * BLOCK, :] for i in range(4)]
                near_out[at, m * 2 * DH : (m + 1) * 2 * DH] = jnp.where(near, parts[0], parts[2])
                far = jnp.where(near, parts[1], parts[3])
                if m == 1:
                    far = far * w["weight"]
                low_out[at, (m + 1) * 2 * DH : (m + 2) * 2 * DH] = far.astype(bf16)


def collect_kernel(pieces, *refs):
    f32, bf16 = jnp.float32, jnp.bfloat16
    count = len(pieces)
    nears, lows, d_weights = refs[:count], refs[count : 2 * count], refs[2 * count : 3 * count]
    partner, partner_rows, steps, summary = refs[3 * count : 3 * count + 4]
    d_qkv, d_mine, flat_mine, g_sort, d_weight, acc, far, d_flat = refs[3 * count + 4 :]
    me = lax.axis_index("blk")
    place = place_of(me)
    for parts, near_ref, low_ref, w_ref in zip(pieces, nears, lows, d_weights):
        at = 0
        for step, start, n in parts:
            owner = ring_of((place + 8 - step) % 8)
            to = pl.ds(pl.multiple_of(owner * SHARD + start, n), n)
            acc[to, :] = near_ref[at : at + n, :]
            far[to, :] = low_ref[at : at + n, 2 * DH :]
            d_qkv[to, : 2 * DH] = low_ref[at : at + n, : 2 * DH]
            if start == 0:
                nb = SHARD // BLOCK
                first = pl.multiple_of(owner * nb, nb)
                d_weight[pl.ds(first, nb), :] = w_ref[at // BLOCK : at // BLOCK + nb, :]
            at += n
    near = first_lanes()
    both = jnp.concatenate([near, near], 1)

    def body(block, _):
        tile = far[pl.ds(pl.multiple_of(block * BLOCK, BLOCK), BLOCK), :].astype(f32)
        for h, kept in ((0, jnp.where(both, tile, 0.0)), (1, jnp.where(both, 0.0, tile))):
            to = pl.ds(pl.multiple_of(partner[h, block] * BLOCK, BLOCK), BLOCK)
            acc[to, :] += kept
        return 0

    lax.fori_loop(0, partner.shape[1], body, 0, unroll=4)
    d_qkv[:, 2 * DH :] = acc[...].astype(bf16)
    d_mine[...] = d_qkv[pl.ds(pl.multiple_of(me * SHARD, SHARD), SHARD), :]
    d_flat[...] = sink_back(d_weight[...], steps, partner_rows)
    n = flat_mine.shape[0]
    flat_mine[...] = d_flat[pl.ds(pl.multiple_of(me * n, n), n), :]
    g_sort[...] = lax.dot_general(
        summary[...],
        d_flat[...],
        (((0,), (0,)), ((), ())),
        precision=HIGHEST,
        preferred_element_type=f32,
    )


def sink_back(d_weight, steps, partner):
    nb = partner.shape[1]
    grads = []
    for h in range(2):
        total = jnp.sum(
            d_weight[:, (2 * h + 1) * DH : (2 * h + 2) * DH], axis=1, keepdims=True
        )
        grads.append(choices(partner, h) * (nb * total))
    last = steps.shape[0] - 1
    grad = jnp.stack(grads) * steps[last]
    for t in range(last, -1, -1):
        grad = grad - steps[t] * jnp.sum(grad, axis=1 if t % 2 else 2, keepdims=True)
    return jnp.concatenate([grad[0], grad[1]], 1) / TEMPER


def weight_kernel(own, m1, o1, m2, o2, m3, o3, m4, o4, d_qkv, g_qkv, h_all):
    me = lax.axis_index("blk")
    core = lax.axis_index("head") % 2
    half = m4.shape[0] - EXTRA
    rows = 2 * half

    def put(owner, start, ref):
        for k in range(ref.shape[0] // (half + EXTRA)):
            at = pl.ds(pl.multiple_of(owner * rows + start + k * half, half), half)
            h_all[at, :] = ref[k * (half + EXTRA) : k * (half + EXTRA) + half, :]

    put(me, 0, own)
    for step, refs in ((1, (m1, o1)), (2, (m2, o2)), (3, (m3, o3))):
        for owner, ref in zip(owners_of(step), refs):
            put(owner, 0, ref)
    owner, _ = owners_of(4)
    put(owner, core * half, m4)
    put(owner, (1 - core) * half, o4)
    out = dot_tn(h_all[...], d_qkv[...])
    width = g_qkv.shape[2]
    for i in range(3):
        g_qkv[i] = out[:, i * width : (i + 1) * width]


def input_kernel(dq_a, dq_b, joint_a, joint_b, flat_a, flat_b, d_h, dq_full, w_full, flat_full, sort_full):
    row = lax.axis_index("head") // 2
    width, nb = dq_a.shape[1], flat_a.shape[1]
    sides = ((dq_a, joint_a, flat_a), (dq_b, joint_b, flat_b))
    for j, (g, joint, flat) in enumerate(sides):
        at = pl.multiple_of((row ^ j) * width, width)
        dq_full[:, pl.ds(at, width)] = g[...]
        w_full[:, pl.ds(at, width)] = joint[:, :width]
        at = pl.multiple_of((row ^ j) * nb, nb)
        flat_full[:, pl.ds(at, nb)] = flat[...]
        sort_full[:, pl.ds(at, nb)] = joint[:, width:]
    part = dot_nt(dq_full[...], w_full[...])
    d_sum = sum(dot_nt(p, sort_full[...]) for p in three_parts(flat_full[...])[::-1]) / BLOCK
    blocks = d_sum.shape[0]
    for i in range(blocks):
        sl = slice(i * BLOCK, (i + 1) * BLOCK)
        d_h[sl, :] = part[sl, :] + d_sum[i : i + 1, :]


def gain_kernel(tokens, d_mine, flat_mine, joint, g_two, out):
    width = d_mine.shape[1]
    normed, _ = norm_parts(tokens[...].astype(jnp.float32))
    part = dot_nt(d_mine[...], joint[:, :width])
    d_sum = sum(dot_nt(p, joint[:, width:]) for p in three_parts(flat_mine[...])[::-1]) / BLOCK
    blocks = d_sum.shape[0]
    sums = jnp.sum(part * normed, 0, keepdims=True)
    means = jnp.sum(normed.reshape(blocks, BLOCK, D), 1)
    sums = sums + jnp.sum(d_sum * means, 0, keepdims=True)
    out[:8, :] = jnp.broadcast_to(sums, g_two.shape)
    out[8:, :] = jnp.where(lax.axis_index("head") == 0, g_two[...], 0.0)


def end_kernel(tokens, gain, own, other, d_middle, d_tokens):
    f32 = jnp.float32
    normed, inv = norm_parts(tokens[...].astype(f32))
    d_h = own[...] + other[...]
    d_tokens[...] = d_middle[...] + norm_back(d_h, normed, inv, gain[...].astype(f32))


VMEM_SPEC = pl.BlockSpec(memory_space=pltpu.VMEM)
SMEM_SPEC = pl.BlockSpec(memory_space=pltpu.SMEM)
ANY_SPEC = pl.BlockSpec(memory_space=pltpu.HBM)


def fetch(pairs, sems, first=0):
    copies = []
    for k, (source, target) in enumerate(pairs):
        copies.append(pltpu.make_async_copy(source, target, sems.at[first + k]))
        copies[-1].start()
    return copies


def wait_all(copies):
    for copy in copies:
        copy.wait()


def call(kernel, outs, *args, scratch=(), smem=(), cold=(), raw=(), out_cold=(), limit=16, name=None):
    cost = int(1e3 * TIMES[name])
    shapes = [jax.ShapeDtypeStruct(s, d) for s, d in outs]
    specs = [
        SMEM_SPEC if i in smem else ANY_SPEC if i in cold or i in raw else VMEM_SPEC
        for i in range(len(args))
    ]
    out_specs = [ANY_SPEC if i in out_cold else VMEM_SPEC for i in range(len(outs))]
    buffers = [pltpu.VMEM(args[i].shape, args[i].dtype) for i in cold]
    buffers += [pltpu.VMEM(*outs[i]) for i in out_cold]
    sem_count = len(cold) + len(out_cold)
    sems = [pltpu.SemaphoreType.DMA((sem_count,))] if sem_count else []
    own = [pltpu.SemaphoreType.DMA((40,))] if raw else []

    def body(*refs):
        refs = list(refs)
        ins, results = refs[: len(args)], refs[len(args) : len(args) + len(outs)]
        rest = refs[len(args) + len(outs) :]
        mine, rest = rest[: len(scratch)], rest[len(scratch) :]
        room, rest = rest[: len(buffers)], rest[len(buffers) :]
        copies = []
        if cold:
            copies = fetch([(ins[i], room[k]) for k, i in enumerate(cold)], rest[0])
            for k, i in enumerate(cold):
                ins[i] = room[k]
        targets = list(results)
        for k, i in enumerate(out_cold):
            results[i] = room[len(cold) + k]
        wait_all(copies)
        kernel(*ins, *results, *mine, *(rest[-1:] if raw else []))
        if out_cold:
            wait_all(fetch([(results[i], targets[i]) for i in out_cold], rest[0], len(cold)))

    result = pl.pallas_call(
        body,
        out_shape=shapes,
        in_specs=specs,
        out_specs=out_specs,
        scratch_shapes=[pltpu.VMEM(s, d) for s, d in scratch] + buffers + sems + own,
        compiler_params=pltpu.CompilerParams(vmem_limit_bytes=limit * 1024 * 1024),
        cost_estimate=pl.CostEstimate(
            flops=cost * FLOPS, bytes_accessed=cost * BYTES, transcendentals=0
        ),
        name=name,
    )(*args)
    return result[0] if len(shapes) == 1 else result


TIMES = {
    "norm_one": 1.7,
    "project_own": 0.45,
    "project": 0.7,
    "attend": 4.2,
    "prepare": 2.9,
    "feed": 4.2,
    "back": 1.2,
    "pull": 2.4,
    "grads": 0.95,
    "relay": 0.2,
    "collect": 4.5,
    "sinkhorn_back": 2.05,
    "total": 0.25,
    "input_back": 1.0,
    "gain_part": 0.8,
    "weights": 3.6,
    "norm_one_back": 1.7,
    "output": 1.1,
    "lay": 1.6,
    "gains": 0.6,
    "halve": 0.1,
    "half": 0.1,
    "pair": 0.1,
    "add_gains": 0.1,
    "sum_gains": 0.1,
}
FLOPS, BYTES = 1150000, 3690


def tie(*values):
    return lax.optimization_barrier(values)


def after(value, *others):
    return lax.optimization_barrier((value,) + others)[0]


RING = (0, 2, 4, 6, 7, 5, 3, 1)
SHARD = 512
EXTRA = 32


def local_eight(
    tokens, gain_attn, gain_ffn, w_qkv, w_out, w_sort, w_up, w_down, gumbel_noise, partner, cotangent
):
    f32, bf16 = jnp.float32, jnp.bfloat16
    rows = tokens.shape[0]
    blocks = rows // BLOCK
    width = w_out.shape[0]
    ff = w_up.shape[1]
    nb = partner.shape[0]
    total = nb * BLOCK
    half, quarter = rows // 2, rows // 4
    core = lax.axis_index("head") % 2

    def ahead(v):
        return lax.ppermute(v, "blk", [(RING[i], RING[(i + 1) % 8]) for i in range(8)])

    def behind(v):
        return lax.ppermute(v, "blk", [(RING[i], RING[(i - 1) % 8]) for i in range(8)])

    def swap_head(v, j):
        return lax.ppermute(v, "head", [(i, i ^ j) for i in range(4)])

    def swap_blk(v, j):
        return lax.ppermute(v, "blk", [(i, i ^ j) for i in range(8)])

    w_in = w_qkv.transpose(1, 0, 2)
    partner_s = partner.T

    def along(v):
        pairs = []
        for i in range(8):
            for h in range(4):
                to = RING[(i + 1) % 8] if h % 2 == 0 else RING[(i - 1) % 8]
                pairs.append((RING[i] * 4 + h, to * 4 + h))
        return lax.ppermute(v, ("blk", "head"), pairs)

    shard, own_summary, own_noise, up_0 = call(
        head_kernel,
        [((rows + 2 * EXTRA, D), bf16), ((blocks, D), f32), ((2, D), f32), ((320, ff), bf16)],
        tokens, gain_attn, gumbel_noise, swap_head(gumbel_noise, 1), w_up,
        cold=(0, 1, 2, 3, 4), limit=62, name="norm_one",
    )

    def project(mine, other):
        return call(
            project_kernel, [((2 * rows, 3 * width), bf16), ((4 * EXTRA, D), bf16)], mine, other, joint,
            name="project",
        )

    m1 = along(shard)
    up_y0 = swap_head(up_0, 2)
    qkv_own, joint, first, second, third = call(
        project_own_kernel,
        [
            ((rows, 3 * width), bf16), ((D, 3 * width + 2 * nb), bf16),
            ((D - 320 + width, D), bf16), ((352, D), bf16), ((ff - 352, D), bf16),
        ],
        shard, w_in, w_sort, w_out, w_up, w_down, name="project_own",
    )
    m1, up_y0, qkv_own = tie(m1, up_y0, qkv_own)
    m2 = along(m1)
    first_y = swap_head(after(first, m1), 2)
    m2, first_y = tie(m2, first_y)
    m3 = along(m2)
    second_y = swap_head(after(second, m2), 2)
    m3, second_y = tie(m3, second_y)
    half_3, wo = call(
        half_kernel, [((half + EXTRA, D), bf16), ((2 * width, D), bf16)], m3, w_out, first_y, name="half"
    )
    m4 = along(half_3)
    third_y = swap_head(after(third, m3), 2)
    o1 = swap_head(after(m1, half_3), 1)
    o2 = swap_head(after(m2, half_3), 1)
    o3 = swap_head(after(m3, half_3), 1)
    qkv1 = project(m1, o1)
    qkv2 = project(m2, o2)
    qkv3 = project(m3, o3)
    m4, third_y, _, _, _ = tie(m4, third_y, qkv1[0], qkv2[0], qkv3[0])
    o4 = swap_head(m4, 1)
    qkv, context, summary, steps, scale_rows, weight_rows = call(
        attend_kernel,
        [
            ((total, 3 * width), bf16), ((rows, width), bf16), ((nb, D), f32),
            ((2 * SINK, 2, nb, nb), f32), ((nb, 4 * DH), f32), ((nb, 2 * DH), f32),
        ],
        qkv_own, qkv1[0], qkv2[0], qkv3[0], qkv1[1], qkv2[1], qkv3[1], m4, o4, joint, own_summary, own_noise,
        partner_s, partner_s, smem=(12,), scratch=[((nb, 2 * nb), f32)], name="attend",
    )
    ctx_y, ctx_c = swap_head(context, 2), swap_head(context, 1)
    wo_other = swap_head(after(wo, context), 1)
    prepared = ((3, 0, rows), (-3, 0, rows), (4, 0, rows))
    amount = sum(n for _, _, n in prepared)
    z_all, probs_all = call(
        functools.partial(prepare_kernel, prepared), [((amount, 4 * DH), f32)] * 2,
        qkv, partner_s, scale_rows, smem=(1,), name="prepare",
    )
    ctx_y, ctx_c, z_all = tie(ctx_y, ctx_c, z_all)
    ctx_yc = swap_head(ctx_y, 1)
    middle, h_two, active, d_hidden, ffn, d_h_two = call(
        feed_kernel,
        [
            ((rows, D), f32),
            ((rows, D), bf16),
            ((rows, ff), bf16),
            ((rows, ff), bf16),
            ((rows, D), f32),
            ((rows, D), f32),
        ],
        tokens, cotangent, gain_ffn, context, ctx_c, ctx_y, ctx_yc, wo, wo_other,
        w_up, up_y0, first_y, w_down, second_y, third_y,
        scratch=[
            ((rows, 4 * width), bf16), ((4 * width, D), bf16), ((D, 2 * ff), bf16), ((2 * ff, D), bf16),
            ((rows, 2 * ff), bf16), ((rows, 2 * ff), bf16),
        ],
        name="feed",
    )
    d_h_two_other = swap_head(d_h_two, 1)
    d_middle, d_low, d_ctx, g_two = call(
        back_kernel,
        [((rows, D), f32), ((rows, D), bf16), ((rows, width), bf16), ((8, D), f32)],
        middle, d_h_two, d_h_two_other, cotangent, gain_ffn, w_out, name="back",
    )

    plans = [[(0, 0)]] + [[(k, 0), (-k, 0)] for k in (1, 2, 3)] + [[(4, 0), (4, half)]]
    offsets = (None, None, None, 0, 2 * blocks)
    pulled = []

    def pull(given):
        plan, offset = plans[len(pulled)], offsets[len(pulled)]
        n = sum(a.shape[0] for a in given)
        pulled.append(
            call(
                functools.partial(pull_kernel, tuple(plan), offset),
                [((n, 4 * DH), f32), ((n, 6 * DH), bf16), ((n // BLOCK, 4 * DH), f32)],
                *given, qkv, partner_s, scale_rows, weight_rows,
                *([] if offset is None else [z_all, probs_all]),
                smem=(len(given) + 1,), name="pull",
            )
        )
        return pulled[-1][0]

    piece = (D + ff + width) // 8
    front = 80
    parts = call(
        grads_kernel,
        [((piece, D), f32)] * 7 + [((front, D), bf16), ((piece - front, D), bf16)],
        h_two, d_hidden, active, cotangent, context, d_low,
        scratch=[((D, ff), f32), ((ff, D), f32), ((width, D), f32)], name="grads",
    )
    keeps, (sum_f, sum_b) = parts[:7], parts[7:]
    given = [d_ctx]
    arrays = [given]
    d_ctx, sum_f, sum_b = tie(d_ctx, sum_f, sum_b)
    f = b = d_ctx
    joint_y = swap_head(after(joint, sum_f), 2)
    for step in range(4):
        if step == 3:
            f, b = call(halve_kernel, [((half, width), bf16)] * 2, f, b, name="halve")
        f, b = ahead(f), behind(b)
        sum_f, sum_b = ahead(sum_f), behind(sum_b)
        done = pull(given)
        hold = [joint_y] if step == 2 else []
        f, b, sum_f, sum_b, _ = tie(f, b, sum_f, sum_b, done, *hold)[:5]
        given = [f, b]
        arrays.append(given)
        if step < 3:
            sum_f, sum_b = call(
                relay_kernel, [((piece, D), bf16)] * 2, keeps[step], keeps[step + 3], sum_f, sum_b,
                name="relay",
            )
    owned = call(total_kernel, [((piece, D), bf16)], keeps[6], sum_f, sum_b, name="total")
    wf1, wb1 = ahead(owned), behind(owned)
    pull(given)
    spans = tuple(
        tuple((step, start, a.shape[0]) for (step, start), a in zip(plan, given))
        for plan, given in zip(plans, arrays)
    )
    d_qkv, d_mine, flat_mine, g_sort = call(
        functools.partial(collect_kernel, spans),
        [
            ((total, 3 * width), bf16), ((rows, 3 * width), bf16), ((blocks, 2 * nb), f32), ((D, 2 * nb), f32),
        ],
        *[p[k] for k in range(3) for p in pulled], partner_s, partner_s, steps, summary, smem=(15,),
        scratch=[
            ((nb, 4 * DH), f32), ((total, 4 * DH), f32), ((total, 4 * DH), bf16), ((nb, 2 * nb), f32),
        ],
        name="collect",
    )
    wf1, wb1, d_mine, flat_mine = tie(wf1, wb1, d_mine, flat_mine)
    wf2, wb2 = ahead(wf1), behind(wb1)
    d_mine_y, flat_y = swap_head(d_mine, 2), swap_head(flat_mine, 2)
    gains_a = call(
        gain_kernel, [((16, D), f32)], tokens, d_mine, flat_mine, joint, g_two, name="gain_part"
    )
    gains_x = swap_blk(gains_a, 1)
    gains = call(add_kernel, [((16, D), f32)], gains_a, gains_x, name="add_gains")
    wf2, wb2, d_mine_y, flat_y, gains = tie(wf2, wb2, d_mine_y, flat_y, gains)
    wf3, wb3 = ahead(wf2), behind(wb2)
    gains1, gains2, gains3 = swap_blk(gains, 2), swap_blk(gains, 4), swap_blk(gains, 6)
    d_h = call(
        input_kernel, [((rows, D), f32)],
        d_mine, d_mine_y, joint, joint_y, flat_mine, flat_y,
        scratch=[
            ((rows, 6 * width), bf16), ((D, 6 * width), bf16), ((blocks, 4 * nb), f32), ((D, 4 * nb), bf16),
        ],
        name="input_back",
    )
    d_h_other = swap_head(d_h, 1)
    g_qkv = call(
        weight_kernel, [((3, D, width), f32)],
        shard, m1, o1, m2, o2, m3, o3, m4, o4, after(d_qkv, d_h),
        scratch=[((total, D), bf16)], limit=24, name="weights",
    )
    wf3, wb3, gains1, gains2, gains3, d_h_other, g_qkv = tie(
        wf3, wb3, gains1, gains2, gains3, d_h_other, g_qkv
    )
    cut_f, cut_b = call(
        cut_kernel, [((front, D), bf16), ((piece - front, D), bf16)], wf3, wb3, name="halve"
    )
    wf4, wb4 = ahead(cut_f), behind(cut_b)
    gains = call(four_kernel, [((16, D), f32)], gains, gains1, gains2, gains3, name="sum_gains")
    gains_y = swap_head(gains, 2)
    d_tokens = call(
        end_kernel, [((rows, D), f32)],
        tokens, gain_attn, d_h, d_h_other, d_middle, name="norm_one_back",
    )
    ffn_other = swap_head(after(ffn, wf3), 1)
    gains = call(add_kernel, [((16, D), f32)], gains, gains_y, name="add_gains")
    gains_c = swap_head(gains, 1)
    output = call(add_kernel, [((rows, D), f32)], ffn, ffn_other, middle, name="output")
    g_up, g_down, g_out = call(
        lay_kernel,
        [((D, ff), f32), ((ff, D), f32), ((width, D), f32)],
        owned, wf1, wb1, wf2, wb2, wf3, wb3, wf4, wb4, name="lay",
    )
    g_one, g_two = call(gains_kernel, [((D,), f32), ((D,), f32)], gains, gains_c, name="gains")
    return output, d_tokens, g_one, g_two, g_qkv.transpose(1, 0, 2), g_out, g_sort, g_up, g_down


def solution(mesh):
    in_specs = (
        P("blk", None),
        P(),
        P(),
        P(None, None, "head"),
        P("head", None),
        P(None, "head"),
        P(None, "head"),
        P("head", None),
        P("blk", "head", None),
        P(None, "head"),
        P("blk", None),
    )
    out_specs = (
        P("blk", None),
        P("blk", None),
        P(),
        P(),
        P(None, None, "head"),
        P("head", None),
        P(None, "head"),
        P(None, "head"),
        P("head", None),
    )
    plan = local_eight if mesh.shape["blk"] == 8 and mesh.shape["head"] == 4 else local
    return jax.shard_map(plan, mesh=mesh, in_specs=in_specs, out_specs=out_specs, check_vma=False)
```

```python
import functools
import math

import jax
import jax.numpy as jnp
from jax import lax
from jax.experimental import pallas as pl
from jax.experimental.pallas import tpu as pltpu
from jax.sharding import PartitionSpec as P

D = 512
DH = 64
BLOCK = 64
SINK = 8


EPS = 1e-05
TEMPER = 0.75
ROOT_HALF = 0.7071067811865476
INV_ROOT_TWO_PI = 0.3989422804014327
HIGHEST = lax.Precision.HIGHEST


def normalize(values, norm_gain):
    average = jnp.mean(values, -1, keepdims=True)
    centred = values - average
    inv_std = lax.rsqrt(jnp.mean(centred * centred, -1, keepdims=True) + EPS)
    normed = centred * inv_std
    return (normed * norm_gain, normed, inv_std)


def norm_back(d_out, normed, inv_std, norm_gain):
    d_normed = d_out * norm_gain
    return inv_std * (
        d_normed
        - jnp.mean(d_normed, -1, keepdims=True)
        - normed * jnp.mean(d_normed * normed, -1, keepdims=True)
    )


def log_total(values, axis):
    highest = jnp.max(values, axis=axis, keepdims=True)
    return highest + jnp.log(jnp.sum(jnp.exp(values - highest), axis=axis, keepdims=True))


def balancing_log_space(sort_logits):
    for sweep in range(SINK):
        sort_logits = sort_logits - log_total(sort_logits, 2)
        sort_logits = sort_logits - log_total(sort_logits, 1)
    return sort_logits


def gelu_value(values):
    return 0.5 * values * (1.0 + lax.erf(values * ROOT_HALF))


def gelu_slope(values):
    return (
        0.5 * (1.0 + lax.erf(values * ROOT_HALF))
        + values * jnp.exp(-0.5 * values * values) * INV_ROOT_TWO_PI
    )


def local(
    tokens,
    gain_attn,
    gain_ffn,
    w_qkv,
    w_out,
    w_sort,
    w_up,
    w_down,
    gumbel_noise,
    partner,
    cotangent,
):
    f32 = jnp.float32
    bf16 = jnp.bfloat16
    tok_rows = tokens.shape[0]
    blocks_dev = tok_rows // BLOCK
    heads_dev = w_out.shape[0] // DH
    width_dev = heads_dev * DH
    requests = blocks_dev * heads_dev
    dev_count = lax.axis_size("blk")
    my_index = lax.axis_index("blk")
    first_block = my_index * blocks_dev
    seq_blocks = partner.shape[0]
    scale = DH ** (-0.5)
    gain_one = gain_attn.astype(f32)
    gain_two = gain_ffn.astype(f32)
    inputs = tokens.astype(f32)
    h_one, normed_one, inv_one = normalize(inputs, gain_one)
    h_one_low = h_one.astype(bf16)
    qkv = jnp.einsum("td,dcf->tcf", h_one_low, w_qkv, preferred_element_type=f32).astype(bf16)
    summary = jnp.mean(h_one.reshape(blocks_dev, BLOCK, D), axis=1)
    sort_mat = w_sort.astype(f32)
    own_rows = (
        jnp.dot(summary, sort_mat, precision=HIGHEST).reshape(blocks_dev, heads_dev, seq_blocks)
        + gumbel_noise
    ) / TEMPER
    every_rows = lax.all_gather(own_rows, "blk", axis=0, tiled=True)
    my_partner = lax.dynamic_slice_in_dim(partner, first_block, blocks_dev, 0)

    def own_weights(sequence_rows):
        balanced_plan = balancing_log_space(sequence_rows.transpose(1, 0, 2))
        mine = lax.dynamic_slice_in_dim(jnp.exp(balanced_plan), first_block, blocks_dev, 1)
        return seq_blocks * jnp.take_along_axis(mine, my_partner.T[:, :, None], axis=2)[:, :, 0]

    weight_hb, sink_pull = jax.vjp(own_weights, every_rows)
    weight_matrix = weight_hb.T
    owner_all = (partner // blocks_dev).reshape(dev_count, requests)
    slot_all = (
        partner % blocks_dev * heads_dev + jnp.arange(heads_dev, dtype=jnp.int32)[None, :]
    ).reshape(dev_count, requests)
    owner_mine = lax.dynamic_index_in_dim(owner_all, my_index, 0, keepdims=False)
    tile_ids = jnp.arange(requests, dtype=jnp.int32)
    key_value = (
        qkv[:, 1:3]
        .reshape(blocks_dev, BLOCK, 2, heads_dev, DH)
        .transpose(0, 3, 1, 2, 4)
        .reshape(requests, BLOCK, 2 * DH)
    )
    empty_tile = jnp.zeros((), bf16)
    wanted = owner_all == my_index
    outgoing = jnp.where(
        wanted[:, :, None, None], jnp.take(key_value, slot_all, axis=0), empty_tile
    )
    incoming = lax.all_to_all(outgoing, "blk", split_axis=0, concat_axis=0, tiled=True)
    partner_tiles = jnp.sum(incoming, axis=0, dtype=f32).astype(bf16)
    far_tiles = partner_tiles.reshape(blocks_dev, heads_dev, BLOCK, 2, DH)
    key_far = far_tiles[:, :, :, 0]
    value_far = far_tiles[:, :, :, 1]
    query_b = qkv[:, 0].reshape(blocks_dev, BLOCK, heads_dev, DH)
    key_b = qkv[:, 1].reshape(blocks_dev, BLOCK, heads_dev, DH)
    value_b = qkv[:, 2].reshape(blocks_dev, BLOCK, heads_dev, DH)
    weight_s = weight_matrix[:, :, None, None]

    def score_parts():
        near_z = scale * jnp.einsum("bqhd,bkhd->bhqk", query_b, key_b, preferred_element_type=f32)
        far_z = scale * jnp.einsum("bqhd,bhkd->bhqk", query_b, key_far, preferred_element_type=f32)
        return (near_z, far_z, jnp.concatenate([near_z, weight_s * far_z], -1))

    near_z, far_z, scores = score_parts()
    highest = jnp.max(scores, -1, keepdims=True)
    expo = jnp.exp(scores - highest)
    row_total = jnp.sum(expo, -1, keepdims=True)
    log_sum = highest + jnp.log(row_total)
    probs_low = (expo / row_total).astype(bf16)
    near_ctx = jnp.einsum(
        "bhqk,bkhd->bqhd", probs_low[..., :BLOCK], value_b, preferred_element_type=f32
    )
    far_ctx = jnp.einsum(
        "bhqk,bhkd->bqhd", probs_low[..., BLOCK:], value_far, preferred_element_type=f32
    )
    context = near_ctx + weight_matrix[:, None, :, None] * far_ctx
    context_low = context.reshape(tok_rows, width_dev).astype(bf16)
    attn = lax.psum(jnp.dot(context_low, w_out, preferred_element_type=f32), "head")
    middle = inputs + attn
    h_two, normed_two, inv_two = normalize(middle, gain_two)
    h_two_low = h_two.astype(bf16)
    hidden_pre = jnp.dot(h_two_low, w_up, preferred_element_type=f32)
    active_low = gelu_value(hidden_pre).astype(bf16)
    ffn = lax.psum(
        jnp.dot(active_low, w_down, preferred_element_type=f32).astype(jnp.bfloat16), "head"
    ).astype(jnp.float32)
    output = middle + ffn
    g_down = jnp.einsum("tf,td->fd", active_low, cotangent, preferred_element_type=f32)
    d_active = jnp.einsum("td,fd->tf", cotangent, w_down, preferred_element_type=f32)
    d_hidden = (d_active * gelu_slope(hidden_pre)).astype(bf16)
    g_up = jnp.einsum("td,tf->df", h_two_low, d_hidden, preferred_element_type=f32)
    d_h_two = lax.psum(jnp.einsum("tf,df->td", d_hidden, w_up, preferred_element_type=f32), "head")
    g_gain_two = jnp.sum(d_h_two * normed_two, 0)
    d_middle = cotangent.astype(f32) + norm_back(d_h_two, normed_two, inv_two, gain_two)
    d_attn_low = d_middle.astype(bf16)
    g_out = jnp.einsum("tf,td->fd", context_low, d_attn_low, preferred_element_type=f32)
    d_context = jnp.einsum("td,fd->tf", d_attn_low, w_out, preferred_element_type=f32).astype(bf16)
    d_context = d_context.reshape(blocks_dev, BLOCK, heads_dev, DH)
    near_z, far_z, scores = score_parts()
    probs = jnp.exp(scores - log_sum)
    probs_low = probs.astype(bf16)
    far_ctx = jnp.einsum(
        "bhqk,bhkd->bqhd", probs_low[..., BLOCK:], value_far, preferred_element_type=f32
    )
    d_probs_near = jnp.einsum("bqhd,bkhd->bhqk", d_context, value_b, preferred_element_type=f32)
    d_probs_far = weight_s * jnp.einsum(
        "bqhd,bhkd->bhqk", d_context, value_far, preferred_element_type=f32
    )
    d_probs = jnp.concatenate([d_probs_near, d_probs_far], -1)
    d_scores = probs * (d_probs - jnp.sum(d_probs * probs, -1, keepdims=True))
    d_near = d_scores[..., :BLOCK].astype(bf16)
    d_far_raw = d_scores[..., BLOCK:]
    d_far = (weight_s * d_far_raw).astype(bf16)
    d_weight = jnp.sum(d_far_raw * far_z, (2, 3)) + jnp.sum(d_context.astype(f32) * far_ctx, (1, 3))
    d_query = scale * (
        jnp.einsum("bhqk,bkhd->bqhd", d_near, key_b, preferred_element_type=f32)
        + jnp.einsum("bhqk,bhkd->bqhd", d_far, key_far, preferred_element_type=f32)
    )
    d_key = scale * jnp.einsum("bhqk,bqhd->bkhd", d_near, query_b, preferred_element_type=f32)
    d_value = jnp.einsum(
        "bhqk,bqhd->bkhd", probs_low[..., :BLOCK], d_context, preferred_element_type=f32
    )
    d_key_far = scale * jnp.einsum("bhqk,bqhd->bhkd", d_far, query_b, preferred_element_type=f32)
    d_value_far = weight_s * jnp.einsum(
        "bhqk,bqhd->bhkd", probs_low[..., BLOCK:], d_context, preferred_element_type=f32
    )
    grad_tiles = jnp.stack([d_key_far.astype(bf16), d_value_far.astype(bf16)], 3).reshape(
        requests, BLOCK * 2 * DH
    )
    peers = jnp.arange(dev_count, dtype=jnp.int32)
    outgoing_grads = jnp.where(
        (owner_mine[None, :] == peers[:, None])[:, :, None], grad_tiles[None], empty_tile
    )
    returned = lax.all_to_all(outgoing_grads, "blk", split_axis=0, concat_axis=0, tiled=True)
    selector = (owner_all == my_index)[:, :, None] & (
        slot_all[:, :, None] == tile_ids[None, None, :]
    )
    selector = selector.reshape(dev_count * requests, requests).astype(bf16)
    remote = jnp.einsum(
        "st,sf->tf",
        selector,
        returned.reshape(dev_count * requests, BLOCK * 2 * DH),
        preferred_element_type=f32,
    )
    remote = (
        remote.reshape(blocks_dev, heads_dev, BLOCK, 2, DH)
        .transpose(0, 2, 3, 1, 4)
        .reshape(tok_rows, 2, width_dev)
    )
    near_kv = (
        jnp.stack([d_key.reshape(tok_rows, width_dev), d_value.reshape(tok_rows, width_dev)], 1)
        + remote
    )
    d_qkv = jnp.concatenate([d_query.reshape(tok_rows, 1, width_dev), near_kv], 1).astype(bf16)
    g_qkv = jnp.einsum("td,tcf->dcf", h_one_low, d_qkv, preferred_element_type=f32)
    d_h_part = jnp.einsum("tcf,dcf->td", d_qkv, w_qkv, preferred_element_type=f32)
    (d_every,) = sink_pull(d_weight.T)
    d_own = lax.psum_scatter(d_every, "blk", scatter_dimension=0, tiled=True) / TEMPER
    d_flat = d_own.reshape(blocks_dev, heads_dev * seq_blocks)
    g_sort = jnp.dot(summary.T, d_flat, precision=HIGHEST)
    d_summary = jnp.dot(d_flat, sort_mat.T, precision=HIGHEST)
    d_h_part = (d_h_part.reshape(blocks_dev, BLOCK, D) + d_summary[:, None, :] / BLOCK).reshape(
        tok_rows, D
    )
    d_h_one = lax.psum(d_h_part, "head")
    g_gain_one = jnp.sum(d_h_one * normed_one, 0)
    d_tokens = d_middle + norm_back(d_h_one, normed_one, inv_one, gain_one)
    summed = lax.psum((g_gain_one, g_gain_two, g_qkv, g_out, g_sort, g_up, g_down), "blk")
    return (
        output,
        d_tokens,
        summed[0],
        summed[1],
        summed[2],
        summed[3],
        summed[4],
        summed[5],
        summed[6],
    )


def mask_pair(values, near):
    zero = jnp.zeros_like(values)
    return jnp.where(near, values, zero), jnp.where(near, zero, values)


def first_lanes():
    return lax.broadcasted_iota(jnp.int32, (1, 2 * DH), 1) < DH


def dot_nn(a, b):
    return lax.dot_general(a, b, (((1,), (0,)), ((), ())), preferred_element_type=jnp.float32)


def dot_nt(a, b):
    return lax.dot_general(a, b, (((1,), (1,)), ((), ())), preferred_element_type=jnp.float32)


def dot_tn(a, b):
    return lax.dot_general(a, b, (((0,), (0,)), ((), ())), preferred_element_type=jnp.float32)


def three_parts(values):
    high = values.astype(jnp.bfloat16)
    rest = values - high.astype(jnp.float32)
    mid = rest.astype(jnp.bfloat16)
    low = (rest - mid.astype(jnp.float32)).astype(jnp.bfloat16)
    return high, mid, low


def norm_parts(values):
    centred = values - jnp.mean(values, -1, keepdims=True)
    inv_std = lax.rsqrt(jnp.mean(centred * centred, -1, keepdims=True) + EPS)
    return centred * inv_std, inv_std


def noise_rows(noise):
    few = noise.shape[0] // 2
    return [
        jnp.concatenate([noise[r * few + i, h : h + 1, :] for i in range(few) for h in range(2)], 1)
        for r in range(2)
    ]


def head_kernel(tokens, gain, noise, other_noise, first, second, summary, own_noise):
    f32, bf16 = jnp.float32, jnp.bfloat16
    rows = tokens.shape[0]
    half = rows // 2
    core = lax.axis_index("head") % 2
    normed, _ = norm_parts(tokens[...].astype(f32))
    h = normed * gain[...].astype(f32)
    low = h.astype(bf16)
    means = jnp.mean(h.reshape(rows // BLOCK, BLOCK, D), axis=1)
    summary[...] = means
    mine = jnp.concatenate(noise_rows(noise), 0)
    other = jnp.concatenate(noise_rows(other_noise), 0)
    own_noise[...] = mine
    both = jnp.where(
        core == 0, jnp.concatenate([mine, other], 0), jnp.concatenate([other, mine], 0)
    )
    few = means.shape[0] // 2
    for k, ref in enumerate((first, second)):
        ref[:half, :] = low[k * half : (k + 1) * half, :]
        parts = [p.astype(f32) for p in three_parts(means[k * few : (k + 1) * few, :])]
        parts += [p.astype(f32) for p in three_parts(both)] if k else [jnp.zeros((12, D), f32)]
        parts.append(jnp.zeros((EXTRA - 24, D), f32))
        ref[half:, :] = jnp.concatenate(parts, 0).astype(bf16)


def project_rows(rows, joint):
    return dot_nn(rows, joint[:, : 6 * DH]).astype(jnp.bfloat16)


def project_own_kernel(h_first, h_second, weight, w_sort, w_out, down, out, joint, first, second):
    width = w_out.shape[0]
    more = first.shape[0] - width
    first[:width, :] = w_out[...]
    first[width:, :] = down[:more, :]
    second[...] = down[more:, :]
    joint[...] = jnp.concatenate([weight[i] for i in range(3)] + [w_sort[...]], 1)
    project_half(h_first, joint, out, 0)
    project_half(h_second, joint, out, h_first.shape[0] - EXTRA)


def project_half(piece, joint, out, to):
    for start in range(0, piece.shape[0] - EXTRA, 2 * BLOCK):
        rows = project_rows(piece[start : start + 2 * BLOCK, :], joint)
        out[to + start : to + start + 2 * BLOCK, :] = rows


def project_kernel(mine1, mine2, other1, other2, joint, out, extra):
    half = mine1.shape[0] - EXTRA
    for k, piece in enumerate((mine1, mine2, other1, other2)):
        project_half(piece, joint, out, k * half)
        extra[k * EXTRA : (k + 1) * EXTRA, :] = piece[half:, :]


def half_kernel(first, second, w_out, w_out_y, half, pair):
    width = w_out.shape[0]
    even = lax.axis_index("head") % 2 == 0
    half[...] = jnp.where(even, first[...], second[...])
    pair[:width, :] = w_out[...]
    pair[width:, :] = w_out_y[:width, :]


def owners_of(step):
    place = place_of(lax.axis_index("blk"))
    core = lax.axis_index("head") % 2
    way = jnp.where(core == 0, 8 - step, step)
    return ring_of((place + way) % 8), ring_of((place + 8 - way) % 8)


def ring_of(position):
    return jnp.where(position < 4, 2 * position, 2 * (7 - position) + 1)


def place_of(index):
    return jnp.where(index % 2 == 0, index // 2, 7 - index // 2)


def far_near(table, at, lanes):
    return table[pl.ds(pl.multiple_of(at * BLOCK, BLOCK), BLOCK), lanes]


def block_operands(qkv, block, first, second, near):
    k_lanes, v_lanes = slice(2 * DH, 4 * DH), slice(4 * DH, 6 * DH)
    query = far_near(qkv, block, slice(0, 2 * DH))
    keys, values = [], []
    for lanes, store in ((k_lanes, keys), (v_lanes, values)):
        own0, own1 = mask_pair(far_near(qkv, block, lanes), near)
        far0, _ = mask_pair(far_near(qkv, first, lanes), near)
        _, far1 = mask_pair(far_near(qkv, second, lanes), near)
        store.extend([own0, far0, own1, far1])
    return query, keys, values


def block_probs(scores):
    probs = []
    for h in range(2):
        part = scores[:, h * 2 * DH : (h + 1) * 2 * DH]
        expo = jnp.exp(part - jnp.max(part, -1, keepdims=True))
        probs.append(expo / jnp.sum(expo, -1, keepdims=True))
    return probs


def choices(partner, h):
    nb = partner.shape[1]
    sides = lax.broadcasted_iota(jnp.int32, (nb, nb), 0)
    hot = (sides == partner[h : h + 1, :]).astype(jnp.bfloat16)
    same = sides == lax.broadcasted_iota(jnp.int32, (nb, nb), 1)
    return dot_nt(same.astype(jnp.bfloat16), hot)


def joined(rows, at, count):
    parts = [rows[at + k * count : at + (k + 1) * count, :].astype(jnp.float32) for k in range(3)]
    return (parts[0] + parts[1]) + parts[2]


def attend_kernel(
    own, step1, step2, step3, extra1, extra2, extra3, mine4, other4, joint, own_summary, own_noise,
    partner, partner_rows, qkv, context, summary, steps, scale_rows, weight_rows, noise,
):
    f32, bf16 = jnp.float32, jnp.bfloat16
    me = lax.axis_index("blk")
    core = lax.axis_index("head") % 2
    nb = partner_rows.shape[1]
    rows = own.shape[0]
    half = rows // 2
    blocks = rows // BLOCK
    few = blocks // 2

    def put(owner, start, values):
        n = values.shape[0]
        qkv[pl.ds(pl.multiple_of(owner * rows + start, n), n), :] = values

    def put_noise(owner, values):
        lines = [
            values[r : r + 1, i * 2 * nb : (i + 1) * 2 * nb] for r in range(2) for i in range(few)
        ]
        at = pl.multiple_of(owner * blocks, blocks)
        noise[pl.ds(at, blocks), :] = jnp.concatenate(lines, 0)

    def put_extra(owner, first, second):
        at = pl.multiple_of(owner * blocks, blocks)
        summary[pl.ds(at, blocks), :] = jnp.concatenate(
            [joined(first, 0, few), joined(second, 0, few)], 0
        )
        both = joined(second, 3 * few, 4)
        put_noise(owner, jnp.where(core == 0, both[:2], both[2:]))

    put(me, 0, own[...])
    summary[pl.ds(pl.multiple_of(me * blocks, blocks), blocks), :] = own_summary[...]
    put_noise(me, own_noise[...])
    for step, ref, extra in ((1, step1, extra1), (2, step2, extra2), (3, step3, extra3)):
        for k, owner in enumerate(owners_of(step)):
            put(owner, 0, ref[k * rows : (k + 1) * rows, :])
            at = 2 * k * EXTRA
            put_extra(owner, extra[at : at + EXTRA, :], extra[at + EXTRA : at + 2 * EXTRA, :])
    owner, _ = owners_of(4)
    for side, ref in ((core, mine4), (1 - core, other4)):
        for start in range(0, half, 2 * BLOCK):
            values = project_rows(ref[start : start + 2 * BLOCK, :], joint)
            put(owner, side * half + start, values)
    ends = [ref[half:, :].astype(f32) for ref in (mine4, other4)]
    put_extra(
        owner, jnp.where(core == 0, ends[0], ends[1]), jnp.where(core == 0, ends[1], ends[0])
    )

    parts = three_parts(summary[...])
    logits = sum(dot_nn(part, joint[:, 6 * DH :]) for part in parts[::-1])
    logits = (logits + noise[...]) / TEMPER
    plan = jnp.stack([logits[:, :nb], logits[:, nb:]])
    for sweep in range(SINK):
        for k, axis in enumerate((2, 1)):
            plan = plan - log_total(plan, axis)
            steps[2 * sweep + k] = jnp.exp(plan)
    final = jnp.exp(plan)
    picked = []
    for h in range(2):
        picked.append(nb * jnp.sum(choices(partner_rows, h) * final[h], axis=1, keepdims=True))
    ones = jnp.ones((nb, DH), f32)
    scale_rows[...] = jnp.concatenate([ones, picked[0] * ones, ones, picked[1] * ones], 1)
    weight_rows[...] = jnp.concatenate([picked[0] * ones, picked[1] * ones], 1)

    near = first_lanes()
    work = []
    for i in range(blocks):
        block = me * blocks + i
        query, keys, values = block_operands(
            qkv, block, partner[0, block], partner[1, block], near
        )
        none = jnp.zeros_like(values[0])
        table = jnp.concatenate(
            [
                jnp.concatenate([values[0], none, values[2], none], 0),
                jnp.concatenate([none, values[1], none, values[3]], 0),
            ],
            1,
        )
        z = dot_nt(query, jnp.concatenate(keys, 0)) * (DH**-0.5)
        work.append((block, z, table))
    probs = [block_probs(z * scale_rows[pl.ds(block, 1), :]) for block, z, _ in work]
    outs = [
        dot_nn(jnp.concatenate([p.astype(bf16) for p in prob], 1), table)
        for prob, (_, _, table) in zip(probs, work)
    ]
    for i, (out, (block, _, _)) in enumerate(zip(outs, work)):
        ctx = out[:, : 2 * DH] + weight_rows[pl.ds(block, 1), :] * out[:, 2 * DH :]
        context[i * BLOCK : (i + 1) * BLOCK, :] = ctx.astype(bf16)


def feed_kernel(
    tokens, cotangent, gain, ctx0, ctx1, ctx2, ctx3, wo, wo_other, up_a, up_b, down_a, first, second,
    middle, h_two, active, d_hidden, ffn, d_h_two,
    ctx_full, wo_full, up_full, down_full, act_full, d_full,
):
    f32, bf16 = jnp.float32, jnp.bfloat16
    hd = lax.axis_index("head")
    row = hd // 2
    width = ctx0.shape[1]
    ff = up_a.shape[1]
    for j, c in enumerate((ctx0, ctx1, ctx2, ctx3)):
        at = pl.multiple_of((hd ^ j) * width, width)
        ctx_full[:, pl.ds(at, width)] = c[...]
        w = wo if j % 2 == 0 else wo_other
        wo_full[pl.ds(at, width), :] = w[j // 2 * width : (j // 2 + 1) * width, :]
    here, there = (pl.multiple_of((row ^ j) * ff, ff) for j in range(2))
    up_full[:, pl.ds(here, ff)] = up_a[...]
    up_full[:, pl.ds(there, ff)] = up_b[...]
    down_full[pl.ds(here, ff), :] = down_a[...]
    more = first.shape[0] - width
    down_full[pl.ds(there, more), :] = first[width:, :]
    down_full[pl.ds(pl.multiple_of(there + more, 32), ff - more), :] = second[...]
    chunk = 256
    for start in range(0, tokens.shape[0], chunk):
        sl = slice(start, start + chunk)
        mid = tokens[sl, :].astype(f32) + dot_nn(ctx_full[sl, :], wo_full[...])
        middle[sl, :] = mid
        normed, _ = norm_parts(mid)
        low = (normed * gain[...].astype(f32)).astype(bf16)
        h_two[sl, :] = low
        ffn_sum = None
        back_sum = None
        for j in range(2):
            cols = slice(j * ff, (j + 1) * ff)
            pre = dot_nn(low, up_full[:, cols])
            d_act = dot_nt(cotangent[sl, :], down_full[cols, :])
            bell = 0.5 * (1.0 + lax.erf(pre * ROOT_HALF))
            act = (pre * bell).astype(bf16)
            slope = bell + pre * jnp.exp(-0.5 * pre * pre) * INV_ROOT_TWO_PI
            d_pre = (d_act * slope).astype(bf16)
            act_full[sl, cols] = act
            d_full[sl, cols] = d_pre
            f = dot_nn(act, down_full[cols, :])
            b = dot_nt(d_pre, up_full[:, cols])
            ffn_sum = f if ffn_sum is None else ffn_sum + f
            back_sum = b if back_sum is None else back_sum + b
        ffn[sl, :] = ffn_sum
        d_h_two[sl, :] = back_sum
    mine = pl.ds(pl.multiple_of(row * ff, ff), ff)
    active[...] = act_full[:, mine]
    d_hidden[...] = d_full[:, mine]


def back_kernel(middle, own, other, cotangent, gain, w_out, d_middle, d_low, d_ctx, g_gain):
    f32, bf16 = jnp.float32, jnp.bfloat16
    normed, inv = norm_parts(middle[...])
    d_h = own[...] + other[...]
    g_gain[...] = jnp.broadcast_to(jnp.sum(d_h * normed, 0, keepdims=True), g_gain.shape)
    d_mid = cotangent[...].astype(f32) + norm_back(d_h, normed, inv, gain[...].astype(f32))
    d_middle[...] = d_mid
    low = d_mid.astype(bf16)
    d_low[...] = low
    d_ctx[...] = dot_nt(low, w_out[...]).astype(bf16)


def grads_kernel(h_two, d_hidden, active, cotangent, context, d_low, *refs):
    keeps, (front, back), (up, down, out) = refs[:7], refs[7:9], refs[9:]
    place = place_of(lax.axis_index("blk"))
    up[...] = dot_tn(h_two[...], d_hidden[...])
    down[...] = dot_tn(active[...], cotangent[...])
    out[...] = dot_tn(context[...], d_low[...])

    def rows_of(distance):
        owner = ring_of((place + distance + 8) % 8)
        parts = []
        for ref in (up, down, out):
            n = ref.shape[0] // 8
            parts.append(ref[pl.ds(pl.multiple_of(owner * n, n), n), :])
        return jnp.concatenate(parts, 0)

    for ref, distance in zip(keeps, (3, 2, 1, -3, -2, -1, 0)):
        ref[...] = rows_of(distance)
    last = rows_of(4).astype(jnp.bfloat16)
    n = front.shape[0]
    front[...] = last[:n]
    back[...] = last[n:]


def relay_kernel(keep_f, keep_b, f, b, out_f, out_b):
    f32 = jnp.float32
    n, m, size = f.shape[0], b.shape[0], keep_f.shape[0]
    out_f[...] = keep_f[...].astype(jnp.bfloat16)
    out_b[...] = keep_b[...].astype(jnp.bfloat16)
    out_f[:n, :] = (keep_f[:n, :] + f[...].astype(f32)).astype(jnp.bfloat16)
    out_b[size - m :, :] = (keep_b[size - m :, :] + b[...].astype(f32)).astype(jnp.bfloat16)


def total_kernel(keep, f, b, out):
    f32 = jnp.float32
    out[...] = (keep[...] + (f[...].astype(f32) + b[...].astype(f32))).astype(jnp.bfloat16)


def cut_kernel(f, b, front, back):
    front[...] = f[: front.shape[0], :]
    back[...] = b[b.shape[0] - back.shape[0] :, :]


def lay_kernel(own, f1, b1, f2, b2, f3, b3, f4, b4, g_up, g_down, g_out):
    f32 = jnp.float32
    place = place_of(lax.axis_index("blk"))
    last = jnp.concatenate([f4[...], b4[...]], 0)
    for distance, piece in (
        (0, own[...]), (-1, f1[...]), (1, b1[...]), (-2, f2[...]), (2, b2[...]), (-3, f3[...]), (3, b3[...]),
        (4, last),
    ):
        owner = ring_of((place + distance + 8) % 8)
        start = 0
        for ref in (g_up, g_down, g_out):
            n = ref.shape[0] // 8
            ref[pl.ds(pl.multiple_of(owner * n, n), n), :] = piece[start : start + n].astype(f32)
            start += n


def halve_kernel(f, b, front, back):
    n = front.shape[0]
    front[...] = f[:n, :]
    back[...] = b[n:, :]


def add_kernel(*refs):
    *terms, out = refs
    total = terms[0][...]
    for term in terms[1:]:
        total = total + term[...]
    out[...] = total


def four_kernel(here, one, two, three, out):
    out[...] = (here[...] + one[...]) + (two[...] + three[...])


def gains_kernel(here, other, first, second):
    total = here[...] + other[...]
    first[...] = total[0, :]
    second[...] = total[8, :]


def block_at(place, step, start, i):
    return ring_of((place + 8 - step) % 8) * (SHARD // BLOCK) + start // BLOCK + i


def prepare_kernel(pieces, qkv, partner, scale_rows, z_out, probs_out):
    place = place_of(lax.axis_index("blk"))
    near = first_lanes()
    blocks = [(step, start, i) for step, start, n in pieces for i in range(n // BLOCK)]
    for first in range(0, len(blocks), 8):
        work = []
        for step, start, i in blocks[first : first + 8]:
            block = block_at(place, step, start, i)
            query, keys, _ = block_operands(qkv, block, partner[0, block], partner[1, block], near)
            work.append((query, jnp.concatenate(keys, 0), scale_rows[pl.ds(block, 1), :]))
        z = [dot_nt(query, keys) * (DH**-0.5) for query, keys, _ in work]
        probs = [block_probs(v * w[2]) for v, w in zip(z, work)]
        for k in range(len(work)):
            at = slice((first + k) * BLOCK, (first + k + 1) * BLOCK)
            z_out[at, :] = z[k]
            probs_out[at, :] = jnp.concatenate(probs[k], 1)


def pull_kernel(pieces, offset, *refs):
    f32, bf16 = jnp.float32, jnp.bfloat16
    count = len(pieces)
    outs, refs = refs[:count], refs[count:]
    qkv, partner, scale_rows, weight_rows, refs = *refs[:4], refs[4:]
    if offset is not None:
        z_all, probs_all, refs = refs[0], refs[1], refs[2:]
    near_out, low_out, d_weight = refs
    place = place_of(lax.axis_index("blk"))
    near = first_lanes()
    scale = DH**-0.5
    blocks = [
        (step, start, d_ctx, i)
        for (step, start), d_ctx in zip(pieces, outs)
        for i in range(d_ctx.shape[0] // BLOCK)
    ]
    for first in range(0, len(blocks), 8):
        work = []
        for k, (step, start, d_ctx, i) in enumerate(blocks[first : first + 8]):
            block = block_at(place, step, start, i)
            query, keys, values = block_operands(
                qkv, block, partner[0, block], partner[1, block], near
            )
            w = dict(
                query=query,
                keys=jnp.concatenate(keys, 0),
                values=jnp.concatenate(values, 0),
                scale=scale_rows[pl.ds(block, 1), :],
                weight=weight_rows[pl.ds(block, 1), :],
                d_out=d_ctx[i * BLOCK : (i + 1) * BLOCK, :],
            )
            if offset is not None:
                at = slice((offset + first + k) * BLOCK, (offset + first + k + 1) * BLOCK)
                w["z"] = z_all[at, :]
                w["probs"] = [probs_all[at, : 2 * DH], probs_all[at, 2 * DH :]]
            work.append(w)
        if offset is None:
            for w in work:
                w["z"] = dot_nt(w["query"], w["keys"]) * scale
        for w in work:
            w["raw"] = dot_nt(w["d_out"], w["values"])
        if offset is None:
            for w in work:
                w["probs"] = block_probs(w["z"] * w["scale"])
        for w in work:
            d_z, low, d_w = [], [], []
            for h in range(2):
                sl = slice(h * 2 * DH, (h + 1) * 2 * DH)
                probs = w["probs"][h]
                d_probs = w["raw"][:, sl] * w["scale"][:, sl]
                d_scores = probs * (d_probs - jnp.sum(d_probs * probs, -1, keepdims=True))
                d_z.append((d_scores * w["scale"][:, sl]).astype(bf16))
                low.append(probs.astype(bf16))
                d_w.append(
                    jnp.sum(
                        d_scores * w["z"][:, sl] + low[h].astype(f32) * w["raw"][:, sl],
                        0,
                        keepdims=True,
                    )
                )
            w["d_z"], w["low"] = jnp.concatenate(d_z, 1), jnp.concatenate(low, 1)
            w["d_w"] = jnp.concatenate(d_w, 1)
        for w in work:
            w["d_query"] = dot_nn(w["d_z"], w["keys"]) * scale
        for w in work:
            w["d_keys"] = dot_tn(w["d_z"], w["query"]) * scale
        for w in work:
            w["d_values"] = dot_tn(w["low"], w["d_out"])
        for k, w in enumerate(work):
            to = first + k
            at = slice(to * BLOCK, (to + 1) * BLOCK)
            d_weight[to : to + 1, :] = w["d_w"]
            low_out[at, : 2 * DH] = w["d_query"].astype(bf16)
            for m, name in enumerate(("d_keys", "d_values")):
                parts = [w[name][i * BLOCK : (i + 1) * BLOCK, :] for i in range(4)]
                near_out[at, m * 2 * DH : (m + 1) * 2 * DH] = jnp.where(near, parts[0], parts[2])
                far = jnp.where(near, parts[1], parts[3])
                if m == 1:
                    far = far * w["weight"]
                low_out[at, (m + 1) * 2 * DH : (m + 2) * 2 * DH] = far.astype(bf16)


def collect_kernel(pieces, *refs):
    f32, bf16 = jnp.float32, jnp.bfloat16
    count = len(pieces)
    nears, lows, d_weights = refs[:count], refs[count : 2 * count], refs[2 * count : 3 * count]
    partner, partner_rows, steps, summary = refs[3 * count : 3 * count + 4]
    d_qkv, d_mine, flat_mine, g_sort, d_weight, acc, far, d_flat = refs[3 * count + 4 :]
    me = lax.axis_index("blk")
    place = place_of(me)
    for parts, near_ref, low_ref, w_ref in zip(pieces, nears, lows, d_weights):
        at = 0
        for step, start, n in parts:
            owner = ring_of((place + 8 - step) % 8)
            to = pl.ds(pl.multiple_of(owner * SHARD + start, n), n)
            acc[to, :] = near_ref[at : at + n, :]
            far[to, :] = low_ref[at : at + n, 2 * DH :]
            d_qkv[to, : 2 * DH] = low_ref[at : at + n, : 2 * DH]
            if start == 0:
                nb = SHARD // BLOCK
                first = pl.multiple_of(owner * nb, nb)
                d_weight[pl.ds(first, nb), :] = w_ref[at // BLOCK : at // BLOCK + nb, :]
            at += n
    near = first_lanes()
    both = jnp.concatenate([near, near], 1)

    def body(block, _):
        tile = far[pl.ds(pl.multiple_of(block * BLOCK, BLOCK), BLOCK), :].astype(f32)
        for h, kept in ((0, jnp.where(both, tile, 0.0)), (1, jnp.where(both, 0.0, tile))):
            to = pl.ds(pl.multiple_of(partner[h, block] * BLOCK, BLOCK), BLOCK)
            acc[to, :] += kept
        return 0

    lax.fori_loop(0, partner.shape[1], body, 0, unroll=4)
    d_qkv[:, 2 * DH :] = acc[...].astype(bf16)
    d_mine[...] = d_qkv[pl.ds(pl.multiple_of(me * SHARD, SHARD), SHARD), :]
    d_flat[...] = sink_back(d_weight[...], steps, partner_rows)
    n = flat_mine.shape[0]
    flat_mine[...] = d_flat[pl.ds(pl.multiple_of(me * n, n), n), :]
    g_sort[...] = lax.dot_general(
        summary[...],
        d_flat[...],
        (((0,), (0,)), ((), ())),
        precision=HIGHEST,
        preferred_element_type=f32,
    )


def sink_back(d_weight, steps, partner):
    nb = partner.shape[1]
    grads = []
    for h in range(2):
        total = jnp.sum(
            d_weight[:, (2 * h + 1) * DH : (2 * h + 2) * DH], axis=1, keepdims=True
        )
        grads.append(choices(partner, h) * (nb * total))
    last = steps.shape[0] - 1
    grad = jnp.stack(grads) * steps[last]
    for t in range(last, -1, -1):
        grad = grad - steps[t] * jnp.sum(grad, axis=1 if t % 2 else 2, keepdims=True)
    return jnp.concatenate([grad[0], grad[1]], 1) / TEMPER


def weight_kernel(*refs):
    *halves, d_qkv, g_qkv, h_all = refs
    me = lax.axis_index("blk")
    core = lax.axis_index("head") % 2
    half = halves[0].shape[0] - EXTRA
    rows = 2 * half

    def put(owner, side, ref):
        at = pl.ds(pl.multiple_of(owner * rows + side * half, half), half)
        h_all[at, :] = ref[:half, :]

    owners = [me] + [owner for step in (1, 2, 3) for owner in owners_of(step)]
    for k, owner in enumerate(owners):
        put(owner, 0, halves[2 * k])
        put(owner, 1, halves[2 * k + 1])
    owner, _ = owners_of(4)
    put(owner, core, halves[14])
    put(owner, 1 - core, halves[15])
    out = dot_tn(h_all[...], d_qkv[...])
    width = g_qkv.shape[2]
    for i in range(3):
        g_qkv[i] = out[:, i * width : (i + 1) * width]


def input_kernel(dq_a, dq_b, joint_a, joint_b, flat_a, flat_b, d_h, dq_full, w_full, flat_full, sort_full):
    row = lax.axis_index("head") // 2
    width, nb = dq_a.shape[1], flat_a.shape[1]
    sides = ((dq_a, joint_a, flat_a), (dq_b, joint_b, flat_b))
    for j, (g, joint, flat) in enumerate(sides):
        at = pl.multiple_of((row ^ j) * width, width)
        dq_full[:, pl.ds(at, width)] = g[...]
        w_full[:, pl.ds(at, width)] = joint[:, :width]
        at = pl.multiple_of((row ^ j) * nb, nb)
        flat_full[:, pl.ds(at, nb)] = flat[...]
        sort_full[:, pl.ds(at, nb)] = joint[:, width:]
    part = dot_nt(dq_full[...], w_full[...])
    d_sum = sum(dot_nt(p, sort_full[...]) for p in three_parts(flat_full[...])[::-1]) / BLOCK
    blocks = d_sum.shape[0]
    for i in range(blocks):
        sl = slice(i * BLOCK, (i + 1) * BLOCK)
        d_h[sl, :] = part[sl, :] + d_sum[i : i + 1, :]


def gain_kernel(tokens, d_mine, flat_mine, joint, g_two, out):
    width = d_mine.shape[1]
    normed, _ = norm_parts(tokens[...].astype(jnp.float32))
    part = dot_nt(d_mine[...], joint[:, :width])
    d_sum = sum(dot_nt(p, joint[:, width:]) for p in three_parts(flat_mine[...])[::-1]) / BLOCK
    blocks = d_sum.shape[0]
    sums = jnp.sum(part * normed, 0, keepdims=True)
    means = jnp.sum(normed.reshape(blocks, BLOCK, D), 1)
    sums = sums + jnp.sum(d_sum * means, 0, keepdims=True)
    out[:8, :] = jnp.broadcast_to(sums, g_two.shape)
    out[8:, :] = jnp.where(lax.axis_index("head") == 0, g_two[...], 0.0)


def end_kernel(tokens, gain, own, other, d_middle, d_tokens):
    f32 = jnp.float32
    normed, inv = norm_parts(tokens[...].astype(f32))
    d_h = own[...] + other[...]
    d_tokens[...] = d_middle[...] + norm_back(d_h, normed, inv, gain[...].astype(f32))


VMEM_SPEC = pl.BlockSpec(memory_space=pltpu.VMEM)
SMEM_SPEC = pl.BlockSpec(memory_space=pltpu.SMEM)
ANY_SPEC = pl.BlockSpec(memory_space=pltpu.HBM)


def fetch(pairs, sems, first=0):
    copies = []
    for k, (source, target) in enumerate(pairs):
        copies.append(pltpu.make_async_copy(source, target, sems.at[first + k]))
        copies[-1].start()
    return copies


def wait_all(copies):
    for copy in copies:
        copy.wait()


def call(kernel, outs, *args, scratch=(), smem=(), cold=(), raw=(), out_cold=(), limit=16, name=None):
    cost = int(1e3 * TIMES[name])
    shapes = [jax.ShapeDtypeStruct(s, d) for s, d in outs]
    specs = [
        SMEM_SPEC if i in smem else ANY_SPEC if i in cold or i in raw else VMEM_SPEC
        for i in range(len(args))
    ]
    out_specs = [ANY_SPEC if i in out_cold else VMEM_SPEC for i in range(len(outs))]
    buffers = [pltpu.VMEM(args[i].shape, args[i].dtype) for i in cold]
    buffers += [pltpu.VMEM(*outs[i]) for i in out_cold]
    sem_count = len(cold) + len(out_cold)
    sems = [pltpu.SemaphoreType.DMA((sem_count,))] if sem_count else []
    own = [pltpu.SemaphoreType.DMA((40,))] if raw else []

    def body(*refs):
        refs = list(refs)
        ins, results = refs[: len(args)], refs[len(args) : len(args) + len(outs)]
        rest = refs[len(args) + len(outs) :]
        mine, rest = rest[: len(scratch)], rest[len(scratch) :]
        room, rest = rest[: len(buffers)], rest[len(buffers) :]
        copies = []
        if cold:
            copies = fetch([(ins[i], room[k]) for k, i in enumerate(cold)], rest[0])
            for k, i in enumerate(cold):
                ins[i] = room[k]
        targets = list(results)
        for k, i in enumerate(out_cold):
            results[i] = room[len(cold) + k]
        wait_all(copies)
        kernel(*ins, *results, *mine, *(rest[-1:] if raw else []))
        if out_cold:
            wait_all(fetch([(results[i], targets[i]) for i in out_cold], rest[0], len(cold)))

    result = pl.pallas_call(
        body,
        out_shape=shapes,
        in_specs=specs,
        out_specs=out_specs,
        scratch_shapes=[pltpu.VMEM(s, d) for s, d in scratch] + buffers + sems + own,
        compiler_params=pltpu.CompilerParams(vmem_limit_bytes=limit * 1024 * 1024),
        cost_estimate=pl.CostEstimate(
            flops=cost * FLOPS, bytes_accessed=cost * BYTES, transcendentals=0
        ),
        name=name,
    )(*args)
    return result[0] if len(shapes) == 1 else result


TIMES = {
    "norm_one": 1.7,
    "project_own": 0.45,
    "project": 0.7,
    "attend": 4.2,
    "prepare": 2.9,
    "feed": 4.2,
    "back": 1.2,
    "pull": 2.4,
    "grads": 0.95,
    "relay": 0.2,
    "collect": 4.5,
    "sinkhorn_back": 2.05,
    "total": 0.25,
    "input_back": 1.0,
    "gain_part": 0.8,
    "weights": 3.6,
    "norm_one_back": 1.7,
    "output": 1.1,
    "lay": 1.6,
    "gains": 0.6,
    "halve": 0.1,
    "half": 0.1,
    "pair": 0.1,
    "add_gains": 0.1,
    "sum_gains": 0.1,
}
FLOPS, BYTES = 1150000, 3690


def tie(*values):
    return lax.optimization_barrier(values)


def after(value, *others):
    return lax.optimization_barrier((value,) + others)[0]


RING = (0, 2, 4, 6, 7, 5, 3, 1)
SHARD = 512
EXTRA = 32
CUT = 320


def local_eight(
    tokens, gain_attn, gain_ffn, w_qkv, w_out, w_sort, w_up, w_down, gumbel_noise, partner, cotangent
):
    f32, bf16 = jnp.float32, jnp.bfloat16
    rows = tokens.shape[0]
    blocks = rows // BLOCK
    width = w_out.shape[0]
    ff = w_up.shape[1]
    nb = partner.shape[0]
    total = nb * BLOCK
    half, quarter = rows // 2, rows // 4
    core = lax.axis_index("head") % 2

    def ahead(v):
        return lax.ppermute(v, "blk", [(RING[i], RING[(i + 1) % 8]) for i in range(8)])

    def behind(v):
        return lax.ppermute(v, "blk", [(RING[i], RING[(i - 1) % 8]) for i in range(8)])

    def swap_head(v, j):
        return lax.ppermute(v, "head", [(i, i ^ j) for i in range(4)])

    def swap_blk(v, j):
        return lax.ppermute(v, "blk", [(i, i ^ j) for i in range(8)])

    w_in = w_qkv.transpose(1, 0, 2)
    partner_s = partner.T

    def along(v):
        pairs = []
        for i in range(8):
            for h in range(4):
                to = RING[(i + 1) % 8] if h % 2 == 0 else RING[(i - 1) % 8]
                pairs.append((RING[i] * 4 + h, to * 4 + h))
        return lax.ppermute(v, ("blk", "head"), pairs)

    a, b, own_summary, own_noise = call(
        head_kernel,
        [((half + EXTRA, D), bf16)] * 2 + [((blocks, D), f32), ((2, D), f32)],
        tokens, gain_attn, gumbel_noise, swap_head(gumbel_noise, 1),
        cold=(0, 1, 2, 3), limit=62, name="norm_one",
    )

    mine = [(a, b)]
    up_y = swap_head(after(w_up, a), 2)
    a, b = along(a), along(b)
    qkv_own, joint, first, second = call(
        project_own_kernel,
        [
            ((rows, 3 * width), bf16), ((D, 3 * width + 2 * nb), bf16), ((CUT, D), bf16),
            ((width + ff - CUT, D), bf16),
        ],
        *mine[0], w_in, w_sort, w_out, w_down, name="project_own",
    )
    mine.append((a, b))
    a, b = along(a), along(b)
    b, up_y, qkv_own = tie(b, up_y, qkv_own)
    mine.append((a, b))
    first_y = swap_head(after(first, a), 2)
    a, b = along(a), along(b)
    b, first_y = tie(b, first_y)
    mine.append((a, b))
    second_y = swap_head(after(second, a), 2)
    half_3, wo = call(
        half_kernel, [((half + EXTRA, D), bf16), ((2 * width, D), bf16)], a, b, w_out, first_y, name="half"
    )
    m4 = along(half_3)
    other, projected = [], []
    for k in (1, 2, 3):
        other.append(tuple(swap_head(after(v, mine[min(k + 1, 3)][0]), 1) for v in mine[k]))
        projected.append(
            call(
                project_kernel, [((2 * rows, 3 * width), bf16), ((4 * EXTRA, D), bf16)],
                *mine[k], *other[-1], joint, name="project",
            )
        )
    m4, second_y = tie(m4, second_y, *[p[0] for p in projected])[:2]
    o4 = swap_head(m4, 1)
    qkv, context, summary, steps, scale_rows, weight_rows = call(
        attend_kernel,
        [
            ((total, 3 * width), bf16), ((rows, width), bf16), ((nb, D), f32),
            ((2 * SINK, 2, nb, nb), f32), ((nb, 4 * DH), f32), ((nb, 2 * DH), f32),
        ],
        qkv_own, *[p[0] for p in projected], *[p[1] for p in projected], m4, o4, joint, own_summary, own_noise,
        partner_s, partner_s, smem=(12,), scratch=[((nb, 2 * nb), f32)], name="attend",
    )
    ctx_y, ctx_c = swap_head(context, 2), swap_head(context, 1)
    wo_other = swap_head(after(wo, context), 1)
    prepared = ((3, 0, rows), (-3, 0, rows), (4, 0, rows))
    amount = sum(n for _, _, n in prepared)
    z_all, probs_all = call(
        functools.partial(prepare_kernel, prepared), [((amount, 4 * DH), f32)] * 2,
        qkv, partner_s, scale_rows, smem=(1,), name="prepare",
    )
    ctx_y, ctx_c, z_all = tie(ctx_y, ctx_c, z_all)
    ctx_yc = swap_head(ctx_y, 1)
    middle, h_two, active, d_hidden, ffn, d_h_two = call(
        feed_kernel,
        [
            ((rows, D), f32),
            ((rows, D), bf16),
            ((rows, ff), bf16),
            ((rows, ff), bf16),
            ((rows, D), f32),
            ((rows, D), f32),
        ],
        tokens, cotangent, gain_ffn, context, ctx_c, ctx_y, ctx_yc, wo, wo_other,
        w_up, up_y, w_down, first_y, second_y,
        scratch=[
            ((rows, 4 * width), bf16), ((4 * width, D), bf16), ((D, 2 * ff), bf16), ((2 * ff, D), bf16),
            ((rows, 2 * ff), bf16), ((rows, 2 * ff), bf16),
        ],
        name="feed",
    )
    d_h_two_other = swap_head(d_h_two, 1)
    d_middle, d_low, d_ctx, g_two = call(
        back_kernel,
        [((rows, D), f32), ((rows, D), bf16), ((rows, width), bf16), ((8, D), f32)],
        middle, d_h_two, d_h_two_other, cotangent, gain_ffn, w_out, name="back",
    )

    plans = [[(0, 0)]] + [[(k, 0), (-k, 0)] for k in (1, 2, 3)] + [[(4, 0), (4, half)]]
    offsets = (None, None, None, 0, 2 * blocks)
    pulled = []

    def pull(given):
        plan, offset = plans[len(pulled)], offsets[len(pulled)]
        n = sum(a.shape[0] for a in given)
        pulled.append(
            call(
                functools.partial(pull_kernel, tuple(plan), offset),
                [((n, 4 * DH), f32), ((n, 6 * DH), bf16), ((n // BLOCK, 4 * DH), f32)],
                *given, qkv, partner_s, scale_rows, weight_rows,
                *([] if offset is None else [z_all, probs_all]),
                smem=(len(given) + 1,), name="pull",
            )
        )
        return pulled[-1][0]

    piece = (D + ff + width) // 8
    front = 80
    parts = call(
        grads_kernel,
        [((piece, D), f32)] * 7 + [((front, D), bf16), ((piece - front, D), bf16)],
        h_two, d_hidden, active, cotangent, context, d_low,
        scratch=[((D, ff), f32), ((ff, D), f32), ((width, D), f32)], name="grads",
    )
    keeps, (sum_f, sum_b) = parts[:7], parts[7:]
    given = [d_ctx]
    arrays = [given]
    d_ctx, sum_f, sum_b = tie(d_ctx, sum_f, sum_b)
    f = b = d_ctx
    joint_y = swap_head(after(joint, sum_f), 2)
    for step in range(4):
        if step == 3:
            f, b = call(halve_kernel, [((half, width), bf16)] * 2, f, b, name="halve")
        f, b = ahead(f), behind(b)
        sum_f, sum_b = ahead(sum_f), behind(sum_b)
        done = pull(given)
        hold = [joint_y] if step == 2 else []
        sum_f, sum_b = tie(sum_f, sum_b, done, *hold)[:2]
        given = [f, b]
        arrays.append(given)
        if step < 3:
            sum_f, sum_b = call(
                relay_kernel, [((piece, D), bf16)] * 2, keeps[step], keeps[step + 3], sum_f, sum_b,
                name="relay",
            )
    owned = call(total_kernel, [((piece, D), bf16)], keeps[6], sum_f, sum_b, name="total")
    wf1, wb1 = ahead(owned), behind(owned)
    pull(given)
    spans = tuple(
        tuple((step, start, a.shape[0]) for (step, start), a in zip(plan, given))
        for plan, given in zip(plans, arrays)
    )
    d_qkv, d_mine, flat_mine, g_sort = call(
        functools.partial(collect_kernel, spans),
        [
            ((total, 3 * width), bf16), ((rows, 3 * width), bf16), ((blocks, 2 * nb), f32), ((D, 2 * nb), f32),
        ],
        *[p[k] for k in range(3) for p in pulled], partner_s, partner_s, steps, summary, smem=(15,),
        scratch=[
            ((nb, 4 * DH), f32), ((total, 4 * DH), f32), ((total, 4 * DH), bf16), ((nb, 2 * nb), f32),
        ],
        name="collect",
    )
    wf1, wb1, d_mine, flat_mine = tie(wf1, wb1, d_mine, flat_mine)
    wf2, wb2 = ahead(wf1), behind(wb1)
    d_mine_y, flat_y = swap_head(d_mine, 2), swap_head(flat_mine, 2)
    gains_a = call(
        gain_kernel, [((16, D), f32)], tokens, d_mine, flat_mine, joint, g_two, name="gain_part"
    )
    gains_x = swap_blk(gains_a, 1)
    gains = call(add_kernel, [((16, D), f32)], gains_a, gains_x, name="add_gains")
    wf2, wb2, d_mine_y, flat_y, gains = tie(wf2, wb2, d_mine_y, flat_y, gains)
    wf3, wb3 = ahead(wf2), behind(wb2)
    gains1, gains2, gains3 = swap_blk(gains, 2), swap_blk(gains, 4), swap_blk(gains, 6)
    d_h = call(
        input_kernel, [((rows, D), f32)],
        d_mine, d_mine_y, joint, joint_y, flat_mine, flat_y,
        scratch=[
            ((rows, 6 * width), bf16), ((D, 6 * width), bf16), ((blocks, 4 * nb), f32), ((D, 4 * nb), bf16),
        ],
        name="input_back",
    )
    d_h_other = swap_head(d_h, 1)
    g_qkv = call(
        weight_kernel, [((3, D, width), f32)],
        *mine[0], *[v for k in (1, 2, 3) for v in (*mine[k], *other[k - 1])], m4, o4, after(d_qkv, d_h),
        scratch=[((total, D), bf16)], limit=24, name="weights",
    )
    wf3, wb3, gains1, gains2, gains3, d_h_other, g_qkv = tie(
        wf3, wb3, gains1, gains2, gains3, d_h_other, g_qkv
    )
    cut_f, cut_b = call(
        cut_kernel, [((front, D), bf16), ((piece - front, D), bf16)], wf3, wb3, name="halve"
    )
    wf4, wb4 = ahead(cut_f), behind(cut_b)
    gains = call(four_kernel, [((16, D), f32)], gains, gains1, gains2, gains3, name="sum_gains")
    gains_y = swap_head(gains, 2)
    d_tokens = call(
        end_kernel, [((rows, D), f32)],
        tokens, gain_attn, d_h, d_h_other, d_middle, name="norm_one_back",
    )
    ffn_other = swap_head(after(ffn, wf3), 1)
    gains = call(add_kernel, [((16, D), f32)], gains, gains_y, name="add_gains")
    gains_c = swap_head(gains, 1)
    output = call(add_kernel, [((rows, D), f32)], ffn, ffn_other, middle, name="output")
    g_up, g_down, g_out = call(
        lay_kernel,
        [((D, ff), f32), ((ff, D), f32), ((width, D), f32)],
        owned, wf1, wb1, wf2, wb2, wf3, wb3, wf4, wb4, name="lay",
    )
    g_one, g_two = call(gains_kernel, [((D,), f32), ((D,), f32)], gains, gains_c, name="gains")
    return output, d_tokens, g_one, g_two, g_qkv.transpose(1, 0, 2), g_out, g_sort, g_up, g_down


def solution(mesh):
    in_specs = (
        P("blk", None),
        P(),
        P(),
        P(None, None, "head"),
        P("head", None),
        P(None, "head"),
        P(None, "head"),
        P("head", None),
        P("blk", "head", None),
        P(None, "head"),
        P("blk", None),
    )
    out_specs = (
        P("blk", None),
        P("blk", None),
        P(),
        P(),
        P(None, None, "head"),
        P("head", None),
        P(None, "head"),
        P(None, "head"),
        P("head", None),
    )
    plan = local_eight if mesh.shape["blk"] == 8 and mesh.shape["head"] == 4 else local
    return jax.shard_map(plan, mesh=mesh, in_specs=in_specs, out_specs=out_specs, check_vma=False)
```

```python
import functools
import math

import jax
import jax.numpy as jnp
from jax import lax
from jax.experimental import pallas as pl
from jax.experimental.pallas import tpu as pltpu
from jax.sharding import PartitionSpec as P

D = 512
DH = 64
BLOCK = 64
SINK = 8


EPS = 1e-05
TEMPER = 0.75
ROOT_HALF = 0.7071067811865476
INV_ROOT_TWO_PI = 0.3989422804014327
HIGHEST = lax.Precision.HIGHEST


def normalize(values, norm_gain):
    average = jnp.mean(values, -1, keepdims=True)
    centred = values - average
    inv_std = lax.rsqrt(jnp.mean(centred * centred, -1, keepdims=True) + EPS)
    normed = centred * inv_std
    return (normed * norm_gain, normed, inv_std)


def norm_back(d_out, normed, inv_std, norm_gain):
    d_normed = d_out * norm_gain
    return inv_std * (
        d_normed
        - jnp.mean(d_normed, -1, keepdims=True)
        - normed * jnp.mean(d_normed * normed, -1, keepdims=True)
    )


def log_total(values, axis):
    highest = jnp.max(values, axis=axis, keepdims=True)
    return highest + jnp.log(jnp.sum(jnp.exp(values - highest), axis=axis, keepdims=True))


def balancing_log_space(sort_logits):
    for sweep in range(SINK):
        sort_logits = sort_logits - log_total(sort_logits, 2)
        sort_logits = sort_logits - log_total(sort_logits, 1)
    return sort_logits


def gelu_value(values):
    return 0.5 * values * (1.0 + lax.erf(values * ROOT_HALF))


def gelu_slope(values):
    return (
        0.5 * (1.0 + lax.erf(values * ROOT_HALF))
        + values * jnp.exp(-0.5 * values * values) * INV_ROOT_TWO_PI
    )


def local(
    tokens,
    gain_attn,
    gain_ffn,
    w_qkv,
    w_out,
    w_sort,
    w_up,
    w_down,
    gumbel_noise,
    partner,
    cotangent,
):
    f32 = jnp.float32
    bf16 = jnp.bfloat16
    tok_rows = tokens.shape[0]
    blocks_dev = tok_rows // BLOCK
    heads_dev = w_out.shape[0] // DH
    width_dev = heads_dev * DH
    requests = blocks_dev * heads_dev
    dev_count = lax.axis_size("blk")
    my_index = lax.axis_index("blk")
    first_block = my_index * blocks_dev
    seq_blocks = partner.shape[0]
    scale = DH ** (-0.5)
    gain_one = gain_attn.astype(f32)
    gain_two = gain_ffn.astype(f32)
    inputs = tokens.astype(f32)
    h_one, normed_one, inv_one = normalize(inputs, gain_one)
    h_one_low = h_one.astype(bf16)
    qkv = jnp.einsum("td,dcf->tcf", h_one_low, w_qkv, preferred_element_type=f32).astype(bf16)
    summary = jnp.mean(h_one.reshape(blocks_dev, BLOCK, D), axis=1)
    sort_mat = w_sort.astype(f32)
    own_rows = (
        jnp.dot(summary, sort_mat, precision=HIGHEST).reshape(blocks_dev, heads_dev, seq_blocks)
        + gumbel_noise
    ) / TEMPER
    every_rows = lax.all_gather(own_rows, "blk", axis=0, tiled=True)
    my_partner = lax.dynamic_slice_in_dim(partner, first_block, blocks_dev, 0)

    def own_weights(sequence_rows):
        balanced_plan = balancing_log_space(sequence_rows.transpose(1, 0, 2))
        mine = lax.dynamic_slice_in_dim(jnp.exp(balanced_plan), first_block, blocks_dev, 1)
        return seq_blocks * jnp.take_along_axis(mine, my_partner.T[:, :, None], axis=2)[:, :, 0]

    weight_hb, sink_pull = jax.vjp(own_weights, every_rows)
    weight_matrix = weight_hb.T
    owner_all = (partner // blocks_dev).reshape(dev_count, requests)
    slot_all = (
        partner % blocks_dev * heads_dev + jnp.arange(heads_dev, dtype=jnp.int32)[None, :]
    ).reshape(dev_count, requests)
    owner_mine = lax.dynamic_index_in_dim(owner_all, my_index, 0, keepdims=False)
    tile_ids = jnp.arange(requests, dtype=jnp.int32)
    key_value = (
        qkv[:, 1:3]
        .reshape(blocks_dev, BLOCK, 2, heads_dev, DH)
        .transpose(0, 3, 1, 2, 4)
        .reshape(requests, BLOCK, 2 * DH)
    )
    empty_tile = jnp.zeros((), bf16)
    wanted = owner_all == my_index
    outgoing = jnp.where(
        wanted[:, :, None, None], jnp.take(key_value, slot_all, axis=0), empty_tile
    )
    incoming = lax.all_to_all(outgoing, "blk", split_axis=0, concat_axis=0, tiled=True)
    partner_tiles = jnp.sum(incoming, axis=0, dtype=f32).astype(bf16)
    far_tiles = partner_tiles.reshape(blocks_dev, heads_dev, BLOCK, 2, DH)
    key_far = far_tiles[:, :, :, 0]
    value_far = far_tiles[:, :, :, 1]
    query_b = qkv[:, 0].reshape(blocks_dev, BLOCK, heads_dev, DH)
    key_b = qkv[:, 1].reshape(blocks_dev, BLOCK, heads_dev, DH)
    value_b = qkv[:, 2].reshape(blocks_dev, BLOCK, heads_dev, DH)
    weight_s = weight_matrix[:, :, None, None]

    def score_parts():
        near_z = scale * jnp.einsum("bqhd,bkhd->bhqk", query_b, key_b, preferred_element_type=f32)
        far_z = scale * jnp.einsum("bqhd,bhkd->bhqk", query_b, key_far, preferred_element_type=f32)
        return (near_z, far_z, jnp.concatenate([near_z, weight_s * far_z], -1))

    near_z, far_z, scores = score_parts()
    highest = jnp.max(scores, -1, keepdims=True)
    expo = jnp.exp(scores - highest)
    row_total = jnp.sum(expo, -1, keepdims=True)
    log_sum = highest + jnp.log(row_total)
    probs_low = (expo / row_total).astype(bf16)
    near_ctx = jnp.einsum(
        "bhqk,bkhd->bqhd", probs_low[..., :BLOCK], value_b, preferred_element_type=f32
    )
    far_ctx = jnp.einsum(
        "bhqk,bhkd->bqhd", probs_low[..., BLOCK:], value_far, preferred_element_type=f32
    )
    context = near_ctx + weight_matrix[:, None, :, None] * far_ctx
    context_low = context.reshape(tok_rows, width_dev).astype(bf16)
    attn = lax.psum(jnp.dot(context_low, w_out, preferred_element_type=f32), "head")
    middle = inputs + attn
    h_two, normed_two, inv_two = normalize(middle, gain_two)
    h_two_low = h_two.astype(bf16)
    hidden_pre = jnp.dot(h_two_low, w_up, preferred_element_type=f32)
    active_low = gelu_value(hidden_pre).astype(bf16)
    ffn = lax.psum(
        jnp.dot(active_low, w_down, preferred_element_type=f32).astype(jnp.bfloat16), "head"
    ).astype(jnp.float32)
    output = middle + ffn
    g_down = jnp.einsum("tf,td->fd", active_low, cotangent, preferred_element_type=f32)
    d_active = jnp.einsum("td,fd->tf", cotangent, w_down, preferred_element_type=f32)
    d_hidden = (d_active * gelu_slope(hidden_pre)).astype(bf16)
    g_up = jnp.einsum("td,tf->df", h_two_low, d_hidden, preferred_element_type=f32)
    d_h_two = lax.psum(jnp.einsum("tf,df->td", d_hidden, w_up, preferred_element_type=f32), "head")
    g_gain_two = jnp.sum(d_h_two * normed_two, 0)
    d_middle = cotangent.astype(f32) + norm_back(d_h_two, normed_two, inv_two, gain_two)
    d_attn_low = d_middle.astype(bf16)
    g_out = jnp.einsum("tf,td->fd", context_low, d_attn_low, preferred_element_type=f32)
    d_context = jnp.einsum("td,fd->tf", d_attn_low, w_out, preferred_element_type=f32).astype(bf16)
    d_context = d_context.reshape(blocks_dev, BLOCK, heads_dev, DH)
    near_z, far_z, scores = score_parts()
    probs = jnp.exp(scores - log_sum)
    probs_low = probs.astype(bf16)
    far_ctx = jnp.einsum(
        "bhqk,bhkd->bqhd", probs_low[..., BLOCK:], value_far, preferred_element_type=f32
    )
    d_probs_near = jnp.einsum("bqhd,bkhd->bhqk", d_context, value_b, preferred_element_type=f32)
    d_probs_far = weight_s * jnp.einsum(
        "bqhd,bhkd->bhqk", d_context, value_far, preferred_element_type=f32
    )
    d_probs = jnp.concatenate([d_probs_near, d_probs_far], -1)
    d_scores = probs * (d_probs - jnp.sum(d_probs * probs, -1, keepdims=True))
    d_near = d_scores[..., :BLOCK].astype(bf16)
    d_far_raw = d_scores[..., BLOCK:]
    d_far = (weight_s * d_far_raw).astype(bf16)
    d_weight = jnp.sum(d_far_raw * far_z, (2, 3)) + jnp.sum(d_context.astype(f32) * far_ctx, (1, 3))
    d_query = scale * (
        jnp.einsum("bhqk,bkhd->bqhd", d_near, key_b, preferred_element_type=f32)
        + jnp.einsum("bhqk,bhkd->bqhd", d_far, key_far, preferred_element_type=f32)
    )
    d_key = scale * jnp.einsum("bhqk,bqhd->bkhd", d_near, query_b, preferred_element_type=f32)
    d_value = jnp.einsum(
        "bhqk,bqhd->bkhd", probs_low[..., :BLOCK], d_context, preferred_element_type=f32
    )
    d_key_far = scale * jnp.einsum("bhqk,bqhd->bhkd", d_far, query_b, preferred_element_type=f32)
    d_value_far = weight_s * jnp.einsum(
        "bhqk,bqhd->bhkd", probs_low[..., BLOCK:], d_context, preferred_element_type=f32
    )
    grad_tiles = jnp.stack([d_key_far.astype(bf16), d_value_far.astype(bf16)], 3).reshape(
        requests, BLOCK * 2 * DH
    )
    peers = jnp.arange(dev_count, dtype=jnp.int32)
    outgoing_grads = jnp.where(
        (owner_mine[None, :] == peers[:, None])[:, :, None], grad_tiles[None], empty_tile
    )
    returned = lax.all_to_all(outgoing_grads, "blk", split_axis=0, concat_axis=0, tiled=True)
    selector = (owner_all == my_index)[:, :, None] & (
        slot_all[:, :, None] == tile_ids[None, None, :]
    )
    selector = selector.reshape(dev_count * requests, requests).astype(bf16)
    remote = jnp.einsum(
        "st,sf->tf",
        selector,
        returned.reshape(dev_count * requests, BLOCK * 2 * DH),
        preferred_element_type=f32,
    )
    remote = (
        remote.reshape(blocks_dev, heads_dev, BLOCK, 2, DH)
        .transpose(0, 2, 3, 1, 4)
        .reshape(tok_rows, 2, width_dev)
    )
    near_kv = (
        jnp.stack([d_key.reshape(tok_rows, width_dev), d_value.reshape(tok_rows, width_dev)], 1)
        + remote
    )
    d_qkv = jnp.concatenate([d_query.reshape(tok_rows, 1, width_dev), near_kv], 1).astype(bf16)
    g_qkv = jnp.einsum("td,tcf->dcf", h_one_low, d_qkv, preferred_element_type=f32)
    d_h_part = jnp.einsum("tcf,dcf->td", d_qkv, w_qkv, preferred_element_type=f32)
    (d_every,) = sink_pull(d_weight.T)
    d_own = lax.psum_scatter(d_every, "blk", scatter_dimension=0, tiled=True) / TEMPER
    d_flat = d_own.reshape(blocks_dev, heads_dev * seq_blocks)
    g_sort = jnp.dot(summary.T, d_flat, precision=HIGHEST)
    d_summary = jnp.dot(d_flat, sort_mat.T, precision=HIGHEST)
    d_h_part = (d_h_part.reshape(blocks_dev, BLOCK, D) + d_summary[:, None, :] / BLOCK).reshape(
        tok_rows, D
    )
    d_h_one = lax.psum(d_h_part, "head")
    g_gain_one = jnp.sum(d_h_one * normed_one, 0)
    d_tokens = d_middle + norm_back(d_h_one, normed_one, inv_one, gain_one)
    summed = lax.psum((g_gain_one, g_gain_two, g_qkv, g_out, g_sort, g_up, g_down), "blk")
    return (
        output,
        d_tokens,
        summed[0],
        summed[1],
        summed[2],
        summed[3],
        summed[4],
        summed[5],
        summed[6],
    )


def mask_pair(values, near):
    zero = jnp.zeros_like(values)
    return jnp.where(near, values, zero), jnp.where(near, zero, values)


def first_lanes():
    return lax.broadcasted_iota(jnp.int32, (1, 2 * DH), 1) < DH


def dot_nn(a, b):
    return lax.dot_general(a, b, (((1,), (0,)), ((), ())), preferred_element_type=jnp.float32)


def dot_nt(a, b):
    return lax.dot_general(a, b, (((1,), (1,)), ((), ())), preferred_element_type=jnp.float32)


def dot_tn(a, b):
    return lax.dot_general(a, b, (((0,), (0,)), ((), ())), preferred_element_type=jnp.float32)


def three_parts(values):
    high = values.astype(jnp.bfloat16)
    rest = values - high.astype(jnp.float32)
    mid = rest.astype(jnp.bfloat16)
    low = (rest - mid.astype(jnp.float32)).astype(jnp.bfloat16)
    return high, mid, low


def norm_parts(values):
    centred = values - jnp.mean(values, -1, keepdims=True)
    inv_std = lax.rsqrt(jnp.mean(centred * centred, -1, keepdims=True) + EPS)
    return centred * inv_std, inv_std


def noise_rows(noise):
    few = noise.shape[0] // 2
    return [
        jnp.concatenate([noise[r * few + i, h : h + 1, :] for i in range(few) for h in range(2)], 1)
        for r in range(2)
    ]


def head_kernel(tokens, gain, noise, other_noise, first, second, summary, own_noise):
    f32, bf16 = jnp.float32, jnp.bfloat16
    rows = tokens.shape[0]
    half = rows // 2
    core = lax.axis_index("head") % 2
    normed, _ = norm_parts(tokens[...].astype(f32))
    h = normed * gain[...].astype(f32)
    low = h.astype(bf16)
    means = jnp.mean(h.reshape(rows // BLOCK, BLOCK, D), axis=1)
    summary[...] = means
    mine = jnp.concatenate(noise_rows(noise), 0)
    other = jnp.concatenate(noise_rows(other_noise), 0)
    own_noise[...] = mine
    both = jnp.where(
        core == 0, jnp.concatenate([mine, other], 0), jnp.concatenate([other, mine], 0)
    )
    few = means.shape[0] // 2
    for k, ref in enumerate((first, second)):
        ref[:half, :] = low[k * half : (k + 1) * half, :]
        parts = [p.astype(f32) for p in three_parts(means[k * few : (k + 1) * few, :])]
        parts += [p.astype(f32) for p in three_parts(both)] if k else [jnp.zeros((12, D), f32)]
        parts.append(jnp.zeros((EXTRA - 24, D), f32))
        ref[half:, :] = jnp.concatenate(parts, 0).astype(bf16)


def project_rows(rows, joint):
    return dot_nn(rows, joint[:, : 6 * DH]).astype(jnp.bfloat16)


def project_own_kernel(h_first, h_second, weight, w_sort, w_out, down, out, joint, first, second):
    width = w_out.shape[0]
    more = first.shape[0] - width
    first[:width, :] = w_out[...]
    first[width:, :] = down[:more, :]
    second[...] = down[more:, :]
    joint[...] = jnp.concatenate([weight[i] for i in range(3)] + [w_sort[...]], 1)
    project_half(h_first, joint, out, 0)
    project_half(h_second, joint, out, h_first.shape[0] - EXTRA)


def project_half(piece, joint, out, to):
    for start in range(0, piece.shape[0] - EXTRA, 2 * BLOCK):
        rows = project_rows(piece[start : start + 2 * BLOCK, :], joint)
        out[to + start : to + start + 2 * BLOCK, :] = rows


def project_kernel(mine1, mine2, other1, other2, joint, out, extra):
    half = mine1.shape[0] - EXTRA
    for k, piece in enumerate((mine1, mine2, other1, other2)):
        project_half(piece, joint, out, k * half)
        extra[k * EXTRA : (k + 1) * EXTRA, :] = piece[half:, :]


def half_kernel(first, second, w_out, w_out_y, half, pair):
    width = w_out.shape[0]
    even = lax.axis_index("head") % 2 == 0
    half[...] = jnp.where(even, first[...], second[...])
    pair[:width, :] = w_out[...]
    pair[width:, :] = w_out_y[:width, :]


def turn():
    return 1 - 2 * (lax.axis_index("head") % 2)


def owners_of(step):
    place = place_of(lax.axis_index("blk"))
    core = lax.axis_index("head") % 2
    way = jnp.where(core == 0, 8 - step, step)
    return ring_of((place + way) % 8), ring_of((place + 8 - way) % 8)


def ring_of(position):
    return jnp.where(position < 4, 2 * position, 2 * (7 - position) + 1)


def place_of(index):
    return jnp.where(index % 2 == 0, index // 2, 7 - index // 2)


def far_near(table, at, lanes):
    return table[pl.ds(pl.multiple_of(at * BLOCK, BLOCK), BLOCK), lanes]


def block_operands(qkv, block, first, second, near):
    k_lanes, v_lanes = slice(2 * DH, 4 * DH), slice(4 * DH, 6 * DH)
    query = far_near(qkv, block, slice(0, 2 * DH))
    keys, values = [], []
    for lanes, store in ((k_lanes, keys), (v_lanes, values)):
        own0, own1 = mask_pair(far_near(qkv, block, lanes), near)
        far0, _ = mask_pair(far_near(qkv, first, lanes), near)
        _, far1 = mask_pair(far_near(qkv, second, lanes), near)
        store.extend([own0, far0, own1, far1])
    return query, keys, values


def block_probs(scores):
    probs = []
    for h in range(2):
        part = scores[:, h * 2 * DH : (h + 1) * 2 * DH]
        expo = jnp.exp(part - jnp.max(part, -1, keepdims=True))
        probs.append(expo / jnp.sum(expo, -1, keepdims=True))
    return probs


def choices(partner, h):
    nb = partner.shape[1]
    sides = lax.broadcasted_iota(jnp.int32, (nb, nb), 0)
    hot = (sides == partner[h : h + 1, :]).astype(jnp.bfloat16)
    same = sides == lax.broadcasted_iota(jnp.int32, (nb, nb), 1)
    return dot_nt(same.astype(jnp.bfloat16), hot)


def joined(rows, at, count):
    parts = [rows[at + k * count : at + (k + 1) * count, :].astype(jnp.float32) for k in range(3)]
    return (parts[0] + parts[1]) + parts[2]


def attend_kernel(
    own, step1, step2, step3, extra1, extra2, extra3, mine4, other4, joint, own_summary, own_noise,
    partner, partner_rows, qkv, context, summary, steps, scale_rows, weight_rows, noise,
):
    f32, bf16 = jnp.float32, jnp.bfloat16
    me = lax.axis_index("blk")
    core = lax.axis_index("head") % 2
    nb = partner_rows.shape[1]
    rows = own.shape[0]
    half = rows // 2
    blocks = rows // BLOCK
    few = blocks // 2

    def put(owner, start, values):
        n = values.shape[0]
        qkv[pl.ds(pl.multiple_of(owner * rows + start, n), n), :] = values

    def put_noise(owner, values):
        lines = [
            values[r : r + 1, i * 2 * nb : (i + 1) * 2 * nb] for r in range(2) for i in range(few)
        ]
        at = pl.multiple_of(owner * blocks, blocks)
        noise[pl.ds(at, blocks), :] = jnp.concatenate(lines, 0)

    def put_extra(owner, first, second):
        at = pl.multiple_of(owner * blocks, blocks)
        summary[pl.ds(at, blocks), :] = jnp.concatenate(
            [joined(first, 0, few), joined(second, 0, few)], 0
        )
        both = joined(second, 3 * few, 4)
        put_noise(owner, jnp.where(core == 0, both[:2], both[2:]))

    put(me, 0, own[...])
    summary[pl.ds(pl.multiple_of(me * blocks, blocks), blocks), :] = own_summary[...]
    put_noise(me, own_noise[...])
    for step, ref, extra in ((1, step1, extra1), (2, step2, extra2), (3, step3, extra3)):
        for k, owner in enumerate(owners_of(step)):
            put(owner, 0, ref[k * rows : (k + 1) * rows, :])
            at = 2 * k * EXTRA
            put_extra(owner, extra[at : at + EXTRA, :], extra[at + EXTRA : at + 2 * EXTRA, :])
    owner, _ = owners_of(4)
    for side, ref in ((core, mine4), (1 - core, other4)):
        for start in range(0, half, 2 * BLOCK):
            values = project_rows(ref[start : start + 2 * BLOCK, :], joint)
            put(owner, side * half + start, values)
    ends = [ref[half:, :].astype(f32) for ref in (mine4, other4)]
    put_extra(
        owner, jnp.where(core == 0, ends[0], ends[1]), jnp.where(core == 0, ends[1], ends[0])
    )

    parts = three_parts(summary[...])
    logits = sum(dot_nn(part, joint[:, 6 * DH :]) for part in parts[::-1])
    logits = (logits + noise[...]) / TEMPER
    plan = jnp.stack([logits[:, :nb], logits[:, nb:]])
    for sweep in range(SINK):
        for k, axis in enumerate((2, 1)):
            plan = plan - log_total(plan, axis)
            steps[2 * sweep + k] = jnp.exp(plan)
    final = jnp.exp(plan)
    picked = []
    for h in range(2):
        picked.append(nb * jnp.sum(choices(partner_rows, h) * final[h], axis=1, keepdims=True))
    ones = jnp.ones((nb, DH), f32)
    scale_rows[...] = jnp.concatenate([ones, picked[0] * ones, ones, picked[1] * ones], 1)
    weight_rows[...] = jnp.concatenate([picked[0] * ones, picked[1] * ones], 1)

    near = first_lanes()
    work = []
    for i in range(blocks):
        block = me * blocks + i
        query, keys, values = block_operands(
            qkv, block, partner[0, block], partner[1, block], near
        )
        none = jnp.zeros_like(values[0])
        table = jnp.concatenate(
            [
                jnp.concatenate([values[0], none, values[2], none], 0),
                jnp.concatenate([none, values[1], none, values[3]], 0),
            ],
            1,
        )
        z = dot_nt(query, jnp.concatenate(keys, 0)) * (DH**-0.5)
        work.append((block, z, table))
    probs = [block_probs(z * scale_rows[pl.ds(block, 1), :]) for block, z, _ in work]
    outs = [
        dot_nn(jnp.concatenate([p.astype(bf16) for p in prob], 1), table)
        for prob, (_, _, table) in zip(probs, work)
    ]
    for i, (out, (block, _, _)) in enumerate(zip(outs, work)):
        ctx = out[:, : 2 * DH] + weight_rows[pl.ds(block, 1), :] * out[:, 2 * DH :]
        context[i * BLOCK : (i + 1) * BLOCK, :] = ctx.astype(bf16)


def feed_kernel(
    tokens, cotangent, gain, ctx0, ctx1, ctx2, ctx3, wo, wo_other, up_a, up_b, down_a, first, second,
    middle, h_two, active, d_hidden, ffn, d_h_two,
    ctx_full, wo_full, up_full, down_full, act_full, d_full,
):
    f32, bf16 = jnp.float32, jnp.bfloat16
    hd = lax.axis_index("head")
    row = hd // 2
    width = ctx0.shape[1]
    ff = up_a.shape[1]
    for j, c in enumerate((ctx0, ctx1, ctx2, ctx3)):
        at = pl.multiple_of((hd ^ j) * width, width)
        ctx_full[:, pl.ds(at, width)] = c[...]
        w = wo if j % 2 == 0 else wo_other
        wo_full[pl.ds(at, width), :] = w[j // 2 * width : (j // 2 + 1) * width, :]
    here, there = (pl.multiple_of((row ^ j) * ff, ff) for j in range(2))
    up_full[:, pl.ds(here, ff)] = up_a[...]
    up_full[:, pl.ds(there, ff)] = up_b[...]
    down_full[pl.ds(here, ff), :] = down_a[...]
    more = first.shape[0] - width
    down_full[pl.ds(there, more), :] = first[width:, :]
    down_full[pl.ds(pl.multiple_of(there + more, 32), ff - more), :] = second[...]
    chunk = 256
    for start in range(0, tokens.shape[0], chunk):
        sl = slice(start, start + chunk)
        mid = tokens[sl, :].astype(f32) + dot_nn(ctx_full[sl, :], wo_full[...])
        middle[sl, :] = mid
        normed, _ = norm_parts(mid)
        low = (normed * gain[...].astype(f32)).astype(bf16)
        h_two[sl, :] = low
        ffn_sum = None
        back_sum = None
        for j in range(2):
            cols = slice(j * ff, (j + 1) * ff)
            pre = dot_nn(low, up_full[:, cols])
            d_act = dot_nt(cotangent[sl, :], down_full[cols, :])
            bell = 0.5 * (1.0 + lax.erf(pre * ROOT_HALF))
            act = (pre * bell).astype(bf16)
            slope = bell + pre * jnp.exp(-0.5 * pre * pre) * INV_ROOT_TWO_PI
            d_pre = (d_act * slope).astype(bf16)
            act_full[sl, cols] = act
            d_full[sl, cols] = d_pre
            f = dot_nn(act, down_full[cols, :])
            b = dot_nt(d_pre, up_full[:, cols])
            ffn_sum = f if ffn_sum is None else ffn_sum + f
            back_sum = b if back_sum is None else back_sum + b
        ffn[sl, :] = ffn_sum
        d_h_two[sl, :] = back_sum
    mine = pl.ds(pl.multiple_of(row * ff, ff), ff)
    active[...] = act_full[:, mine]
    d_hidden[...] = d_full[:, mine]


def back_kernel(middle, own, other, cotangent, gain, w_out, d_middle, d_low, d_ctx, g_gain):
    f32, bf16 = jnp.float32, jnp.bfloat16
    normed, inv = norm_parts(middle[...])
    d_h = own[...] + other[...]
    g_gain[...] = jnp.broadcast_to(jnp.sum(d_h * normed, 0, keepdims=True), g_gain.shape)
    d_mid = cotangent[...].astype(f32) + norm_back(d_h, normed, inv, gain[...].astype(f32))
    d_middle[...] = d_mid
    low = d_mid.astype(bf16)
    d_low[...] = low
    d_ctx[...] = dot_nt(low, w_out[...]).astype(bf16)


def stacked(rows):
    return jnp.concatenate([rows[:, k * 2 * DH : (k + 1) * 2 * DH] for k in range(D // (2 * DH))], 0)


def grads_kernel(h_two, d_hidden, active, cotangent, context, d_low, d_ctx, *refs):
    keeps, (ahead, behind), (up, down, out) = refs[:7], refs[7:9], refs[9:]
    place = place_of(lax.axis_index("blk"))
    up[...] = dot_tn(h_two[...], d_hidden[...])
    down[...] = dot_tn(active[...], cotangent[...])
    out[...] = dot_tn(context[...], d_low[...])

    def rows_of(distance):
        owner = ring_of((place + turn() * distance + 8) % 8)
        parts = []
        for ref in (up, down, out):
            n = ref.shape[0] // 8
            parts.append(ref[pl.ds(pl.multiple_of(owner * n, n), n), :])
        return jnp.concatenate(parts, 0)

    for ref, distance in zip(keeps, (3, 2, 1, -3, -2, -1, 0)):
        ref[...] = stacked(rows_of(distance))
    last = rows_of(4).astype(jnp.bfloat16)
    rows = d_ctx.shape[0]
    n = (ahead.shape[0] - rows) // 4
    for ref, part in ((ahead, last[:n]), (behind, last[n:])):
        ref[:rows, :] = d_ctx[...]
        ref[rows:, :] = stacked(part)


def relay_kernel(start, count, at, keep, arrived, out):
    f32, bf16 = jnp.float32, jnp.bfloat16
    size = keep.shape[0] // 4
    n = (arrived.shape[0] - SHARD) // 4
    out[:count, :] = arrived[start : start + count, :]
    out[count:, :] = keep[...].astype(bf16)
    for k in range(4):
        here = slice(k * size + at, k * size + at + n)
        total = keep[here, :] + arrived[SHARD + k * n : SHARD + (k + 1) * n, :].astype(f32)
        out[count + k * size + at : count + k * size + at + n, :] = total.astype(bf16)


def total_kernel(keep, x, y, out):
    f32 = jnp.float32
    size = keep.shape[0] // 4
    skip = x.shape[0] - 4 * size
    for k in range(4):
        rows = slice(k * size, (k + 1) * size)
        there = slice(skip + k * size, skip + (k + 1) * size)
        total = keep[rows, :] + (x[there, :].astype(f32) + y[there, :].astype(f32))
        out[:, k * 2 * DH : (k + 1) * 2 * DH] = total.astype(jnp.bfloat16)


def cut_kernel(f, b, front, back):
    front[...] = f[: front.shape[0], :]
    back[...] = b[b.shape[0] - back.shape[0] :, :]


def lay_kernel(own, f1, b1, f2, b2, f3, b3, f4, b4, gains, other, g_up, g_down, g_out, g_one, g_two):
    f32 = jnp.float32
    total = gains[...] + other[...]
    g_one[...] = total[0, :]
    g_two[...] = total[8, :]
    place = place_of(lax.axis_index("blk"))
    last = jnp.concatenate([f4[...], b4[...]], 0)
    for distance, piece in (
        (0, own[...]), (-1, f1[...]), (1, b1[...]), (-2, f2[...]), (2, b2[...]), (-3, f3[...]), (3, b3[...]),
        (4, last),
    ):
        owner = ring_of((place + turn() * distance + 8) % 8)
        start = 0
        for ref in (g_up, g_down, g_out):
            n = ref.shape[0] // 8
            ref[pl.ds(pl.multiple_of(owner * n, n), n), :] = piece[start : start + n].astype(f32)
            start += n


def halve_kernel(f, b, front, back):
    n = front.shape[0]
    front[...] = f[:n, :]
    back[...] = b[n:, :]


def add_kernel(*refs):
    *terms, out = refs
    total = terms[0][...]
    for term in terms[1:]:
        total = total + term[...]
    out[...] = total


def four_kernel(here, one, two, three, out):
    out[...] = (here[...] + one[...]) + (two[...] + three[...])


def block_at(place, step, start, i):
    return ring_of((place + 8 - turn() * step) % 8) * (SHARD // BLOCK) + start // BLOCK + i


def prepare_kernel(pieces, qkv, partner, scale_rows, z_out, probs_out):
    place = place_of(lax.axis_index("blk"))
    near = first_lanes()
    blocks = [(step, start, i) for step, start, n in pieces for i in range(n // BLOCK)]
    for first in range(0, len(blocks), 8):
        work = []
        for step, start, i in blocks[first : first + 8]:
            block = block_at(place, step, start, i)
            query, keys, _ = block_operands(qkv, block, partner[0, block], partner[1, block], near)
            work.append((query, jnp.concatenate(keys, 0), scale_rows[pl.ds(block, 1), :]))
        z = [dot_nt(query, keys) * (DH**-0.5) for query, keys, _ in work]
        probs = [block_probs(v * w[2]) for v, w in zip(z, work)]
        for k in range(len(work)):
            at = slice((first + k) * BLOCK, (first + k + 1) * BLOCK)
            z_out[at, :] = z[k]
            probs_out[at, :] = jnp.concatenate(probs[k], 1)


def pull_kernel(pieces, offset, *refs):
    f32, bf16 = jnp.float32, jnp.bfloat16
    count = len(pieces)
    outs, refs = refs[:count], refs[count:]
    qkv, partner, scale_rows, weight_rows, refs = *refs[:4], refs[4:]
    if offset is not None:
        z_all, probs_all, refs = refs[0], refs[1], refs[2:]
    near_out, low_out, d_weight = refs
    place = place_of(lax.axis_index("blk"))
    near = first_lanes()
    scale = DH**-0.5
    blocks = [
        (step, start, d_ctx, i)
        for (step, start, n), d_ctx in zip(pieces, outs)
        for i in range(n // BLOCK)
    ]
    for first in range(0, len(blocks), 8):
        work = []
        for k, (step, start, d_ctx, i) in enumerate(blocks[first : first + 8]):
            block = block_at(place, step, start, i)
            query, keys, values = block_operands(
                qkv, block, partner[0, block], partner[1, block], near
            )
            w = dict(
                query=query,
                keys=jnp.concatenate(keys, 0),
                values=jnp.concatenate(values, 0),
                scale=scale_rows[pl.ds(block, 1), :],
                weight=weight_rows[pl.ds(block, 1), :],
                d_out=d_ctx[i * BLOCK : (i + 1) * BLOCK, :],
            )
            if offset is not None:
                at = slice((offset + first + k) * BLOCK, (offset + first + k + 1) * BLOCK)
                w["z"] = z_all[at, :]
                w["probs"] = [probs_all[at, : 2 * DH], probs_all[at, 2 * DH :]]
            work.append(w)
        if offset is None:
            for w in work:
                w["z"] = dot_nt(w["query"], w["keys"]) * scale
        for w in work:
            w["raw"] = dot_nt(w["d_out"], w["values"])
        if offset is None:
            for w in work:
                w["probs"] = block_probs(w["z"] * w["scale"])
        for w in work:
            d_z, low, d_w = [], [], []
            for h in range(2):
                sl = slice(h * 2 * DH, (h + 1) * 2 * DH)
                probs = w["probs"][h]
                d_probs = w["raw"][:, sl] * w["scale"][:, sl]
                d_scores = probs * (d_probs - jnp.sum(d_probs * probs, -1, keepdims=True))
                d_z.append((d_scores * w["scale"][:, sl]).astype(bf16))
                low.append(probs.astype(bf16))
                d_w.append(
                    jnp.sum(
                        d_scores * w["z"][:, sl] + low[h].astype(f32) * w["raw"][:, sl],
                        0,
                        keepdims=True,
                    )
                )
            w["d_z"], w["low"] = jnp.concatenate(d_z, 1), jnp.concatenate(low, 1)
            w["d_w"] = jnp.concatenate(d_w, 1)
        for w in work:
            w["d_query"] = dot_nn(w["d_z"], w["keys"]) * scale
        for w in work:
            w["d_keys"] = dot_tn(w["d_z"], w["query"]) * scale
        for w in work:
            w["d_values"] = dot_tn(w["low"], w["d_out"])
        for k, w in enumerate(work):
            to = first + k
            at = slice(to * BLOCK, (to + 1) * BLOCK)
            d_weight[to : to + 1, :] = w["d_w"]
            low_out[at, : 2 * DH] = w["d_query"].astype(bf16)
            for m, name in enumerate(("d_keys", "d_values")):
                parts = [w[name][i * BLOCK : (i + 1) * BLOCK, :] for i in range(4)]
                near_out[at, m * 2 * DH : (m + 1) * 2 * DH] = jnp.where(near, parts[0], parts[2])
                far = jnp.where(near, parts[1], parts[3])
                if m == 1:
                    far = far * w["weight"]
                low_out[at, (m + 1) * 2 * DH : (m + 2) * 2 * DH] = far.astype(bf16)


def collect_kernel(pieces, *refs):
    f32, bf16 = jnp.float32, jnp.bfloat16
    count = len(pieces)
    nears, lows, d_weights = refs[:count], refs[count : 2 * count], refs[2 * count : 3 * count]
    partner, partner_rows, steps, summary = refs[3 * count : 3 * count + 4]
    d_qkv, d_mine, flat_mine, g_sort, d_weight, acc, far, d_flat = refs[3 * count + 4 :]
    me = lax.axis_index("blk")
    place = place_of(me)
    for parts, near_ref, low_ref, w_ref in zip(pieces, nears, lows, d_weights):
        at = 0
        for step, start, n in parts:
            owner = ring_of((place + 8 - turn() * step) % 8)
            to = pl.ds(pl.multiple_of(owner * SHARD + start, n), n)
            acc[to, :] = near_ref[at : at + n, :]
            far[to, :] = low_ref[at : at + n, 2 * DH :]
            d_qkv[to, : 2 * DH] = low_ref[at : at + n, : 2 * DH]
            if start == 0:
                nb = SHARD // BLOCK
                first = pl.multiple_of(owner * nb, nb)
                d_weight[pl.ds(first, nb), :] = w_ref[at // BLOCK : at // BLOCK + nb, :]
            at += n
    near = first_lanes()
    both = jnp.concatenate([near, near], 1)

    def body(block, _):
        tile = far[pl.ds(pl.multiple_of(block * BLOCK, BLOCK), BLOCK), :].astype(f32)
        for h, kept in ((0, jnp.where(both, tile, 0.0)), (1, jnp.where(both, 0.0, tile))):
            to = pl.ds(pl.multiple_of(partner[h, block] * BLOCK, BLOCK), BLOCK)
            acc[to, :] += kept
        return 0

    lax.fori_loop(0, partner.shape[1], body, 0, unroll=4)
    d_qkv[:, 2 * DH :] = acc[...].astype(bf16)
    d_mine[...] = d_qkv[pl.ds(pl.multiple_of(me * SHARD, SHARD), SHARD), :]
    d_flat[...] = sink_back(d_weight[...], steps, partner_rows)
    n = flat_mine.shape[0]
    flat_mine[...] = d_flat[pl.ds(pl.multiple_of(me * n, n), n), :]
    g_sort[...] = lax.dot_general(
        summary[...],
        d_flat[...],
        (((0,), (0,)), ((), ())),
        precision=HIGHEST,
        preferred_element_type=f32,
    )


def sink_back(d_weight, steps, partner):
    nb = partner.shape[1]
    grads = []
    for h in range(2):
        total = jnp.sum(
            d_weight[:, (2 * h + 1) * DH : (2 * h + 2) * DH], axis=1, keepdims=True
        )
        grads.append(choices(partner, h) * (nb * total))
    last = steps.shape[0] - 1
    grad = jnp.stack(grads) * steps[last]
    for t in range(last, -1, -1):
        grad = grad - steps[t] * jnp.sum(grad, axis=1 if t % 2 else 2, keepdims=True)
    return jnp.concatenate([grad[0], grad[1]], 1) / TEMPER


def weight_kernel(*refs):
    *halves, d_qkv, g_qkv, h_all = refs
    me = lax.axis_index("blk")
    core = lax.axis_index("head") % 2
    half = halves[0].shape[0] - EXTRA
    rows = 2 * half

    def put(owner, side, ref):
        at = pl.ds(pl.multiple_of(owner * rows + side * half, half), half)
        h_all[at, :] = ref[:half, :]

    owners = [me] + [owner for step in (1, 2, 3) for owner in owners_of(step)]
    for k, owner in enumerate(owners):
        put(owner, 0, halves[2 * k])
        put(owner, 1, halves[2 * k + 1])
    owner, _ = owners_of(4)
    put(owner, core, halves[14])
    put(owner, 1 - core, halves[15])
    out = dot_tn(h_all[...], d_qkv[...])
    width = g_qkv.shape[2]
    for i in range(3):
        g_qkv[i] = out[:, i * width : (i + 1) * width]


def input_kernel(dq_a, dq_b, joint_a, joint_b, flat_a, flat_b, d_h, dq_full, w_full, flat_full, sort_full):
    row = lax.axis_index("head") // 2
    width, nb = dq_a.shape[1], flat_a.shape[1]
    sides = ((dq_a, joint_a, flat_a), (dq_b, joint_b, flat_b))
    for j, (g, joint, flat) in enumerate(sides):
        at = pl.multiple_of((row ^ j) * width, width)
        dq_full[:, pl.ds(at, width)] = g[...]
        w_full[:, pl.ds(at, width)] = joint[:, :width]
        at = pl.multiple_of((row ^ j) * nb, nb)
        flat_full[:, pl.ds(at, nb)] = flat[...]
        sort_full[:, pl.ds(at, nb)] = joint[:, width:]
    part = dot_nt(dq_full[...], w_full[...])
    d_sum = sum(dot_nt(p, sort_full[...]) for p in three_parts(flat_full[...])[::-1]) / BLOCK
    blocks = d_sum.shape[0]
    for i in range(blocks):
        sl = slice(i * BLOCK, (i + 1) * BLOCK)
        d_h[sl, :] = part[sl, :] + d_sum[i : i + 1, :]


def gain_kernel(tokens, d_mine, flat_mine, joint, g_two, out):
    width = d_mine.shape[1]
    normed, _ = norm_parts(tokens[...].astype(jnp.float32))
    part = dot_nt(d_mine[...], joint[:, :width])
    d_sum = sum(dot_nt(p, joint[:, width:]) for p in three_parts(flat_mine[...])[::-1]) / BLOCK
    blocks = d_sum.shape[0]
    sums = jnp.sum(part * normed, 0, keepdims=True)
    means = jnp.sum(normed.reshape(blocks, BLOCK, D), 1)
    sums = sums + jnp.sum(d_sum * means, 0, keepdims=True)
    out[:8, :] = jnp.broadcast_to(sums, g_two.shape)
    out[8:, :] = jnp.where(lax.axis_index("head") == 0, g_two[...], 0.0)


def end_kernel(tokens, gain, own, other, d_middle, d_tokens):
    f32 = jnp.float32
    normed, inv = norm_parts(tokens[...].astype(f32))
    d_h = own[...] + other[...]
    d_tokens[...] = d_middle[...] + norm_back(d_h, normed, inv, gain[...].astype(f32))


VMEM_SPEC = pl.BlockSpec(memory_space=pltpu.VMEM)
SMEM_SPEC = pl.BlockSpec(memory_space=pltpu.SMEM)
ANY_SPEC = pl.BlockSpec(memory_space=pltpu.HBM)
FREE_SPEC = pl.BlockSpec(memory_space=pl.ANY)


def fetch(pairs, sems, first=0):
    copies = []
    for k, (source, target) in enumerate(pairs):
        copies.append(pltpu.make_async_copy(source, target, sems.at[first + k]))
        copies[-1].start()
    return copies


def wait_all(copies):
    for copy in copies:
        copy.wait()


def call(kernel, outs, *args, scratch=(), smem=(), cold=(), free=(), raw=(), out_cold=(), limit=16, name=None):
    cost = int(1e3 * TIMES[name])
    shapes = [jax.ShapeDtypeStruct(s, d) for s, d in outs]
    specs = [
        SMEM_SPEC if i in smem else FREE_SPEC if i in free else ANY_SPEC if i in cold or i in raw else VMEM_SPEC
        for i in range(len(args))
    ]
    out_specs = [ANY_SPEC if i in out_cold else VMEM_SPEC for i in range(len(outs))]
    buffers = [pltpu.VMEM(args[i].shape, args[i].dtype) for i in cold]
    buffers += [pltpu.VMEM(*outs[i]) for i in out_cold]
    sem_count = len(cold) + len(out_cold)
    sems = [pltpu.SemaphoreType.DMA((sem_count,))] if sem_count else []
    own = [pltpu.SemaphoreType.DMA((40,))] if raw else []

    def body(*refs):
        refs = list(refs)
        ins, results = refs[: len(args)], refs[len(args) : len(args) + len(outs)]
        rest = refs[len(args) + len(outs) :]
        mine, rest = rest[: len(scratch)], rest[len(scratch) :]
        room, rest = rest[: len(buffers)], rest[len(buffers) :]
        copies = []
        if cold:
            copies = fetch([(ins[i], room[k]) for k, i in enumerate(cold)], rest[0])
            for k, i in enumerate(cold):
                ins[i] = room[k]
        targets = list(results)
        for k, i in enumerate(out_cold):
            results[i] = room[len(cold) + k]
        wait_all(copies)
        kernel(*ins, *results, *mine, *(rest[-1:] if raw else []))
        if out_cold:
            wait_all(fetch([(results[i], targets[i]) for i in out_cold], rest[0], len(cold)))

    result = pl.pallas_call(
        body,
        out_shape=shapes,
        in_specs=specs,
        out_specs=out_specs,
        scratch_shapes=[pltpu.VMEM(s, d) for s, d in scratch] + buffers + sems + own,
        compiler_params=pltpu.CompilerParams(vmem_limit_bytes=limit * 1024 * 1024),
        cost_estimate=pl.CostEstimate(
            flops=cost * FLOPS, bytes_accessed=cost * BYTES, transcendentals=0
        ),
        name=name,
    )(*args)
    return result[0] if len(shapes) == 1 else result


TIMES = {
    "norm_one": 1.7,
    "project_own": 0.45,
    "project": 0.7,
    "attend": 4.2,
    "prepare": 2.9,
    "feed": 4.2,
    "back": 1.2,
    "pull": 0.1,
    "grads": 0.95,
    "relay": 0.3,
    "collect": 4.5,
    "sinkhorn_back": 2.05,
    "total": 0.25,
    "input_back": 1.0,
    "gain_part": 0.8,
    "weights": 3.6,
    "norm_one_back": 1.7,
    "output": 1.1,
    "lay": 1.6,
    "gains": 0.6,
    "halve": 0.1,
    "half": 0.1,
    "pair": 0.1,
    "add_gains": 0.1,
    "sum_gains": 0.1,
}
FLOPS, BYTES = 1150000, 3690


def tie(*values):
    return lax.optimization_barrier(values)


def after(value, *others):
    return lax.optimization_barrier((value,) + others)[0]


RING = (0, 2, 4, 6, 7, 5, 3, 1)
SHARD = 512
EXTRA = 32
CUT = 320


def local_eight(
    tokens, gain_attn, gain_ffn, w_qkv, w_out, w_sort, w_up, w_down, gumbel_noise, partner, cotangent
):
    f32, bf16 = jnp.float32, jnp.bfloat16
    rows = tokens.shape[0]
    blocks = rows // BLOCK
    width = w_out.shape[0]
    ff = w_up.shape[1]
    nb = partner.shape[0]
    total = nb * BLOCK
    half, quarter = rows // 2, rows // 4
    core = lax.axis_index("head") % 2

    def along(v, way=1):
        pairs = []
        for i in range(8):
            for h in range(4):
                to = RING[(i + (way if h % 2 == 0 else -way)) % 8]
                pairs.append((RING[i] * 4 + h, to * 4 + h))
        return lax.ppermute(v, ("blk", "head"), pairs)

    def ahead(v):
        return along(v)

    def behind(v):
        return along(v, -1)

    def swap_head(v, j):
        return lax.ppermute(v, "head", [(i, i ^ j) for i in range(4)])

    def swap_blk(v, j):
        return lax.ppermute(v, "blk", [(i, i ^ j) for i in range(8)])

    w_in = w_qkv.transpose(1, 0, 2)
    partner_s = partner.T

    a, b, own_summary, own_noise = call(
        head_kernel,
        [((half + EXTRA, D), bf16)] * 2 + [((blocks, D), f32), ((2, D), f32)],
        tokens, gain_attn, gumbel_noise, swap_head(gumbel_noise, 1),
        cold=(0, 1, 2, 3), free=(3,), limit=62, name="norm_one",
    )

    mine = [(a, b)]
    up_y = swap_head(after(w_up, a), 2)
    a, b = along(a), along(b)
    qkv_own, joint, first, second = call(
        project_own_kernel,
        [
            ((rows, 3 * width), bf16), ((D, 3 * width + 2 * nb), bf16), ((CUT, D), bf16),
            ((width + ff - CUT, D), bf16),
        ],
        *mine[0], w_in, w_sort, w_out, w_down, name="project_own",
    )
    a, qkv_own = tie(a, qkv_own)
    mine.append((a, b))
    a, b = along(a), along(b)
    b, up_y = tie(b, up_y)
    mine.append((a, b))
    first_y = swap_head(after(first, a), 2)
    a, b = along(a), along(b)
    b, first_y = tie(b, first_y)
    mine.append((a, b))
    second_y = swap_head(after(second, a), 2)
    half_3, wo = call(
        half_kernel, [((half + EXTRA, D), bf16), ((2 * width, D), bf16)], a, b, w_out, first_y, name="half"
    )
    m4 = along(half_3)
    other, projected = [], []
    for k in (1, 2, 3):
        other.append(tuple(swap_head(after(v, mine[min(k + 1, 3)][0]), 1) for v in mine[k]))
        projected.append(
            call(
                project_kernel, [((2 * rows, 3 * width), bf16), ((4 * EXTRA, D), bf16)],
                *mine[k], *other[-1], joint, name="project",
            )
        )
    m4, second_y = tie(m4, second_y, *[p[0] for p in projected])[:2]
    o4 = swap_head(m4, 1)
    qkv, context, summary, steps, scale_rows, weight_rows = call(
        attend_kernel,
        [
            ((total, 3 * width), bf16), ((rows, width), bf16), ((nb, D), f32),
            ((2 * SINK, 2, nb, nb), f32), ((nb, 4 * DH), f32), ((nb, 2 * DH), f32),
        ],
        qkv_own, *[p[0] for p in projected], *[p[1] for p in projected], m4, o4, joint, own_summary, own_noise,
        partner_s, partner_s, smem=(12,), scratch=[((nb, 2 * nb), f32)], name="attend",
    )
    ctx_y, ctx_c = swap_head(context, 2), swap_head(context, 1)
    wo_other = swap_head(after(wo, context), 1)
    prepared = ((3, 0, rows), (-3, 0, rows), (4, 0, rows))
    amount = sum(n for _, _, n in prepared)
    z_all, probs_all = call(
        functools.partial(prepare_kernel, prepared), [((amount, 4 * DH), f32)] * 2,
        qkv, partner_s, scale_rows, smem=(1,), name="prepare",
    )
    ctx_y, ctx_c, z_all = tie(ctx_y, ctx_c, z_all)
    ctx_yc = swap_head(ctx_y, 1)
    middle, h_two, active, d_hidden, ffn, d_h_two = call(
        feed_kernel,
        [
            ((rows, D), f32),
            ((rows, D), bf16),
            ((rows, ff), bf16),
            ((rows, ff), bf16),
            ((rows, D), f32),
            ((rows, D), f32),
        ],
        tokens, cotangent, gain_ffn, context, ctx_c, ctx_y, ctx_yc, wo, wo_other,
        w_up, up_y, w_down, first_y, second_y,
        scratch=[
            ((rows, 4 * width), bf16), ((4 * width, D), bf16), ((D, 2 * ff), bf16), ((2 * ff, D), bf16),
            ((rows, 2 * ff), bf16), ((rows, 2 * ff), bf16),
        ],
        name="feed",
    )
    d_h_two_other = swap_head(d_h_two, 1)
    d_middle, d_low, d_ctx, g_two = call(
        back_kernel,
        [((rows, D), f32), ((rows, D), bf16), ((rows, width), bf16), ((8, D), f32)],
        middle, d_h_two, d_h_two_other, cotangent, gain_ffn, w_out, name="back",
    )

    plans = [[(0, 0, rows)]] + [[(k, 0, rows), (-k, 0, rows)] for k in (1, 2, 3)]
    plans.append([(4, 0, half), (4, half, half)])
    offsets = (None, None, None, 0, 2 * blocks)
    pulled = []

    def pull(given):
        plan, offset = plans[len(pulled)], offsets[len(pulled)]
        n = sum(count for _, _, count in plan)
        pulled.append(
            call(
                functools.partial(pull_kernel, tuple(plan), offset),
                [((n, 4 * DH), f32), ((n, 6 * DH), bf16), ((n // BLOCK, 4 * DH), f32)],
                *given, qkv, partner_s, scale_rows, weight_rows,
                *([] if offset is None else [z_all, probs_all]),
                smem=(len(given) + 1,), name="pull",
            )
        )
        return pulled[-1][0]

    piece = (D + ff + width) // 8
    front = 80
    parts = call(
        grads_kernel,
        [((4 * piece, width), f32)] * 7
        + [((rows + 4 * front, width), bf16), ((rows + 4 * (piece - front), width), bf16)],
        h_two, d_hidden, active, cotangent, context, d_low, d_ctx,
        scratch=[((D, ff), f32), ((ff, D), f32), ((width, D), f32)], name="grads",
    )
    keeps, (x, y) = parts[:7], parts[7:]

    def relay(start, count, at, keep, arrived):
        return call(
            functools.partial(relay_kernel, start, count, at), [((count + 4 * piece, width), bf16)],
            keep, arrived, name="relay",
        )

    given = [d_ctx]
    for step in range(4):
        x, y = ahead(x), behind(y)
        done = pull(given)
        given = [x, y]
        if step == 0:
            joint_y = swap_head(after(joint, done), 2)
        hold = [joint_y] if step == 2 else []
        y = tie(y, done, *hold)[0]
        if step < 3:
            count = half if step == 2 else rows
            x = relay(0, count, 0, keeps[step], x)
            y = relay(rows - count, count, 0 if step else front, keeps[step + 3], y)
    owned = call(total_kernel, [((piece, D), bf16)], keeps[6], x, y, name="total")
    wf1, wb1 = ahead(owned), behind(owned)
    pull(given)

    spans = tuple(tuple(plan) for plan in plans)
    d_qkv, d_mine, flat_mine, g_sort = call(
        functools.partial(collect_kernel, spans),
        [
            ((total, 3 * width), bf16), ((rows, 3 * width), bf16), ((blocks, 2 * nb), f32), ((D, 2 * nb), f32),
        ],
        *[p[k] for k in range(3) for p in pulled], partner_s, partner_s, steps, summary, smem=(15,),
        scratch=[
            ((nb, 4 * DH), f32), ((total, 4 * DH), f32), ((total, 4 * DH), bf16), ((nb, 2 * nb), f32),
        ],
        name="collect",
    )
    wf1, wb1, d_mine, flat_mine = tie(wf1, wb1, d_mine, flat_mine)
    ffn_other = swap_head(after(ffn, d_mine), 1)
    output = call(add_kernel, [((rows, D), f32)], ffn, ffn_other, middle, name="output")
    wf2, wb2 = ahead(wf1), behind(wb1)
    d_mine_y, flat_y = swap_head(d_mine, 2), swap_head(flat_mine, 2)
    gains_a = call(
        gain_kernel, [((16, D), f32)], tokens, d_mine, flat_mine, joint, g_two, name="gain_part"
    )
    gains_x = swap_blk(gains_a, 1)
    gains = call(add_kernel, [((16, D), f32)], gains_a, gains_x, name="add_gains")
    wf2, wb2, gains, flat_y, d_mine_y = tie(wf2, wb2, gains, flat_y, d_mine_y)
    wf3, wb3 = ahead(wf2), behind(wb2)
    gains1 = swap_blk(gains, 2)
    gains = call(add_kernel, [((16, D), f32)], gains, gains1, name="add_gains")
    gains2 = swap_blk(gains, 4)
    d_h = call(
        input_kernel, [((rows, D), f32)],
        d_mine, d_mine_y, joint, joint_y, flat_mine, flat_y,
        scratch=[
            ((rows, 6 * width), bf16), ((D, 6 * width), bf16), ((blocks, 4 * nb), f32), ((D, 4 * nb), bf16),
        ],
        name="input_back",
    )
    d_h_other = swap_head(d_h, 1)
    g_qkv = call(
        weight_kernel, [((3, D, width), f32)],
        *mine[0], *[v for k in (1, 2, 3) for v in (*mine[k], *other[k - 1])], m4, o4, after(d_qkv, d_h),
        scratch=[((total, D), bf16)], limit=24, name="weights",
    )
    wf3, wb3, gains, gains2, g_qkv, d_h_other = tie(
        wf3, wb3, gains, gains2, g_qkv, d_h_other
    )
    cut_f, cut_b = call(
        cut_kernel, [((front, D), bf16), ((piece - front, D), bf16)], wf3, wb3, name="halve"
    )
    wf4, wb4 = ahead(cut_f), behind(cut_b)
    gains = call(add_kernel, [((16, D), f32)], gains, gains2, name="add_gains")
    gains_y = swap_head(gains, 2)
    d_tokens = call(
        end_kernel, [((rows, D), f32)],
        tokens, gain_attn, d_h, d_h_other, d_middle, name="norm_one_back",
    )
    gains = call(add_kernel, [((16, D), f32)], gains, gains_y, name="add_gains")
    gains_c = swap_head(gains, 1)
    g_up, g_down, g_out, g_one, g_two = call(
        lay_kernel,
        [((D, ff), f32), ((ff, D), f32), ((width, D), f32), ((D,), f32), ((D,), f32)],
        owned, wf1, wb1, wf2, wb2, wf3, wb3, wf4, wb4, gains, gains_c, name="lay",
    )
    return output, d_tokens, g_one, g_two, g_qkv.transpose(1, 0, 2), g_out, g_sort, g_up, g_down


def solution(mesh):
    in_specs = (
        P("blk", None),
        P(),
        P(),
        P(None, None, "head"),
        P("head", None),
        P(None, "head"),
        P(None, "head"),
        P("head", None),
        P("blk", "head", None),
        P(None, "head"),
        P("blk", None),
    )
    out_specs = (
        P("blk", None),
        P("blk", None),
        P(),
        P(),
        P(None, None, "head"),
        P("head", None),
        P(None, "head"),
        P(None, "head"),
        P("head", None),
    )
    plan = local_eight if mesh.shape["blk"] == 8 and mesh.shape["head"] == 4 else local
    return jax.shard_map(plan, mesh=mesh, in_specs=in_specs, out_specs=out_specs, check_vma=False)
```

```python
import functools
import math

import jax
import jax.numpy as jnp
from jax import lax
from jax.experimental import pallas as pl
from jax.experimental.pallas import tpu as pltpu
from jax.sharding import PartitionSpec as P

D = 512
DH = 64
BLOCK = 64
SINK = 8


EPS = 1e-05
TEMPER = 0.75
ROOT_HALF = 0.7071067811865476
INV_ROOT_TWO_PI = 0.3989422804014327
HIGHEST = lax.Precision.HIGHEST


def normalize(values, norm_gain):
    average = jnp.mean(values, -1, keepdims=True)
    centred = values - average
    inv_std = lax.rsqrt(jnp.mean(centred * centred, -1, keepdims=True) + EPS)
    normed = centred * inv_std
    return (normed * norm_gain, normed, inv_std)


def norm_back(d_out, normed, inv_std, norm_gain):
    d_normed = d_out * norm_gain
    return inv_std * (
        d_normed
        - jnp.mean(d_normed, -1, keepdims=True)
        - normed * jnp.mean(d_normed * normed, -1, keepdims=True)
    )


def log_total(values, axis):
    highest = jnp.max(values, axis=axis, keepdims=True)
    return highest + jnp.log(jnp.sum(jnp.exp(values - highest), axis=axis, keepdims=True))


def balancing_log_space(sort_logits):
    for sweep in range(SINK):
        sort_logits = sort_logits - log_total(sort_logits, 2)
        sort_logits = sort_logits - log_total(sort_logits, 1)
    return sort_logits


def gelu_value(values):
    return 0.5 * values * (1.0 + lax.erf(values * ROOT_HALF))


def gelu_slope(values):
    return (
        0.5 * (1.0 + lax.erf(values * ROOT_HALF))
        + values * jnp.exp(-0.5 * values * values) * INV_ROOT_TWO_PI
    )


def local(
    tokens,
    gain_attn,
    gain_ffn,
    w_qkv,
    w_out,
    w_sort,
    w_up,
    w_down,
    gumbel_noise,
    partner,
    cotangent,
):
    f32 = jnp.float32
    bf16 = jnp.bfloat16
    tok_rows = tokens.shape[0]
    blocks_dev = tok_rows // BLOCK
    heads_dev = w_out.shape[0] // DH
    width_dev = heads_dev * DH
    requests = blocks_dev * heads_dev
    dev_count = lax.axis_size("blk")
    my_index = lax.axis_index("blk")
    first_block = my_index * blocks_dev
    seq_blocks = partner.shape[0]
    scale = DH ** (-0.5)
    gain_one = gain_attn.astype(f32)
    gain_two = gain_ffn.astype(f32)
    inputs = tokens.astype(f32)
    h_one, normed_one, inv_one = normalize(inputs, gain_one)
    h_one_low = h_one.astype(bf16)
    qkv = jnp.einsum("td,dcf->tcf", h_one_low, w_qkv, preferred_element_type=f32).astype(bf16)
    summary = jnp.mean(h_one.reshape(blocks_dev, BLOCK, D), axis=1)
    sort_mat = w_sort.astype(f32)
    own_rows = (
        jnp.dot(summary, sort_mat, precision=HIGHEST).reshape(blocks_dev, heads_dev, seq_blocks)
        + gumbel_noise
    ) / TEMPER
    every_rows = lax.all_gather(own_rows, "blk", axis=0, tiled=True)
    my_partner = lax.dynamic_slice_in_dim(partner, first_block, blocks_dev, 0)

    def own_weights(sequence_rows):
        balanced_plan = balancing_log_space(sequence_rows.transpose(1, 0, 2))
        mine = lax.dynamic_slice_in_dim(jnp.exp(balanced_plan), first_block, blocks_dev, 1)
        return seq_blocks * jnp.take_along_axis(mine, my_partner.T[:, :, None], axis=2)[:, :, 0]

    weight_hb, sink_pull = jax.vjp(own_weights, every_rows)
    weight_matrix = weight_hb.T
    owner_all = (partner // blocks_dev).reshape(dev_count, requests)
    slot_all = (
        partner % blocks_dev * heads_dev + jnp.arange(heads_dev, dtype=jnp.int32)[None, :]
    ).reshape(dev_count, requests)
    owner_mine = lax.dynamic_index_in_dim(owner_all, my_index, 0, keepdims=False)
    tile_ids = jnp.arange(requests, dtype=jnp.int32)
    key_value = (
        qkv[:, 1:3]
        .reshape(blocks_dev, BLOCK, 2, heads_dev, DH)
        .transpose(0, 3, 1, 2, 4)
        .reshape(requests, BLOCK, 2 * DH)
    )
    empty_tile = jnp.zeros((), bf16)
    wanted = owner_all == my_index
    outgoing = jnp.where(
        wanted[:, :, None, None], jnp.take(key_value, slot_all, axis=0), empty_tile
    )
    incoming = lax.all_to_all(outgoing, "blk", split_axis=0, concat_axis=0, tiled=True)
    partner_tiles = jnp.sum(incoming, axis=0, dtype=f32).astype(bf16)
    far_tiles = partner_tiles.reshape(blocks_dev, heads_dev, BLOCK, 2, DH)
    key_far = far_tiles[:, :, :, 0]
    value_far = far_tiles[:, :, :, 1]
    query_b = qkv[:, 0].reshape(blocks_dev, BLOCK, heads_dev, DH)
    key_b = qkv[:, 1].reshape(blocks_dev, BLOCK, heads_dev, DH)
    value_b = qkv[:, 2].reshape(blocks_dev, BLOCK, heads_dev, DH)
    weight_s = weight_matrix[:, :, None, None]

    def score_parts():
        near_z = scale * jnp.einsum("bqhd,bkhd->bhqk", query_b, key_b, preferred_element_type=f32)
        far_z = scale * jnp.einsum("bqhd,bhkd->bhqk", query_b, key_far, preferred_element_type=f32)
        return (near_z, far_z, jnp.concatenate([near_z, weight_s * far_z], -1))

    near_z, far_z, scores = score_parts()
    highest = jnp.max(scores, -1, keepdims=True)
    expo = jnp.exp(scores - highest)
    row_total = jnp.sum(expo, -1, keepdims=True)
    log_sum = highest + jnp.log(row_total)
    probs_low = (expo / row_total).astype(bf16)
    near_ctx = jnp.einsum(
        "bhqk,bkhd->bqhd", probs_low[..., :BLOCK], value_b, preferred_element_type=f32
    )
    far_ctx = jnp.einsum(
        "bhqk,bhkd->bqhd", probs_low[..., BLOCK:], value_far, preferred_element_type=f32
    )
    context = near_ctx + weight_matrix[:, None, :, None] * far_ctx
    context_low = context.reshape(tok_rows, width_dev).astype(bf16)
    attn = lax.psum(jnp.dot(context_low, w_out, preferred_element_type=f32), "head")
    middle = inputs + attn
    h_two, normed_two, inv_two = normalize(middle, gain_two)
    h_two_low = h_two.astype(bf16)
    hidden_pre = jnp.dot(h_two_low, w_up, preferred_element_type=f32)
    active_low = gelu_value(hidden_pre).astype(bf16)
    ffn = lax.psum(
        jnp.dot(active_low, w_down, preferred_element_type=f32).astype(jnp.bfloat16), "head"
    ).astype(jnp.float32)
    output = middle + ffn
    g_down = jnp.einsum("tf,td->fd", active_low, cotangent, preferred_element_type=f32)
    d_active = jnp.einsum("td,fd->tf", cotangent, w_down, preferred_element_type=f32)
    d_hidden = (d_active * gelu_slope(hidden_pre)).astype(bf16)
    g_up = jnp.einsum("td,tf->df", h_two_low, d_hidden, preferred_element_type=f32)
    d_h_two = lax.psum(jnp.einsum("tf,df->td", d_hidden, w_up, preferred_element_type=f32), "head")
    g_gain_two = jnp.sum(d_h_two * normed_two, 0)
    d_middle = cotangent.astype(f32) + norm_back(d_h_two, normed_two, inv_two, gain_two)
    d_attn_low = d_middle.astype(bf16)
    g_out = jnp.einsum("tf,td->fd", context_low, d_attn_low, preferred_element_type=f32)
    d_context = jnp.einsum("td,fd->tf", d_attn_low, w_out, preferred_element_type=f32).astype(bf16)
    d_context = d_context.reshape(blocks_dev, BLOCK, heads_dev, DH)
    near_z, far_z, scores = score_parts()
    probs = jnp.exp(scores - log_sum)
    probs_low = probs.astype(bf16)
    far_ctx = jnp.einsum(
        "bhqk,bhkd->bqhd", probs_low[..., BLOCK:], value_far, preferred_element_type=f32
    )
    d_probs_near = jnp.einsum("bqhd,bkhd->bhqk", d_context, value_b, preferred_element_type=f32)
    d_probs_far = weight_s * jnp.einsum(
        "bqhd,bhkd->bhqk", d_context, value_far, preferred_element_type=f32
    )
    d_probs = jnp.concatenate([d_probs_near, d_probs_far], -1)
    d_scores = probs * (d_probs - jnp.sum(d_probs * probs, -1, keepdims=True))
    d_near = d_scores[..., :BLOCK].astype(bf16)
    d_far_raw = d_scores[..., BLOCK:]
    d_far = (weight_s * d_far_raw).astype(bf16)
    d_weight = jnp.sum(d_far_raw * far_z, (2, 3)) + jnp.sum(d_context.astype(f32) * far_ctx, (1, 3))
    d_query = scale * (
        jnp.einsum("bhqk,bkhd->bqhd", d_near, key_b, preferred_element_type=f32)
        + jnp.einsum("bhqk,bhkd->bqhd", d_far, key_far, preferred_element_type=f32)
    )
    d_key = scale * jnp.einsum("bhqk,bqhd->bkhd", d_near, query_b, preferred_element_type=f32)
    d_value = jnp.einsum(
        "bhqk,bqhd->bkhd", probs_low[..., :BLOCK], d_context, preferred_element_type=f32
    )
    d_key_far = scale * jnp.einsum("bhqk,bqhd->bhkd", d_far, query_b, preferred_element_type=f32)
    d_value_far = weight_s * jnp.einsum(
        "bhqk,bqhd->bhkd", probs_low[..., BLOCK:], d_context, preferred_element_type=f32
    )
    grad_tiles = jnp.stack([d_key_far.astype(bf16), d_value_far.astype(bf16)], 3).reshape(
        requests, BLOCK * 2 * DH
    )
    peers = jnp.arange(dev_count, dtype=jnp.int32)
    outgoing_grads = jnp.where(
        (owner_mine[None, :] == peers[:, None])[:, :, None], grad_tiles[None], empty_tile
    )
    returned = lax.all_to_all(outgoing_grads, "blk", split_axis=0, concat_axis=0, tiled=True)
    selector = (owner_all == my_index)[:, :, None] & (
        slot_all[:, :, None] == tile_ids[None, None, :]
    )
    selector = selector.reshape(dev_count * requests, requests).astype(bf16)
    remote = jnp.einsum(
        "st,sf->tf",
        selector,
        returned.reshape(dev_count * requests, BLOCK * 2 * DH),
        preferred_element_type=f32,
    )
    remote = (
        remote.reshape(blocks_dev, heads_dev, BLOCK, 2, DH)
        .transpose(0, 2, 3, 1, 4)
        .reshape(tok_rows, 2, width_dev)
    )
    near_kv = (
        jnp.stack([d_key.reshape(tok_rows, width_dev), d_value.reshape(tok_rows, width_dev)], 1)
        + remote
    )
    d_qkv = jnp.concatenate([d_query.reshape(tok_rows, 1, width_dev), near_kv], 1).astype(bf16)
    g_qkv = jnp.einsum("td,tcf->dcf", h_one_low, d_qkv, preferred_element_type=f32)
    d_h_part = jnp.einsum("tcf,dcf->td", d_qkv, w_qkv, preferred_element_type=f32)
    (d_every,) = sink_pull(d_weight.T)
    d_own = lax.psum_scatter(d_every, "blk", scatter_dimension=0, tiled=True) / TEMPER
    d_flat = d_own.reshape(blocks_dev, heads_dev * seq_blocks)
    g_sort = jnp.dot(summary.T, d_flat, precision=HIGHEST)
    d_summary = jnp.dot(d_flat, sort_mat.T, precision=HIGHEST)
    d_h_part = (d_h_part.reshape(blocks_dev, BLOCK, D) + d_summary[:, None, :] / BLOCK).reshape(
        tok_rows, D
    )
    d_h_one = lax.psum(d_h_part, "head")
    g_gain_one = jnp.sum(d_h_one * normed_one, 0)
    d_tokens = d_middle + norm_back(d_h_one, normed_one, inv_one, gain_one)
    summed = lax.psum((g_gain_one, g_gain_two, g_qkv, g_out, g_sort, g_up, g_down), "blk")
    return (
        output,
        d_tokens,
        summed[0],
        summed[1],
        summed[2],
        summed[3],
        summed[4],
        summed[5],
        summed[6],
    )


def mask_pair(values, near):
    zero = jnp.zeros_like(values)
    return jnp.where(near, values, zero), jnp.where(near, zero, values)


def first_lanes():
    return lax.broadcasted_iota(jnp.int32, (1, 2 * DH), 1) < DH


def dot_nn(a, b):
    return lax.dot_general(a, b, (((1,), (0,)), ((), ())), preferred_element_type=jnp.float32)


def dot_nt(a, b):
    return lax.dot_general(a, b, (((1,), (1,)), ((), ())), preferred_element_type=jnp.float32)


def dot_tn(a, b):
    return lax.dot_general(a, b, (((0,), (0,)), ((), ())), preferred_element_type=jnp.float32)


def three_parts(values):
    high = values.astype(jnp.bfloat16)
    rest = values - high.astype(jnp.float32)
    mid = rest.astype(jnp.bfloat16)
    low = (rest - mid.astype(jnp.float32)).astype(jnp.bfloat16)
    return high, mid, low


def norm_parts(values):
    centred = values - jnp.mean(values, -1, keepdims=True)
    inv_std = lax.rsqrt(jnp.mean(centred * centred, -1, keepdims=True) + EPS)
    return centred * inv_std, inv_std


def noise_rows(noise):
    few = noise.shape[0] // 2
    return [
        jnp.concatenate([noise[r * few + i, h : h + 1, :] for i in range(few) for h in range(2)], 1)
        for r in range(2)
    ]


def head_kernel(tokens, gain, noise, other_noise, first, second, summary, own_noise):
    f32, bf16 = jnp.float32, jnp.bfloat16
    rows = tokens.shape[0]
    half = rows // 2
    core = lax.axis_index("head") % 2
    normed, _ = norm_parts(tokens[...].astype(f32))
    h = normed * gain[...].astype(f32)
    low = h.astype(bf16)
    means = jnp.mean(h.reshape(rows // BLOCK, BLOCK, D), axis=1)
    summary[...] = means
    mine = jnp.concatenate(noise_rows(noise), 0)
    other = jnp.concatenate(noise_rows(other_noise), 0)
    own_noise[...] = mine
    both = jnp.where(
        core == 0, jnp.concatenate([mine, other], 0), jnp.concatenate([other, mine], 0)
    )
    few = means.shape[0] // 2
    for k, ref in enumerate((first, second)):
        ref[:half, :] = low[k * half : (k + 1) * half, :]
        parts = [p.astype(f32) for p in three_parts(means[k * few : (k + 1) * few, :])]
        parts += [p.astype(f32) for p in three_parts(both)] if k else [jnp.zeros((12, D), f32)]
        parts.append(jnp.zeros((EXTRA - 24, D), f32))
        ref[half:, :] = jnp.concatenate(parts, 0).astype(bf16)


def project_rows(rows, joint):
    return dot_nn(rows, joint[:, : 6 * DH]).astype(jnp.bfloat16)


def project_own_kernel(h_first, h_second, weight, w_sort, w_out, down, out, joint, first, second):
    width = w_out.shape[0]
    more = first.shape[0] - width
    first[:width, :] = w_out[...]
    first[width:, :] = down[:more, :]
    second[...] = down[more:, :]
    joint[...] = jnp.concatenate([weight[i] for i in range(3)] + [w_sort[...]], 1)
    project_half(h_first, joint, out, 0)
    project_half(h_second, joint, out, h_first.shape[0] - EXTRA)


def project_half(piece, joint, out, to):
    for start in range(0, piece.shape[0] - EXTRA, 2 * BLOCK):
        rows = project_rows(piece[start : start + 2 * BLOCK, :], joint)
        out[to + start : to + start + 2 * BLOCK, :] = rows


def project_kernel(mine1, mine2, other1, other2, joint, out, extra):
    half = mine1.shape[0] - EXTRA
    for k, piece in enumerate((mine1, mine2, other1, other2)):
        project_half(piece, joint, out, k * half)
        extra[k * EXTRA : (k + 1) * EXTRA, :] = piece[half:, :]


def half_kernel(first, second, w_out, w_out_y, half, pair):
    width = w_out.shape[0]
    even = lax.axis_index("head") % 2 == 0
    half[...] = jnp.where(even, first[...], second[...])
    pair[:width, :] = w_out[...]
    pair[width:, :] = w_out_y[:width, :]


def turn():
    return 1 - 2 * (lax.axis_index("head") % 2)


def owners_of(step):
    place = place_of(lax.axis_index("blk"))
    core = lax.axis_index("head") % 2
    way = jnp.where(core == 0, 8 - step, step)
    return ring_of((place + way) % 8), ring_of((place + 8 - way) % 8)


def ring_of(position):
    return jnp.where(position < 4, 2 * position, 2 * (7 - position) + 1)


def place_of(index):
    return jnp.where(index % 2 == 0, index // 2, 7 - index // 2)


def far_near(table, at, lanes):
    return table[pl.ds(pl.multiple_of(at * BLOCK, BLOCK), BLOCK), lanes]


def block_operands(qkv, block, first, second, near):
    k_lanes, v_lanes = slice(2 * DH, 4 * DH), slice(4 * DH, 6 * DH)
    query = far_near(qkv, block, slice(0, 2 * DH))
    keys, values = [], []
    for lanes, store in ((k_lanes, keys), (v_lanes, values)):
        own0, own1 = mask_pair(far_near(qkv, block, lanes), near)
        far0, _ = mask_pair(far_near(qkv, first, lanes), near)
        _, far1 = mask_pair(far_near(qkv, second, lanes), near)
        store.extend([own0, far0, own1, far1])
    return query, keys, values


def block_probs(scores):
    probs = []
    for h in range(2):
        part = scores[:, h * 2 * DH : (h + 1) * 2 * DH]
        expo = jnp.exp(part - jnp.max(part, -1, keepdims=True))
        probs.append(expo / jnp.sum(expo, -1, keepdims=True))
    return probs


def choices(partner, h):
    nb = partner.shape[1]
    sides = lax.broadcasted_iota(jnp.int32, (nb, nb), 0)
    hot = (sides == partner[h : h + 1, :]).astype(jnp.bfloat16)
    same = sides == lax.broadcasted_iota(jnp.int32, (nb, nb), 1)
    return dot_nt(same.astype(jnp.bfloat16), hot)


def joined(rows, at, count):
    parts = [rows[at + k * count : at + (k + 1) * count, :].astype(jnp.float32) for k in range(3)]
    return (parts[0] + parts[1]) + parts[2]


def attend_kernel(
    own, step1, step2, step3, extra1, extra2, extra3, mine4, other4, joint, own_summary, own_noise,
    partner, partner_rows, qkv, context, summary, steps, scale_rows, weight_rows, noise,
):
    f32, bf16 = jnp.float32, jnp.bfloat16
    me = lax.axis_index("blk")
    core = lax.axis_index("head") % 2
    nb = partner_rows.shape[1]
    rows = own.shape[0]
    half = rows // 2
    blocks = rows // BLOCK
    few = blocks // 2

    def put(owner, start, values):
        n = values.shape[0]
        qkv[pl.ds(pl.multiple_of(owner * rows + start, n), n), :] = values

    def put_noise(owner, values):
        lines = [
            values[r : r + 1, i * 2 * nb : (i + 1) * 2 * nb] for r in range(2) for i in range(few)
        ]
        at = pl.multiple_of(owner * blocks, blocks)
        noise[pl.ds(at, blocks), :] = jnp.concatenate(lines, 0)

    def put_extra(owner, first, second):
        at = pl.multiple_of(owner * blocks, blocks)
        summary[pl.ds(at, blocks), :] = jnp.concatenate(
            [joined(first, 0, few), joined(second, 0, few)], 0
        )
        both = joined(second, 3 * few, 4)
        put_noise(owner, jnp.where(core == 0, both[:2], both[2:]))

    put(me, 0, own[...])
    summary[pl.ds(pl.multiple_of(me * blocks, blocks), blocks), :] = own_summary[...]
    put_noise(me, own_noise[...])
    for step, ref, extra in ((1, step1, extra1), (2, step2, extra2), (3, step3, extra3)):
        for k, owner in enumerate(owners_of(step)):
            put(owner, 0, ref[k * rows : (k + 1) * rows, :])
            at = 2 * k * EXTRA
            put_extra(owner, extra[at : at + EXTRA, :], extra[at + EXTRA : at + 2 * EXTRA, :])
    owner, _ = owners_of(4)
    for side, ref in ((core, mine4), (1 - core, other4)):
        for start in range(0, half, 2 * BLOCK):
            values = project_rows(ref[start : start + 2 * BLOCK, :], joint)
            put(owner, side * half + start, values)
    ends = [ref[half:, :].astype(f32) for ref in (mine4, other4)]
    put_extra(
        owner, jnp.where(core == 0, ends[0], ends[1]), jnp.where(core == 0, ends[1], ends[0])
    )

    parts = three_parts(summary[...])
    logits = sum(dot_nn(part, joint[:, 6 * DH :]) for part in parts[::-1])
    logits = (logits + noise[...]) / TEMPER
    plan = jnp.stack([logits[:, :nb], logits[:, nb:]])
    for sweep in range(SINK):
        for k, axis in enumerate((2, 1)):
            plan = plan - log_total(plan, axis)
            steps[2 * sweep + k] = jnp.exp(plan)
    final = jnp.exp(plan)
    picked = []
    for h in range(2):
        picked.append(nb * jnp.sum(choices(partner_rows, h) * final[h], axis=1, keepdims=True))
    ones = jnp.ones((nb, DH), f32)
    scale_rows[...] = jnp.concatenate([ones, picked[0] * ones, ones, picked[1] * ones], 1)
    weight_rows[...] = jnp.concatenate([picked[0] * ones, picked[1] * ones], 1)

    near = first_lanes()
    work = []
    for i in range(blocks):
        block = me * blocks + i
        query, keys, values = block_operands(
            qkv, block, partner[0, block], partner[1, block], near
        )
        none = jnp.zeros_like(values[0])
        table = jnp.concatenate(
            [
                jnp.concatenate([values[0], none, values[2], none], 0),
                jnp.concatenate([none, values[1], none, values[3]], 0),
            ],
            1,
        )
        z = dot_nt(query, jnp.concatenate(keys, 0)) * (DH**-0.5)
        work.append((block, z, table))
    probs = [block_probs(z * scale_rows[pl.ds(block, 1), :]) for block, z, _ in work]
    outs = [
        dot_nn(jnp.concatenate([p.astype(bf16) for p in prob], 1), table)
        for prob, (_, _, table) in zip(probs, work)
    ]
    for i, (out, (block, _, _)) in enumerate(zip(outs, work)):
        ctx = out[:, : 2 * DH] + weight_rows[pl.ds(block, 1), :] * out[:, 2 * DH :]
        context[i * BLOCK : (i + 1) * BLOCK, :] = ctx.astype(bf16)


def feed_kernel(
    tokens, cotangent, gain, ctx0, ctx1, ctx2, ctx3, wo, wo_other, up_a, up_b, down_a, first, second,
    middle, h_two, active, d_hidden, ffn, d_h_two,
    ctx_full, wo_full, up_full, down_full, act_full, d_full,
):
    f32, bf16 = jnp.float32, jnp.bfloat16
    hd = lax.axis_index("head")
    row = hd // 2
    width = ctx0.shape[1]
    ff = up_a.shape[1]
    for j, c in enumerate((ctx0, ctx1, ctx2, ctx3)):
        at = pl.multiple_of((hd ^ j) * width, width)
        ctx_full[:, pl.ds(at, width)] = c[...]
        w = wo if j % 2 == 0 else wo_other
        wo_full[pl.ds(at, width), :] = w[j // 2 * width : (j // 2 + 1) * width, :]
    here, there = (pl.multiple_of((row ^ j) * ff, ff) for j in range(2))
    up_full[:, pl.ds(here, ff)] = up_a[...]
    up_full[:, pl.ds(there, ff)] = up_b[...]
    down_full[pl.ds(here, ff), :] = down_a[...]
    more = first.shape[0] - width
    down_full[pl.ds(there, more), :] = first[width:, :]
    down_full[pl.ds(pl.multiple_of(there + more, 32), ff - more), :] = second[...]
    chunk = 256
    for start in range(0, tokens.shape[0], chunk):
        sl = slice(start, start + chunk)
        mid = tokens[sl, :].astype(f32) + dot_nn(ctx_full[sl, :], wo_full[...])
        middle[sl, :] = mid
        normed, _ = norm_parts(mid)
        low = (normed * gain[...].astype(f32)).astype(bf16)
        h_two[sl, :] = low
        ffn_sum = None
        back_sum = None
        for j in range(2):
            cols = slice(j * ff, (j + 1) * ff)
            pre = dot_nn(low, up_full[:, cols])
            d_act = dot_nt(cotangent[sl, :], down_full[cols, :])
            bell = 0.5 * (1.0 + lax.erf(pre * ROOT_HALF))
            act = (pre * bell).astype(bf16)
            slope = bell + pre * jnp.exp(-0.5 * pre * pre) * INV_ROOT_TWO_PI
            d_pre = (d_act * slope).astype(bf16)
            act_full[sl, cols] = act
            d_full[sl, cols] = d_pre
            f = dot_nn(act, down_full[cols, :])
            b = dot_nt(d_pre, up_full[:, cols])
            ffn_sum = f if ffn_sum is None else ffn_sum + f
            back_sum = b if back_sum is None else back_sum + b
        ffn[sl, :] = ffn_sum
        d_h_two[sl, :] = back_sum
    mine = pl.ds(pl.multiple_of(row * ff, ff), ff)
    active[...] = act_full[:, mine]
    d_hidden[...] = d_full[:, mine]


def back_kernel(middle, own, other, cotangent, gain, w_out, d_middle, d_low, d_ctx, g_gain):
    f32, bf16 = jnp.float32, jnp.bfloat16
    normed, inv = norm_parts(middle[...])
    d_h = own[...] + other[...]
    g_gain[...] = jnp.broadcast_to(jnp.sum(d_h * normed, 0, keepdims=True), g_gain.shape)
    d_mid = cotangent[...].astype(f32) + norm_back(d_h, normed, inv, gain[...].astype(f32))
    d_middle[...] = d_mid
    low = d_mid.astype(bf16)
    d_low[...] = low
    d_ctx[...] = dot_nt(low, w_out[...]).astype(bf16)


def stacked(rows):
    return jnp.concatenate([rows[:, k * 2 * DH : (k + 1) * 2 * DH] for k in range(D // (2 * DH))], 0)


def grads_kernel(h_two, d_hidden, active, cotangent, context, d_low, d_ctx, *refs):
    keeps, (ahead, behind), (up, down, out) = refs[:7], refs[7:9], refs[9:]
    place = place_of(lax.axis_index("blk"))
    up[...] = dot_tn(h_two[...], d_hidden[...])
    down[...] = dot_tn(active[...], cotangent[...])
    out[...] = dot_tn(context[...], d_low[...])

    def rows_of(distance):
        owner = ring_of((place + turn() * distance + 8) % 8)
        parts = []
        for ref in (up, down, out):
            n = ref.shape[0] // 8
            parts.append(ref[pl.ds(pl.multiple_of(owner * n, n), n), :])
        return jnp.concatenate(parts, 0)

    for ref, distance in zip(keeps, (3, 2, 1, -3, -2, -1, 0)):
        ref[...] = stacked(rows_of(distance))
    last = rows_of(4).astype(jnp.bfloat16)
    rows = d_ctx.shape[0]
    n = (ahead.shape[0] - rows) // 4
    for ref, part in ((ahead, last[:n]), (behind, last[n:])):
        ref[:rows, :] = d_ctx[...]
        ref[rows:, :] = stacked(part)


def relay_kernel(start, count, at, keep, arrived, out):
    f32, bf16 = jnp.float32, jnp.bfloat16
    size = keep.shape[0] // 4
    n = (arrived.shape[0] - SHARD) // 4
    out[:count, :] = arrived[start : start + count, :]
    out[count:, :] = keep[...].astype(bf16)
    for k in range(4):
        here = slice(k * size + at, k * size + at + n)
        total = keep[here, :] + arrived[SHARD + k * n : SHARD + (k + 1) * n, :].astype(f32)
        out[count + k * size + at : count + k * size + at + n, :] = total.astype(bf16)


def total_kernel(keep, x, y, out):
    f32 = jnp.float32
    size = keep.shape[0] // 4
    skip = x.shape[0] - 4 * size
    for k in range(4):
        rows = slice(k * size, (k + 1) * size)
        there = slice(skip + k * size, skip + (k + 1) * size)
        total = keep[rows, :] + (x[there, :].astype(f32) + y[there, :].astype(f32))
        out[:, k * 2 * DH : (k + 1) * 2 * DH] = total.astype(jnp.bfloat16)


def cut_kernel(f, b, front, back):
    front[...] = f[: front.shape[0], :]
    back[...] = b[b.shape[0] - back.shape[0] :, :]


def lay_kernel(own, f1, b1, f2, b2, f3, b3, f4, b4, gains, other, g_up, g_down, g_out, g_one, g_two):
    f32 = jnp.float32
    total = gains[...] + other[...]
    g_one[...] = total[0, :]
    g_two[...] = total[8, :]
    place = place_of(lax.axis_index("blk"))
    last = jnp.concatenate([f4[...], b4[...]], 0)
    for distance, piece in (
        (0, own[...]), (-1, f1[...]), (1, b1[...]), (-2, f2[...]), (2, b2[...]), (-3, f3[...]), (3, b3[...]),
        (4, last),
    ):
        owner = ring_of((place + turn() * distance + 8) % 8)
        start = 0
        for ref in (g_up, g_down, g_out):
            n = ref.shape[0] // 8
            ref[pl.ds(pl.multiple_of(owner * n, n), n), :] = piece[start : start + n].astype(f32)
            start += n


def halve_kernel(f, b, front, back):
    n = front.shape[0]
    front[...] = f[:n, :]
    back[...] = b[n:, :]


def add_kernel(*refs):
    *terms, out = refs
    total = terms[0][...]
    for term in terms[1:]:
        total = total + term[...]
    out[...] = total


def four_kernel(here, one, two, three, out):
    out[...] = (here[...] + one[...]) + (two[...] + three[...])


def block_at(place, step, start, i):
    return ring_of((place + 8 - turn() * step) % 8) * (SHARD // BLOCK) + start // BLOCK + i


def prepare_kernel(pieces, qkv, partner, scale_rows, z_out, probs_out):
    place = place_of(lax.axis_index("blk"))
    near = first_lanes()
    blocks = [(step, start, i) for step, start, n in pieces for i in range(n // BLOCK)]
    for first in range(0, len(blocks), 8):
        work = []
        for step, start, i in blocks[first : first + 8]:
            block = block_at(place, step, start, i)
            query, keys, _ = block_operands(qkv, block, partner[0, block], partner[1, block], near)
            work.append((query, jnp.concatenate(keys, 0), scale_rows[pl.ds(block, 1), :]))
        z = [dot_nt(query, keys) * (DH**-0.5) for query, keys, _ in work]
        probs = [block_probs(v * w[2]) for v, w in zip(z, work)]
        for k in range(len(work)):
            at = slice((first + k) * BLOCK, (first + k + 1) * BLOCK)
            z_out[at, :] = z[k]
            probs_out[at, :] = jnp.concatenate(probs[k], 1)


def pull_kernel(pieces, offset, *refs):
    f32, bf16 = jnp.float32, jnp.bfloat16
    count = len(pieces)
    outs, refs = refs[:count], refs[count:]
    qkv, partner, scale_rows, weight_rows, refs = *refs[:4], refs[4:]
    if offset is not None:
        z_all, probs_all, refs = refs[0], refs[1], refs[2:]
    near_out, low_out, d_weight = refs
    place = place_of(lax.axis_index("blk"))
    near = first_lanes()
    scale = DH**-0.5
    blocks = [
        (step, start, d_ctx, i)
        for (step, start, n), d_ctx in zip(pieces, outs)
        for i in range(n // BLOCK)
    ]
    for first in range(0, len(blocks), 8):
        work = []
        for k, (step, start, d_ctx, i) in enumerate(blocks[first : first + 8]):
            block = block_at(place, step, start, i)
            query, keys, values = block_operands(
                qkv, block, partner[0, block], partner[1, block], near
            )
            w = dict(
                query=query,
                keys=jnp.concatenate(keys, 0),
                values=jnp.concatenate(values, 0),
                scale=scale_rows[pl.ds(block, 1), :],
                weight=weight_rows[pl.ds(block, 1), :],
                d_out=d_ctx[i * BLOCK : (i + 1) * BLOCK, :],
            )
            if offset is not None:
                at = slice((offset + first + k) * BLOCK, (offset + first + k + 1) * BLOCK)
                w["z"] = z_all[at, :]
                w["probs"] = [probs_all[at, : 2 * DH], probs_all[at, 2 * DH :]]
            work.append(w)
        if offset is None:
            for w in work:
                w["z"] = dot_nt(w["query"], w["keys"]) * scale
        for w in work:
            w["raw"] = dot_nt(w["d_out"], w["values"])
        if offset is None:
            for w in work:
                w["probs"] = block_probs(w["z"] * w["scale"])
        for w in work:
            d_z, low, d_w = [], [], []
            for h in range(2):
                sl = slice(h * 2 * DH, (h + 1) * 2 * DH)
                probs = w["probs"][h]
                d_probs = w["raw"][:, sl] * w["scale"][:, sl]
                d_scores = probs * (d_probs - jnp.sum(d_probs * probs, -1, keepdims=True))
                d_z.append((d_scores * w["scale"][:, sl]).astype(bf16))
                low.append(probs.astype(bf16))
                d_w.append(
                    jnp.sum(
                        d_scores * w["z"][:, sl] + low[h].astype(f32) * w["raw"][:, sl],
                        0,
                        keepdims=True,
                    )
                )
            w["d_z"], w["low"] = jnp.concatenate(d_z, 1), jnp.concatenate(low, 1)
            w["d_w"] = jnp.concatenate(d_w, 1)
        for w in work:
            w["d_query"] = dot_nn(w["d_z"], w["keys"]) * scale
        for w in work:
            w["d_keys"] = dot_tn(w["d_z"], w["query"]) * scale
        for w in work:
            w["d_values"] = dot_tn(w["low"], w["d_out"])
        for k, w in enumerate(work):
            to = first + k
            at = slice(to * BLOCK, (to + 1) * BLOCK)
            d_weight[to : to + 1, :] = w["d_w"]
            low_out[at, : 2 * DH] = w["d_query"].astype(bf16)
            for m, name in enumerate(("d_keys", "d_values")):
                parts = [w[name][i * BLOCK : (i + 1) * BLOCK, :] for i in range(4)]
                near_out[at, m * 2 * DH : (m + 1) * 2 * DH] = jnp.where(near, parts[0], parts[2])
                far = jnp.where(near, parts[1], parts[3])
                if m == 1:
                    far = far * w["weight"]
                low_out[at, (m + 1) * 2 * DH : (m + 2) * 2 * DH] = far.astype(bf16)


def collect_kernel(pieces, *refs):
    f32, bf16 = jnp.float32, jnp.bfloat16
    count = len(pieces)
    nears, lows, d_weights = refs[:count], refs[count : 2 * count], refs[2 * count : 3 * count]
    partner, partner_rows, steps, summary = refs[3 * count : 3 * count + 4]
    d_qkv, d_mine, flat_mine, g_sort, d_weight, acc, far, d_flat = refs[3 * count + 4 :]
    me = lax.axis_index("blk")
    place = place_of(me)
    for parts, near_ref, low_ref, w_ref in zip(pieces, nears, lows, d_weights):
        at = 0
        for step, start, n in parts:
            owner = ring_of((place + 8 - turn() * step) % 8)
            to = pl.ds(pl.multiple_of(owner * SHARD + start, n), n)
            acc[to, :] = near_ref[at : at + n, :]
            far[to, :] = low_ref[at : at + n, 2 * DH :]
            d_qkv[to, : 2 * DH] = low_ref[at : at + n, : 2 * DH]
            if start == 0:
                nb = SHARD // BLOCK
                first = pl.multiple_of(owner * nb, nb)
                d_weight[pl.ds(first, nb), :] = w_ref[at // BLOCK : at // BLOCK + nb, :]
            at += n
    near = first_lanes()
    both = jnp.concatenate([near, near], 1)

    def body(block, _):
        tile = far[pl.ds(pl.multiple_of(block * BLOCK, BLOCK), BLOCK), :].astype(f32)
        for h, kept in ((0, jnp.where(both, tile, 0.0)), (1, jnp.where(both, 0.0, tile))):
            to = pl.ds(pl.multiple_of(partner[h, block] * BLOCK, BLOCK), BLOCK)
            acc[to, :] += kept
        return 0

    lax.fori_loop(0, partner.shape[1], body, 0, unroll=4)
    d_qkv[:, 2 * DH :] = acc[...].astype(bf16)
    d_mine[...] = d_qkv[pl.ds(pl.multiple_of(me * SHARD, SHARD), SHARD), :]
    d_flat[...] = sink_back(d_weight[...], steps, partner_rows)
    n = flat_mine.shape[0]
    flat_mine[...] = d_flat[pl.ds(pl.multiple_of(me * n, n), n), :]
    g_sort[...] = lax.dot_general(
        summary[...],
        d_flat[...],
        (((0,), (0,)), ((), ())),
        precision=HIGHEST,
        preferred_element_type=f32,
    )


def sink_back(d_weight, steps, partner):
    nb = partner.shape[1]
    grads = []
    for h in range(2):
        total = jnp.sum(
            d_weight[:, (2 * h + 1) * DH : (2 * h + 2) * DH], axis=1, keepdims=True
        )
        grads.append(choices(partner, h) * (nb * total))
    last = steps.shape[0] - 1
    grad = jnp.stack(grads) * steps[last]
    for t in range(last, -1, -1):
        grad = grad - steps[t] * jnp.sum(grad, axis=1 if t % 2 else 2, keepdims=True)
    return jnp.concatenate([grad[0], grad[1]], 1) / TEMPER


def weight_kernel(*refs):
    *halves, d_qkv, g_qkv, h_all = refs
    me = lax.axis_index("blk")
    core = lax.axis_index("head") % 2
    half = halves[0].shape[0] - EXTRA
    rows = 2 * half

    def put(owner, side, ref):
        at = pl.ds(pl.multiple_of(owner * rows + side * half, half), half)
        h_all[at, :] = ref[:half, :]

    owners = [me] + [owner for step in (1, 2, 3) for owner in owners_of(step)]
    for k, owner in enumerate(owners):
        put(owner, 0, halves[2 * k])
        put(owner, 1, halves[2 * k + 1])
    owner, _ = owners_of(4)
    put(owner, core, halves[14])
    put(owner, 1 - core, halves[15])
    out = dot_tn(h_all[...], d_qkv[...])
    width = g_qkv.shape[2]
    for i in range(3):
        g_qkv[i] = out[:, i * width : (i + 1) * width]


def input_kernel(dq_a, dq_b, joint_a, joint_b, flat_a, flat_b, d_h, dq_full, w_full, flat_full, sort_full):
    row = lax.axis_index("head") // 2
    width, nb = dq_a.shape[1], flat_a.shape[1]
    sides = ((dq_a, joint_a, flat_a), (dq_b, joint_b, flat_b))
    for j, (g, joint, flat) in enumerate(sides):
        at = pl.multiple_of((row ^ j) * width, width)
        dq_full[:, pl.ds(at, width)] = g[...]
        w_full[:, pl.ds(at, width)] = joint[:, :width]
        at = pl.multiple_of((row ^ j) * nb, nb)
        flat_full[:, pl.ds(at, nb)] = flat[...]
        sort_full[:, pl.ds(at, nb)] = joint[:, width:]
    part = dot_nt(dq_full[...], w_full[...])
    d_sum = sum(dot_nt(p, sort_full[...]) for p in three_parts(flat_full[...])[::-1]) / BLOCK
    blocks = d_sum.shape[0]
    for i in range(blocks):
        sl = slice(i * BLOCK, (i + 1) * BLOCK)
        d_h[sl, :] = part[sl, :] + d_sum[i : i + 1, :]


def gain_kernel(tokens, d_mine, flat_mine, joint, g_two, out):
    width = d_mine.shape[1]
    normed, _ = norm_parts(tokens[...].astype(jnp.float32))
    part = dot_nt(d_mine[...], joint[:, :width])
    d_sum = sum(dot_nt(p, joint[:, width:]) for p in three_parts(flat_mine[...])[::-1]) / BLOCK
    blocks = d_sum.shape[0]
    sums = jnp.sum(part * normed, 0, keepdims=True)
    means = jnp.sum(normed.reshape(blocks, BLOCK, D), 1)
    sums = sums + jnp.sum(d_sum * means, 0, keepdims=True)
    out[:8, :] = jnp.broadcast_to(sums, g_two.shape)
    out[8:, :] = jnp.where(lax.axis_index("head") == 0, g_two[...], 0.0)


def end_kernel(tokens, gain, own, other, d_middle, d_tokens):
    f32 = jnp.float32
    normed, inv = norm_parts(tokens[...].astype(f32))
    d_h = own[...] + other[...]
    d_tokens[...] = d_middle[...] + norm_back(d_h, normed, inv, gain[...].astype(f32))


VMEM_SPEC = pl.BlockSpec(memory_space=pltpu.VMEM)
SMEM_SPEC = pl.BlockSpec(memory_space=pltpu.SMEM)
ANY_SPEC = pl.BlockSpec(memory_space=pltpu.HBM)
FREE_SPEC = pl.BlockSpec(memory_space=pl.ANY)


def fetch(pairs, sems, first=0):
    copies = []
    for k, (source, target) in enumerate(pairs):
        copies.append(pltpu.make_async_copy(source, target, sems.at[first + k]))
        copies[-1].start()
    return copies


def wait_all(copies):
    for copy in copies:
        copy.wait()


def call(kernel, outs, *args, scratch=(), smem=(), cold=(), free=(), raw=(), out_cold=(), limit=16, name=None):
    cost = int(1e3 * TIMES[name])
    shapes = [jax.ShapeDtypeStruct(s, d) for s, d in outs]
    specs = [
        SMEM_SPEC if i in smem else FREE_SPEC if i in free else ANY_SPEC if i in cold or i in raw else VMEM_SPEC
        for i in range(len(args))
    ]
    out_specs = [ANY_SPEC if i in out_cold else VMEM_SPEC for i in range(len(outs))]
    buffers = [pltpu.VMEM(args[i].shape, args[i].dtype) for i in cold]
    buffers += [pltpu.VMEM(*outs[i]) for i in out_cold]
    sem_count = len(cold) + len(out_cold)
    sems = [pltpu.SemaphoreType.DMA((sem_count,))] if sem_count else []
    own = [pltpu.SemaphoreType.DMA((40,))] if raw else []

    def body(*refs):
        refs = list(refs)
        ins, results = refs[: len(args)], refs[len(args) : len(args) + len(outs)]
        rest = refs[len(args) + len(outs) :]
        mine, rest = rest[: len(scratch)], rest[len(scratch) :]
        room, rest = rest[: len(buffers)], rest[len(buffers) :]
        copies = []
        if cold:
            copies = fetch([(ins[i], room[k]) for k, i in enumerate(cold)], rest[0])
            for k, i in enumerate(cold):
                ins[i] = room[k]
        targets = list(results)
        for k, i in enumerate(out_cold):
            results[i] = room[len(cold) + k]
        wait_all(copies)
        kernel(*ins, *results, *mine, *(rest[-1:] if raw else []))
        if out_cold:
            wait_all(fetch([(results[i], targets[i]) for i in out_cold], rest[0], len(cold)))

    result = pl.pallas_call(
        body,
        out_shape=shapes,
        in_specs=specs,
        out_specs=out_specs,
        scratch_shapes=[pltpu.VMEM(s, d) for s, d in scratch] + buffers + sems + own,
        compiler_params=pltpu.CompilerParams(vmem_limit_bytes=limit * 1024 * 1024),
        cost_estimate=pl.CostEstimate(
            flops=cost * FLOPS, bytes_accessed=cost * BYTES, transcendentals=0
        ),
        name=name,
    )(*args)
    return result[0] if len(shapes) == 1 else result


TIMES = {
    "norm_one": 1.7,
    "project_own": 0.45,
    "project": 0.7,
    "attend": 4.2,
    "prepare": 2.9,
    "feed": 4.2,
    "back": 1.2,
    "pull": 0.1,
    "grads": 0.95,
    "relay": 0.3,
    "collect": 9.0,
    "sinkhorn_back": 2.05,
    "total": 0.25,
    "input_back": 1.0,
    "gain_part": 0.8,
    "weights": 3.6,
    "norm_one_back": 1.7,
    "output": 1.1,
    "lay": 1.6,
    "gains": 0.6,
    "halve": 0.1,
    "half": 0.1,
    "pair": 0.1,
    "add_gains": 0.1,
    "sum_gains": 0.1,
}
FLOPS, BYTES = 1150000, 3690


def tie(*values):
    return lax.optimization_barrier(values)


def after(value, *others):
    return lax.optimization_barrier((value,) + others)[0]


RING = (0, 2, 4, 6, 7, 5, 3, 1)
SHARD = 512
EXTRA = 32
CUT = 256


def local_eight(
    tokens, gain_attn, gain_ffn, w_qkv, w_out, w_sort, w_up, w_down, gumbel_noise, partner, cotangent
):
    f32, bf16 = jnp.float32, jnp.bfloat16
    rows = tokens.shape[0]
    blocks = rows // BLOCK
    width = w_out.shape[0]
    ff = w_up.shape[1]
    nb = partner.shape[0]
    total = nb * BLOCK
    half, quarter = rows // 2, rows // 4
    core = lax.axis_index("head") % 2

    def along(v, way=1):
        pairs = []
        for i in range(8):
            for h in range(4):
                to = RING[(i + (way if h % 2 == 0 else -way)) % 8]
                pairs.append((RING[i] * 4 + h, to * 4 + h))
        return lax.ppermute(v, ("blk", "head"), pairs)

    def ahead(v):
        return along(v)

    def behind(v):
        return along(v, -1)

    def swap_head(v, j):
        return lax.ppermute(v, "head", [(i, i ^ j) for i in range(4)])

    def swap_blk(v, j):
        return lax.ppermute(v, "blk", [(i, i ^ j) for i in range(8)])

    w_in = w_qkv.transpose(1, 0, 2)
    partner_s = partner.T

    a, b, own_summary, own_noise = call(
        head_kernel,
        [((half + EXTRA, D), bf16)] * 2 + [((blocks, D), f32), ((2, D), f32)],
        tokens, gain_attn, gumbel_noise, swap_head(gumbel_noise, 1),
        cold=(0, 1, 2, 3), free=(3,), limit=62, name="norm_one",
    )

    mine = [(a, b)]
    up_y = swap_head(after(w_up, a), 2)
    a, b = along(a), along(b)
    qkv_own, joint, first, second = call(
        project_own_kernel,
        [
            ((rows, 3 * width), bf16), ((D, 3 * width + 2 * nb), bf16), ((CUT, D), bf16),
            ((width + ff - CUT, D), bf16),
        ],
        *mine[0], w_in, w_sort, w_out, w_down, name="project_own",
    )
    a, qkv_own = tie(a, qkv_own)
    mine.append((a, b))
    a, b = along(a), along(b)
    b, up_y = tie(b, up_y)
    mine.append((a, b))
    first_y = swap_head(after(first, a), 2)
    a, b = along(a), along(b)
    b, first_y = tie(b, first_y)
    mine.append((a, b))
    second_y = swap_head(after(second, a), 2)
    half_3, wo = call(
        half_kernel, [((half + EXTRA, D), bf16), ((2 * width, D), bf16)], a, b, w_out, first_y, name="half"
    )
    m4 = along(half_3)
    other, projected = [], []
    for k in (1, 2, 3):
        other.append(tuple(swap_head(after(v, mine[min(k + 1, 3)][0]), 1) for v in mine[k]))
        projected.append(
            call(
                project_kernel, [((2 * rows, 3 * width), bf16), ((4 * EXTRA, D), bf16)],
                *mine[k], *other[-1], joint, name="project",
            )
        )
    m4, second_y = tie(m4, second_y, *[p[0] for p in projected])[:2]
    o4 = swap_head(m4, 1)
    qkv, context, summary, steps, scale_rows, weight_rows = call(
        attend_kernel,
        [
            ((total, 3 * width), bf16), ((rows, width), bf16), ((nb, D), f32),
            ((2 * SINK, 2, nb, nb), f32), ((nb, 4 * DH), f32), ((nb, 2 * DH), f32),
        ],
        qkv_own, *[p[0] for p in projected], *[p[1] for p in projected], m4, o4, joint, own_summary, own_noise,
        partner_s, partner_s, smem=(12,), scratch=[((nb, 2 * nb), f32)], name="attend",
    )
    ctx_y, ctx_c = swap_head(context, 2), swap_head(context, 1)
    wo_other = swap_head(after(wo, context), 1)
    prepared = ((3, 0, rows), (-3, 0, rows), (4, 0, rows))
    amount = sum(n for _, _, n in prepared)
    z_all, probs_all = call(
        functools.partial(prepare_kernel, prepared), [((amount, 4 * DH), f32)] * 2,
        qkv, partner_s, scale_rows, smem=(1,), name="prepare",
    )
    ctx_y, ctx_c, z_all = tie(ctx_y, ctx_c, z_all)
    ctx_yc = swap_head(ctx_y, 1)
    middle, h_two, active, d_hidden, ffn, d_h_two = call(
        feed_kernel,
        [
            ((rows, D), f32),
            ((rows, D), bf16),
            ((rows, ff), bf16),
            ((rows, ff), bf16),
            ((rows, D), f32),
            ((rows, D), f32),
        ],
        tokens, cotangent, gain_ffn, context, ctx_c, ctx_y, ctx_yc, wo, wo_other,
        w_up, up_y, w_down, first_y, second_y,
        scratch=[
            ((rows, 4 * width), bf16), ((4 * width, D), bf16), ((D, 2 * ff), bf16), ((2 * ff, D), bf16),
            ((rows, 2 * ff), bf16), ((rows, 2 * ff), bf16),
        ],
        name="feed",
    )
    d_h_two_other = swap_head(d_h_two, 1)
    d_middle, d_low, d_ctx, g_two = call(
        back_kernel,
        [((rows, D), f32), ((rows, D), bf16), ((rows, width), bf16), ((8, D), f32)],
        middle, d_h_two, d_h_two_other, cotangent, gain_ffn, w_out, name="back",
    )

    plans = [[(0, 0, rows)]] + [[(k, 0, rows), (-k, 0, rows)] for k in (1, 2, 3)]
    plans.append([(4, 0, half), (4, half, half)])
    offsets = (None, None, None, 0, 2 * blocks)
    pulled = []

    def pull(given):
        plan, offset = plans[len(pulled)], offsets[len(pulled)]
        n = sum(count for _, _, count in plan)
        pulled.append(
            call(
                functools.partial(pull_kernel, tuple(plan), offset),
                [((n, 4 * DH), f32), ((n, 6 * DH), bf16), ((n // BLOCK, 4 * DH), f32)],
                *given, qkv, partner_s, scale_rows, weight_rows,
                *([] if offset is None else [z_all, probs_all]),
                smem=(len(given) + 1,), name="pull",
            )
        )
        return pulled[-1][0]

    piece = (D + ff + width) // 8
    front = 80
    parts = call(
        grads_kernel,
        [((4 * piece, width), f32)] * 7
        + [((rows + 4 * front, width), bf16), ((rows + 4 * (piece - front), width), bf16)],
        h_two, d_hidden, active, cotangent, context, d_low, d_ctx,
        scratch=[((D, ff), f32), ((ff, D), f32), ((width, D), f32)], name="grads",
    )
    keeps, (x, y) = parts[:7], parts[7:]

    def relay(start, count, at, keep, arrived):
        return call(
            functools.partial(relay_kernel, start, count, at), [((count + 4 * piece, width), bf16)],
            keep, arrived, name="relay",
        )

    given = [d_ctx]
    for step in range(4):
        x, y = ahead(x), behind(y)
        done = pull(given)
        given = [x, y]
        if step == 0:
            joint_y = swap_head(after(joint, done), 2)
        hold = [joint_y] if step == 2 else []
        y = tie(y, done, *hold)[0]
        if step < 3:
            count = half if step == 2 else rows
            x = relay(0, count, 0, keeps[step], x)
            y = relay(rows - count, count, 0 if step else front, keeps[step + 3], y)
    owned = call(total_kernel, [((piece, D), bf16)], keeps[6], x, y, name="total")
    wf1, wb1 = ahead(owned), behind(owned)
    pull(given)

    spans = tuple(tuple(plan) for plan in plans)
    d_qkv, d_mine, flat_mine, g_sort = call(
        functools.partial(collect_kernel, spans),
        [
            ((total, 3 * width), bf16), ((rows, 3 * width), bf16), ((blocks, 2 * nb), f32), ((D, 2 * nb), f32),
        ],
        *[p[k] for k in range(3) for p in pulled], partner_s, partner_s, steps, summary, smem=(15,),
        scratch=[
            ((nb, 4 * DH), f32), ((total, 4 * DH), f32), ((total, 4 * DH), bf16), ((nb, 2 * nb), f32),
        ],
        name="collect",
    )
    wf1, wb1, d_mine, flat_mine = tie(wf1, wb1, d_mine, flat_mine)
    ffn_other = swap_head(after(ffn, d_mine), 1)
    output = call(add_kernel, [((rows, D), f32)], ffn, ffn_other, middle, name="output")
    wf2, wb2 = ahead(wf1), behind(wb1)
    d_mine_y, flat_y = swap_head(d_mine, 2), swap_head(flat_mine, 2)
    gains_a = call(
        gain_kernel, [((16, D), f32)], tokens, d_mine, flat_mine, joint, g_two, name="gain_part"
    )
    gains_x = swap_blk(gains_a, 1)
    gains = call(add_kernel, [((16, D), f32)], gains_a, gains_x, name="add_gains")
    wf2, wb2, gains, flat_y, d_mine_y = tie(wf2, wb2, gains, flat_y, d_mine_y)
    wf3, wb3 = ahead(wf2), behind(wb2)
    gains1 = swap_blk(gains, 2)
    gains = call(add_kernel, [((16, D), f32)], gains, gains1, name="add_gains")
    gains2 = swap_blk(gains, 4)
    d_h = call(
        input_kernel, [((rows, D), f32)],
        d_mine, d_mine_y, joint, joint_y, flat_mine, flat_y,
        scratch=[
            ((rows, 6 * width), bf16), ((D, 6 * width), bf16), ((blocks, 4 * nb), f32), ((D, 4 * nb), bf16),
        ],
        name="input_back",
    )
    d_h_other = swap_head(d_h, 1)
    g_qkv = call(
        weight_kernel, [((3, D, width), f32)],
        *mine[0], *[v for k in (1, 2, 3) for v in (*mine[k], *other[k - 1])], m4, o4, after(d_qkv, d_h),
        scratch=[((total, D), bf16)], limit=24, name="weights",
    )
    wf3, wb3, gains, gains2, g_qkv, d_h_other = tie(
        wf3, wb3, gains, gains2, g_qkv, d_h_other
    )
    cut_f, cut_b = call(
        cut_kernel, [((front, D), bf16), ((piece - front, D), bf16)], wf3, wb3, name="halve"
    )
    wf4, wb4 = ahead(cut_f), behind(cut_b)
    gains = call(add_kernel, [((16, D), f32)], gains, gains2, name="add_gains")
    gains_y = swap_head(gains, 2)
    d_tokens = call(
        end_kernel, [((rows, D), f32)],
        tokens, gain_attn, d_h, d_h_other, d_middle, name="norm_one_back",
    )
    gains = call(add_kernel, [((16, D), f32)], gains, gains_y, name="add_gains")
    gains_c = swap_head(gains, 1)
    g_up, g_down, g_out, g_one, g_two = call(
        lay_kernel,
        [((D, ff), f32), ((ff, D), f32), ((width, D), f32), ((D,), f32), ((D,), f32)],
        owned, wf1, wb1, wf2, wb2, wf3, wb3, wf4, wb4, gains, gains_c, name="lay",
    )
    return output, d_tokens, g_one, g_two, g_qkv.transpose(1, 0, 2), g_out, g_sort, g_up, g_down


def solution(mesh):
    in_specs = (
        P("blk", None),
        P(),
        P(),
        P(None, None, "head"),
        P("head", None),
        P(None, "head"),
        P(None, "head"),
        P("head", None),
        P("blk", "head", None),
        P(None, "head"),
        P("blk", None),
    )
    out_specs = (
        P("blk", None),
        P("blk", None),
        P(),
        P(),
        P(None, None, "head"),
        P("head", None),
        P(None, "head"),
        P(None, "head"),
        P("head", None),
    )
    plan = local_eight if mesh.shape["blk"] == 8 and mesh.shape["head"] == 4 else local
    return jax.shard_map(plan, mesh=mesh, in_specs=in_specs, out_specs=out_specs, check_vma=False)
```
